32 devices in a mesh: crops: 2 (over x), row: 4 (over z), col: 4 (over y, core).
Axes of the slice: x: 2, y: 2, z: 4, core: 2. Of those that a mesh axis runs over, the one named last changes fastest.
Arguments:
- pair_state: bfloat16 [384, 192, 128], P(('crops', 'row'), 'col'), parts along dimension 0, may hold values from -6 to 6
- token_count: int32 [2], P('crops'), parts along dimension 0, may hold values from 96 to 192
- in_gain: float32 [128], replicated, may hold values from 0.1 to 1.9
- in_bias: float32 [128], replicated, may hold values from -3 to 3
- in_weights: bfloat16 [128, 512], replicated, may hold values from -0.5 to 0.5
- gate_weights: bfloat16 [128, 128], replicated, may hold values from -0.5 to 0.5
- out_gain: float32 [128], replicated, may hold values from 0.1 to 1.9
- out_bias: float32 [128], replicated, may hold values from -3 to 3
- out_weights: bfloat16 [128, 128], replicated, may hold values from -0.5 to 0.5
Outputs:
- update: bfloat16 [384, 192, 128], P(('crops', 'row'), 'col'), parts along dimension 0
The draws below stay inside these ranges and needn't reach their ends.
There are 2 independent parts, one for each index of `crops`. The reference program is written for one: setup_inputs(seed, part) draws one part's arguments, and reference() takes and returns one part's arrays. A program takes and returns all parts, laid end to end along the dimension named above; an argument that names none is the same for every part. Nothing has to cross between parts.
Inputs may be any that keep to these rules, and one draw needn't show every extreme that they name: Tokens from index token_count on are padding.
All inputs are finite; a program needn't handle non-finite values.
Results may differ from the reference program's by a relative error of at most 0.0057.
Values may be sent and summed in bfloat16 or wider, within the bound.
No kernel may reach another device: no remote copies, remote signals or barrier semaphores. Data moves between devices by JAX's collectives and lax.ppermute only.
A program may use at most 128 MiB of HBM per device.

```python
import jax
import jax.numpy as jnp
from jax import lax

C = 128
H = 128
TOKB = 48
N = 192
NBLK = 4
WIN = 2


def level_of(rng, shape, cuts, least, top_value):
    def one(axis_at, parts):
        steps = jax.random.uniform(jax.random.fold_in(jax.random.fold_in(rng, 6), axis_at), (parts,), jnp.float32, least / len(cuts), top_value / len(cuts))
        return jnp.repeat(jnp.exp(steps), shape[axis_at] // parts).reshape((-1,) + (1,) * (len(shape) - axis_at - 1))

    level = one(*cuts[0])
    for cut in cuts[1:]:
        level = level * one(*cut)
    return level


def gaussian(rng, shape, spread, most, shards=(), kind=jnp.bfloat16):
    entries = jax.random.normal(rng, shape, jnp.float32) * spread
    if len(shards) > 0:
        entries = level_of(rng, shape, shards, -0.22, 0.18) * entries
    return jnp.clip(entries, min=-most, max=most).astype(kind)


def setup_inputs(seed: int = 0, part: int = 0) -> dict:
    seeds = jax.random.split(jax.random.key(seed), 10)
    part_splits = jax.random.split(jax.random.fold_in(seeds[9], part), 10)
    pair_state = gaussian(part_splits[0], (N, N, C), 1.0, 6.0, ((0, 4), (1, 4)))
    token_count = jax.random.randint(part_splits[1], (1,), N // 2, N + 1).astype(jnp.int32)
    in_gain = jnp.clip(1.0 + 0.18 * jax.random.normal(seeds[2], (C,), jnp.float32), 0.1, 1.9)
    in_bias = gaussian(seeds[3], (C,), 0.5, 3.0, (), jnp.float32)
    in_weights = gaussian(seeds[4], (C, 4 * H), C ** -0.5, 0.5)
    gate_weights = gaussian(seeds[5], (C, C), C ** -0.5, 0.5)
    out_gain = jnp.clip(1.0 + 0.18 * jax.random.normal(seeds[6], (H,), jnp.float32), 0.1, 1.9)
    out_bias = gaussian(seeds[7], (H,), 0.5, 3.0, (), jnp.float32)
    out_weights = gaussian(seeds[8], (H, C), H ** -0.5, 0.5)
    return dict(pair_state=pair_state, token_count=token_count, in_gain=in_gain, in_bias=in_bias, in_weights=in_weights, gate_weights=gate_weights, out_gain=out_gain, out_bias=out_bias, out_weights=out_weights)


def layer_norm(values, gain, offset):
    average = lax.optimization_barrier(jnp.mean(values, axis=-1, keepdims=True))
    centered = values - average
    variance = lax.optimization_barrier(jnp.mean(centered * centered, axis=-1, keepdims=True))
    return centered * lax.rsqrt(variance + 1e-05) * gain + offset

def reference(pair_state, token_count, in_gain, in_bias, in_weights, gate_weights, out_gain, out_bias, out_weights):
    normed = layer_norm(pair_state.astype(jnp.float32), in_gain, in_bias).astype(jnp.bfloat16)
    flat_normed = normed.reshape(N * N, C)
    projected = jnp.dot(flat_normed, in_weights, preferred_element_type=jnp.float32).reshape(N, N, 4, H)
    positions = jnp.arange(N, dtype=jnp.int32)
    valid = (positions < token_count[0]).astype(jnp.float32)
    pair_mask = (valid[:, None] * valid[None, :])[:, :, None]
    left_factor = (pair_mask * jax.nn.sigmoid(projected[:, :, 0]) * projected[:, :, 1]).astype(jnp.bfloat16)
    right_factor = (pair_mask * jax.nn.sigmoid(projected[:, :, 2]) * projected[:, :, 3]).astype(jnp.bfloat16)
    out_gate = jax.nn.sigmoid(jnp.dot(flat_normed, gate_weights, preferred_element_type=jnp.float32))

    def one_block(block_id):
        third = ((block_id * TOKB + jnp.arange(WIN * TOKB, dtype=jnp.int32)) % N).astype(jnp.int32)
        left_band = jnp.take(left_factor, third, axis=1).astype(jnp.float32)
        right_rows = lax.dynamic_slice_in_dim(right_factor, (block_id * TOKB).astype(jnp.int32), TOKB, 0)
        right_band = jnp.take(right_rows, third, axis=1).astype(jnp.float32)
        return jnp.einsum('ikh,jkh->ijh', left_band, right_band, precision=lax.Precision.HIGHEST)
    blocks = lax.map(one_block, jnp.arange(NBLK, dtype=jnp.int32))
    product = jnp.transpose(blocks, (1, 0, 2, 3)).reshape(N, N, H)
    mixed = layer_norm(product, out_gain, out_bias).astype(jnp.bfloat16)
    projected_out = jnp.dot(mixed.reshape(N * N, H), out_weights, preferred_element_type=jnp.float32)
    return (out_gate * projected_out).astype(jnp.bfloat16).reshape(N, N, C)
```

```python
import jax
import jax.numpy as jnp
from jax import lax
from jax.sharding import PartitionSpec as P


def shifted(array, axis, by):
    devices = lax.axis_size(axis)
    return lax.ppermute(array, axis, [(i, (i + by) % devices) for i in range(devices)])


def from_root(array, axis, root):
    mine = lax.axis_index(axis) == root
    return lax.psum(jnp.where(mine, array, jnp.zeros_like(array)), axis)


def layer_norm(values, gain, offset):
    average = jnp.mean(values, axis=-1, keepdims=True)
    centered = values - average
    variance = jnp.mean(centered * centered, axis=-1, keepdims=True)
    return centered * lax.rsqrt(variance + 1e-05) * gain + offset


def contract(summed, left_piece, right_piece):
    return summed + jnp.einsum(
        "ikh,jkh->ijh", left_piece, right_piece, preferred_element_type=jnp.float32
    )


def band_by_sums(right_factor, cols_here, window, row_count, col_count):
    blocks_per_row = col_count // row_count
    col_pos = lax.axis_index("col")
    pieces = []
    for offset in range(window):
        block_id = (col_pos - offset) % col_count
        start = block_id % blocks_per_row * cols_here
        received = from_root(
            lax.dynamic_slice_in_dim(right_factor, start, cols_here, 0),
            "row",
            block_id // blocks_per_row,
        )
        pieces.append(received if offset == 0 else shifted(received, "col", -offset))
    return pieces


def band_by_hops(right_factor):
    row_pos = lax.axis_index("row")
    col_pos = lax.axis_index("col")

    def at(r, c):
        return r % 4 * 4 + c % 4

    def move(array, pairs):
        return lax.ppermute(array, ("row", "col"), pairs)

    everyone = [(r, c) for r in range(4) for c in range(4)]
    roots = [(r, c) for r, c in everyone if (c - r) % 4 < 2]
    far = move(right_factor, [(at(r, c), at(r ^ 2, c)) for r, c in roots])
    is_root = (col_pos - row_pos) % 4 < 2
    held = jnp.where(is_root, right_factor, far)
    near = move(
        held,
        [
            (at(r, c), at(r ^ 1, c) if (r + c) % 2 == 0 else at(r, c - 1))
            for r, c in everyone
        ],
    )
    cross = move(
        held, [(at(r, c), at(r ^ 1, c - 1)) for r, c in everyone if (r + c) % 2 == 1]
    )
    even = (row_pos + col_pos) % 2 == 0
    return [jnp.where(even, held, near), jnp.where(even, near, cross)]


def on_device(
    pair_state,
    token_count,
    in_gain,
    in_bias,
    in_weights,
    gate_weights,
    out_gain,
    out_bias,
    out_weights,
):
    rows_here, cols_here, channels = pair_state.shape
    hidden = out_weights.shape[0]
    col_count = lax.axis_size("col")
    row_count = lax.axis_size("row")
    window = col_count // 2
    row_pos = lax.axis_index("row")
    col_pos = lax.axis_index("col")
    normed = layer_norm(pair_state.astype(jnp.float32), in_gain, in_bias).astype(jnp.bfloat16)
    flat_normed = normed.reshape(rows_here * cols_here, channels)
    projected = jnp.dot(flat_normed, in_weights, preferred_element_type=jnp.float32).reshape(
        rows_here, cols_here, 4, hidden
    )
    row_tokens = row_pos * rows_here + jnp.arange(rows_here, dtype=jnp.int32)
    col_tokens = col_pos * cols_here + jnp.arange(cols_here, dtype=jnp.int32)
    row_valid = (row_tokens < token_count[0]).astype(jnp.float32)
    col_valid = (col_tokens < token_count[0]).astype(jnp.float32)
    pair_mask = (row_valid[:, None] * col_valid[None, :])[:, :, None]
    left_factor = (pair_mask * jax.nn.sigmoid(projected[:, :, 0]) * projected[:, :, 1]).astype(
        jnp.bfloat16
    )
    right_factor = (pair_mask * jax.nn.sigmoid(projected[:, :, 2]) * projected[:, :, 3]).astype(
        jnp.bfloat16
    )
    out_gate = jax.nn.sigmoid(
        jnp.dot(flat_normed, gate_weights, preferred_element_type=jnp.float32)
    )
    if row_count == 4 and col_count == 4:
        pieces = band_by_hops(right_factor)
    else:
        pieces = band_by_sums(right_factor, cols_here, window, row_count, col_count)
    summed = jnp.zeros((rows_here, cols_here, hidden), jnp.float32)
    carried = left_factor
    for offset in range(window):
        if offset > 0:
            carried = shifted(carried, "col", -1)
        summed = contract(summed, carried, pieces[offset])
    mixed = layer_norm(summed, out_gain, out_bias).astype(jnp.bfloat16)
    projected_out = jnp.dot(
        mixed.reshape(rows_here * cols_here, hidden),
        out_weights,
        preferred_element_type=jnp.float32,
    )
    return (out_gate * projected_out).astype(jnp.bfloat16).reshape(rows_here, cols_here, channels)


def solution(mesh):
    placed = (P(("crops", "row"), "col", None), P("crops"), P(), P(), P(), P(), P(), P(), P())
    return jax.shard_map(
        on_device,
        mesh=mesh,
        in_specs=placed,
        out_specs=P(("crops", "row"), "col", None),
        check_vma=False,
    )
```

```python
import functools

import jax
import jax.numpy as jnp
from jax import lax
from jax.experimental import pallas as pl
from jax.experimental.pallas import tpu as pltpu
from jax.sharding import PartitionSpec as P

CHUNK = 16
VMEM_LIMIT = 56 * 1024 * 1024


def whole(memory_space=pltpu.VMEM):
    return pl.BlockSpec(memory_space=memory_space)


def shifted(array, axis, by):
    devices = lax.axis_size(axis)
    return lax.ppermute(array, axis, [(i, (i + by) % devices) for i in range(devices)])


def from_root(array, axis, root):
    mine = lax.axis_index(axis) == root
    return lax.psum(jnp.where(mine, array, jnp.zeros_like(array)), axis)


def layer_norm(values, gain, offset):
    average = jnp.mean(values, axis=-1, keepdims=True)
    centered = values - average
    variance = jnp.mean(centered * centered, axis=-1, keepdims=True)
    return centered * lax.rsqrt(variance + 1e-05) * gain + offset


def normed_rows(pair_ref, gain_ref, bias_ref, first, count):
    _, columns, channels = pair_ref.shape
    values = pair_ref[pl.ds(first, count)].reshape(count * columns, channels)
    return layer_norm(values.astype(jnp.float32), gain_ref[...], bias_ref[...]).astype(jnp.bfloat16)


def gated(normed, weights_ref, start, hidden):
    both = jnp.dot(
        normed, weights_ref[:, start : start + 2 * hidden], preferred_element_type=jnp.float32
    )
    return jax.nn.sigmoid(both[:, :hidden]) * both[:, hidden:]


def masked(values, tokens_ref, first, count, rows, columns):
    tokens = tokens_ref[0]
    row_start = lax.axis_index("row") * rows + first
    col_start = lax.axis_index("col") * columns
    valid_columns = tokens - col_start
    position = lax.broadcasted_iota(jnp.int32, (columns, values.shape[-1]), 0)
    parts = []
    for row in range(count):
        limit = jnp.where(row_start + row < tokens, valid_columns, 0)
        part = values[row * columns : (row + 1) * columns]
        parts.append(jnp.where(position < limit, part, 0.0))
    return parts


def right_kernel(tokens_ref, pair_ref, gain_ref, bias_ref, weights_ref, *refs):
    outs, scratch = refs[:-1], refs[-1]
    rows, columns, _ = pair_ref.shape
    hidden = scratch.shape[1]
    step = 4
    for first in range(0, rows, step):
        normed = normed_rows(pair_ref, gain_ref, bias_ref, first, step)
        right = gated(normed, weights_ref, 2 * hidden, hidden)
        parts = masked(right, tokens_ref, first, step, rows, columns)
        for row, part in enumerate(parts):
            scratch[pl.ds((first + row) * columns, columns), :] = part
    for at, out in enumerate(outs):
        for third in range(columns):
            start = at * CHUNK * columns + third
            out[third] = scratch[pl.ds(start, CHUNK, stride=columns), :].astype(jnp.bfloat16)


def left_kernel(
    tokens_ref, pair_ref, gain_ref, bias_ref, weights_ref, gate_weights_ref, left_ref, gate_ref
):
    rows, columns, _ = pair_ref.shape
    hidden = left_ref.shape[2]
    channels = gate_ref.shape[2]
    step = 4
    for first in range(0, rows, step):
        normed = normed_rows(pair_ref, gain_ref, bias_ref, first, step)
        left = gated(normed, weights_ref, 0, hidden)
        for row, part in enumerate(masked(left, tokens_ref, first, step, rows, columns)):
            left_ref[first + row] = part.astype(jnp.bfloat16)
        gate = jax.nn.sigmoid(
            jnp.dot(normed, gate_weights_ref[...], preferred_element_type=jnp.float32)
        )
        gate_ref[pl.ds(first, step)] = gate.reshape(step, columns, channels)


def product_kernel(picks, lefts, rights, *refs):
    left_refs, refs = refs[:lefts], refs[lefts:]
    right_refs, refs = refs[:rights], refs[rights:]
    gate_ref, gain_ref, bias_ref, weights_ref, *_, out_ref, left_rows, right_rows, product = refs
    rows, columns, hidden = left_refs[0].shape
    depth = lefts * columns
    even = (lax.axis_index("row") + lax.axis_index("col")) % 2 == 0

    @pl.loop(0, rows)
    def _(row):
        for at, ref in enumerate(left_refs):
            left_rows[pl.ds(row * depth + at * columns, columns), :] = ref[row].astype(jnp.float32)

    for at, (at_even, at_odd) in enumerate(picks):
        for third in range(columns):
            piece = right_refs[at_even][third].astype(jnp.float32)
            if at_odd != at_even:
                piece = jnp.where(even, piece, right_refs[at_odd][third].astype(jnp.float32))
            right_rows[pl.ds((at * columns + third) * CHUNK, CHUNK), :] = piece

    group, unroll = 8, 8
    halves = CHUNK // 8

    @pl.loop(0, rows // group)
    def _(at):
        def add(step, sums):
            sums = list(sums)
            for inner in range(unroll):
                third = step * unroll + inner
                right = [
                    right_rows[pl.ds(third * CHUNK + 8 * half, 8), :] for half in range(halves)
                ]
                for row in range(group):
                    left = left_rows[pl.ds((at * group + row) * depth + third, 8, stride=0), :]
                    for half in range(halves):
                        sums[row * halves + half] += left * right[half]
            return tuple(sums)

        zeros = tuple(jnp.zeros((8, hidden), jnp.float32) for _ in range(group * halves))
        sums = lax.fori_loop(0, depth // unroll, add, zeros)
        for row in range(group):
            for half in range(halves):
                start = (at * group + row) * CHUNK + 8 * half
                product[pl.ds(start, 8), :] = sums[row * halves + half]

    for first in range(0, rows, group):
        values = product[pl.ds(first * CHUNK, group * CHUNK), :]
        mixed = layer_norm(values, gain_ref[...], bias_ref[...]).astype(jnp.bfloat16)
        update = jnp.dot(mixed, weights_ref[...], preferred_element_type=jnp.float32)
        gate = gate_ref[pl.ds(first, group)]
        out_ref[pl.ds(first, group)] = (gate * update.reshape(gate.shape)).astype(jnp.bfloat16)


def band_by_sums(chunks, window, row_count, col_count):
    blocks_per_row = col_count // row_count
    col_pos = lax.axis_index("col")
    per_block = len(chunks) // blocks_per_row
    stacked = jnp.stack(chunks)
    pieces = []
    for offset in range(window):
        block_id = (col_pos - offset) % col_count
        start = block_id % blocks_per_row * per_block
        received = from_root(
            lax.dynamic_slice_in_dim(stacked, start, per_block, 0), "row", block_id // blocks_per_row
        )
        pieces.append(received if offset == 0 else shifted(received, "col", -offset))
    bands = [[piece[at] for piece in pieces] for at in range(per_block)]
    return bands, [(offset, offset) for offset in range(window)]


def band_by_hops(chunks):
    row_pos = lax.axis_index("row")
    col_pos = lax.axis_index("col")

    def at(r, c):
        return r % 4 * 4 + c % 4

    def move(array, pairs):
        return lax.ppermute(array, ("row", "col"), pairs)

    everyone = [(r, c) for r in range(4) for c in range(4)]
    roots = [(r, c) for r, c in everyone if (c - r) % 4 < 2]
    is_root = (col_pos - row_pos) % 4 < 2
    bands = []
    for chunk in chunks:
        far = move(chunk, [(at(r, c), at(r ^ 2, c)) for r, c in roots])
        held = jnp.where(is_root, chunk, far)
        near = move(
            held,
            [
                (at(r, c), at(r ^ 1, c) if (r + c) % 2 == 0 else at(r, c - 1))
                for r, c in everyone
            ],
        )
        cross = move(
            held, [(at(r, c), at(r ^ 1, c - 1)) for r, c in everyone if (r + c) % 2 == 1]
        )
        bands.append([held, near, cross])
    return bands, [(0, 1), (1, 2)]


def on_device(
    pair_state,
    token_count,
    in_gain,
    in_bias,
    in_weights,
    gate_weights,
    out_gain,
    out_bias,
    out_weights,
):
    rows, columns, channels = pair_state.shape
    hidden = out_weights.shape[0]
    tokens = rows * columns
    col_count = lax.axis_size("col")
    row_count = lax.axis_size("row")
    window = col_count // 2
    in_gain, in_bias = in_gain.reshape(1, channels), in_bias.reshape(1, channels)
    out_gain, out_bias = out_gain.reshape(1, hidden), out_bias.reshape(1, hidden)
    params = pltpu.CompilerParams(vmem_limit_bytes=VMEM_LIMIT)
    smem, vmem = whole(pltpu.SMEM), whole()

    chunks = pl.pallas_call(
        right_kernel,
        out_shape=[jax.ShapeDtypeStruct((columns, CHUNK, hidden), jnp.bfloat16)] * (rows // CHUNK),
        in_specs=[smem] + [vmem] * 4,
        out_specs=[vmem] * (rows // CHUNK),
        scratch_shapes=[pltpu.VMEM((tokens, hidden), jnp.float32)],
        compiler_params=params,
        cost_estimate=pl.CostEstimate(
            flops=4 * tokens * channels * hidden, bytes_accessed=4 * tokens * channels, transcendentals=0
        ),
        name="right",
    )(token_count, pair_state, in_gain, in_bias, in_weights)

    left, gate = pl.pallas_call(
        left_kernel,
        out_shape=[
            jax.ShapeDtypeStruct((rows, columns, hidden), jnp.bfloat16),
            jax.ShapeDtypeStruct((rows, columns, channels), jnp.float32),
        ],
        in_specs=[smem] + [vmem] * 5,
        out_specs=[vmem] * 2,
        compiler_params=params,
        cost_estimate=pl.CostEstimate(
            flops=6 * tokens * channels * hidden, bytes_accessed=8 * tokens * channels, transcendentals=0
        ),
        name="left_and_gate",
    )(token_count, pair_state, in_gain, in_bias, in_weights, gate_weights)

    if row_count == 4 and col_count == 4:
        bands, picks = band_by_hops(chunks)
    else:
        bands, picks = band_by_sums(chunks, window, row_count, col_count)
    lefts = [left]
    for _ in range(window - 1):
        lefts.append(shifted(lefts[-1], "col", -1))

    update = []
    depth = window * columns
    for at, band in enumerate(bands):
        chunk_of = pl.BlockSpec((rows, CHUNK, channels), lambda step, at=at: (0, at, 0))
        filled = pl.pallas_call(
            functools.partial(product_kernel, picks, len(lefts), len(band)),
            grid=(1,),
            out_shape=jax.ShapeDtypeStruct((rows, columns, channels), jnp.bfloat16),
            in_specs=[vmem] * (len(lefts) + len(band))
            + [chunk_of]
            + [vmem] * 3
            + [whole(pl.ANY)] * len(update),
            out_specs=chunk_of,
            scratch_shapes=[
                pltpu.VMEM((rows * depth + 8, hidden), jnp.float32),
                pltpu.VMEM((depth * CHUNK, hidden), jnp.float32),
                pltpu.VMEM((rows * CHUNK, hidden), jnp.float32),
            ],
            input_output_aliases={len(lefts) + len(band) + 4: 0} if update else {},
            compiler_params=params,
            cost_estimate=pl.CostEstimate(
                flops=2 * rows * CHUNK * depth * hidden,
                bytes_accessed=2 * rows * depth * hidden,
                transcendentals=0,
            ),
            name="product",
        )(*lefts, *band, gate, out_gain, out_bias, out_weights, *update)
        update = [filled]
    return filled


def solution(mesh):
    placed = (P(("crops", "row"), "col", None), P("crops"), P(), P(), P(), P(), P(), P(), P())
    return jax.shard_map(
        on_device,
        mesh=mesh,
        in_specs=placed,
        out_specs=P(("crops", "row"), "col", None),
        check_vma=False,
    )
```

```python
import functools

import jax
import jax.numpy as jnp
from jax import lax
from jax.experimental import pallas as pl
from jax.experimental.pallas import tpu as pltpu
from jax.sharding import PartitionSpec as P

CHUNK = 16
LANES = 128
VMEM_LIMIT = 56 * 1024 * 1024


def whole(memory_space=pltpu.VMEM):
    return pl.BlockSpec(memory_space=memory_space)


def shifted(array, axis, by):
    devices = lax.axis_size(axis)
    return lax.ppermute(array, axis, [(i, (i + by) % devices) for i in range(devices)])


def from_root(array, axis, root):
    mine = lax.axis_index(axis) == root
    return lax.psum(jnp.where(mine, array, jnp.zeros_like(array)), axis)


def layer_norm(values, gain, offset):
    average = jnp.mean(values, axis=-1, keepdims=True)
    centered = values - average
    variance = jnp.mean(centered * centered, axis=-1, keepdims=True)
    return centered * lax.rsqrt(variance + 1e-05) * gain + offset


def normed_rows(pair_ref, gain_ref, bias_ref, first, count):
    _, columns, channels = pair_ref.shape
    values = pair_ref[pl.ds(first, count)].reshape(count * columns, channels)
    return layer_norm(values.astype(jnp.float32), gain_ref[...], bias_ref[...]).astype(jnp.bfloat16)


def gated(normed, weights_ref, start, hidden):
    both = jnp.dot(
        normed, weights_ref[:, start : start + 2 * hidden], preferred_element_type=jnp.float32
    )
    return jax.nn.sigmoid(both[:, :hidden]) * both[:, hidden:]


def masked(values, tokens_ref, first, count, rows, columns):
    tokens = tokens_ref[0]
    row_start = lax.axis_index("row") * rows + first
    col_start = lax.axis_index("col") * columns
    valid_columns = tokens - col_start
    position = lax.broadcasted_iota(jnp.int32, (columns, values.shape[-1]), 0)
    parts = []
    for row in range(count):
        limit = jnp.where(row_start + row < tokens, valid_columns, 0)
        part = values[row * columns : (row + 1) * columns]
        parts.append(jnp.where(position < limit, part, 0.0))
    return parts


def right_kernel(tokens_ref, pair_ref, gain_ref, bias_ref, weights_ref, *outs):
    rows, columns, _ = pair_ref.shape
    hidden = outs[0].shape[2]
    step = 4
    for first in range(0, rows, step):
        normed = normed_rows(pair_ref, gain_ref, bias_ref, first, step)
        right = gated(normed, weights_ref, 2 * hidden, hidden)
        for row, part in enumerate(masked(right, tokens_ref, first, step, rows, columns)):
            outs[(first + row) // CHUNK][(first + row) % CHUNK] = part.astype(jnp.bfloat16)


def left_kernel(
    tokens_ref, pair_ref, gain_ref, bias_ref, weights_ref, gate_weights_ref, left_ref, gate_ref
):
    rows, columns, _ = pair_ref.shape
    hidden = left_ref.shape[2]
    channels = gate_ref.shape[2]
    step = 4
    for first in range(0, rows, step):
        normed = normed_rows(pair_ref, gain_ref, bias_ref, first, step)
        left = gated(normed, weights_ref, 0, hidden)
        for row, part in enumerate(masked(left, tokens_ref, first, step, rows, columns)):
            left_ref[first + row] = part.astype(jnp.bfloat16)
        gate = jax.nn.sigmoid(
            jnp.dot(normed, gate_weights_ref[...], preferred_element_type=jnp.float32)
        )
        gate_ref[pl.ds(first, step)] = gate.reshape(step, columns, channels)


def turned(pieces, width):
    rows = sum(piece.shape[0] for piece in pieces)
    hidden = pieces[0].shape[1]
    if width > rows:
        pieces = pieces + [jnp.zeros((width - rows, hidden), pieces[0].dtype)]
    stacked = jnp.concatenate(pieces, axis=0)
    row = lax.broadcasted_iota(jnp.int32, (hidden, hidden), 0)
    column = lax.broadcasted_iota(jnp.int32, (hidden, hidden), 1)
    identity = (row == column).astype(jnp.float32).astype(jnp.bfloat16)
    return lax.dot_general(
        identity, stacked, (((1,), (1,)), ((), ())), preferred_element_type=jnp.float32
    )


def turn_kernel(*refs):
    pieces, (out_ref, scratch) = refs[:-2], refs[-2:]
    rows, _, hidden = pieces[0].shape
    width = out_ref.shape[2]
    for row in range(rows):
        one = turned([ref[row] for ref in pieces], width)
        for at in range(0, width, LANES):
            scratch[at // LANES, pl.ds(row, hidden, stride=rows), :] = one[:, at : at + LANES]
    for channel in range(hidden):
        for at in range(0, width, LANES):
            one = scratch[at // LANES, pl.ds(channel * rows, rows), :]
            out_ref[channel, :, at : at + LANES] = one.astype(jnp.bfloat16)


def product_kernel(picks, rights, *refs):
    right_refs, refs = refs[:rights], refs[rights:]
    left_ref, gate_ref, gain_ref, bias_ref, weights_ref, *_, out_ref = refs[:-5]
    held, arrived, right, product, updates = refs[-5:]
    hidden, rows, width = left_ref.shape
    even = (lax.axis_index("row") + lax.axis_index("col")) % 2 == 0

    def fetch(source, at):
        return pltpu.make_async_copy(right_refs[source], held.at[at], arrived.at[at])

    for at, (at_even, at_odd) in enumerate(picks):
        if at_even == at_odd:
            fetch(at_even, at).start()
        else:
            pl.when(even)(fetch(at_even, at).start)
            pl.when(jnp.logical_not(even))(fetch(at_odd, at).start)
    for at, (at_even, _) in enumerate(picks):
        fetch(at_even, at).wait()

    for token in range(CHUNK):
        pieces = [held[at, token] for at in range(len(picks))]
        one = turned(pieces, width)
        for at in range(0, width, LANES):
            right[at // LANES, pl.ds(token, hidden, stride=CHUNK), :] = one[:, at : at + LANES]

    total = jnp.zeros((CHUNK, rows), jnp.float32)
    for channel in range(hidden):
        one = 0.0
        for at in range(0, width, LANES):
            one += lax.dot_general(
                right[at // LANES, pl.ds(channel * CHUNK, CHUNK), :].astype(jnp.bfloat16),
                left_ref[channel, :, at : at + LANES],
                (((1,), (1,)), ((), ())),
                preferred_element_type=jnp.float32,
            )
        product[pl.ds(channel * CHUNK, CHUNK), :rows] = one
        total += one
    average = total / hidden
    total = jnp.zeros((CHUNK, rows), jnp.float32)
    for channel in range(hidden):
        centered = product[pl.ds(channel * CHUNK, CHUNK), :rows] - average
        total += centered * centered
    scale = lax.rsqrt(total / hidden + 1e-05)
    for channel in range(hidden):
        place = pl.ds(channel * CHUNK, CHUNK)
        centered = product[place, :rows] - average
        product[place, :rows] = centered * scale * gain_ref[channel] + bias_ref[channel]
    for token in range(CHUNK):
        mixed = product[pl.ds(token, hidden, stride=CHUNK), :][:, :rows].astype(jnp.bfloat16)
        updates[pl.ds(token, rows, stride=CHUNK), :] = lax.dot_general(
            mixed, weights_ref[...], (((0,), (0,)), ((), ())), preferred_element_type=jnp.float32
        )
    step = 8
    for first in range(0, rows, step):
        gate = gate_ref[pl.ds(first, step)]
        update = updates[pl.ds(first * CHUNK, step * CHUNK), :].reshape(gate.shape)
        out_ref[pl.ds(first, step)] = (gate * update).astype(jnp.bfloat16)


def band_by_sums(chunks, window, row_count, col_count):
    blocks_per_row = col_count // row_count
    col_pos = lax.axis_index("col")
    per_block = len(chunks) // blocks_per_row
    stacked = jnp.stack(chunks)
    pieces = []
    for offset in range(window):
        block_id = (col_pos - offset) % col_count
        start = block_id % blocks_per_row * per_block
        received = from_root(
            lax.dynamic_slice_in_dim(stacked, start, per_block, 0), "row", block_id // blocks_per_row
        )
        pieces.append(received if offset == 0 else shifted(received, "col", -offset))
    bands = [[piece[at] for piece in pieces] for at in range(per_block)]
    return bands, [(offset, offset) for offset in range(window)]


def band_by_hops(chunks):
    row_pos = lax.axis_index("row")
    col_pos = lax.axis_index("col")

    def at(r, c):
        return r % 4 * 4 + c % 4

    def move(array, pairs):
        return lax.ppermute(array, ("row", "col"), pairs)

    everyone = [(r, c) for r in range(4) for c in range(4)]
    roots = [(r, c) for r, c in everyone if (c - r) % 4 < 2]
    is_root = (col_pos - row_pos) % 4 < 2
    bands = []
    for chunk in chunks:
        far = move(chunk, [(at(r, c), at(r ^ 2, c)) for r, c in roots])
        held = jnp.where(is_root, chunk, far)
        near = move(
            held,
            [
                (at(r, c), at(r ^ 1, c) if (r + c) % 2 == 0 else at(r, c - 1))
                for r, c in everyone
            ],
        )
        cross = move(
            held, [(at(r, c), at(r ^ 1, c - 1)) for r, c in everyone if (r + c) % 2 == 1]
        )
        bands.append([held, near, cross])
    return bands, [(0, 1), (1, 2)]


def on_device(
    pair_state,
    token_count,
    in_gain,
    in_bias,
    in_weights,
    gate_weights,
    out_gain,
    out_bias,
    out_weights,
):
    rows, columns, channels = pair_state.shape
    hidden = out_weights.shape[0]
    tokens = rows * columns
    col_count = lax.axis_size("col")
    row_count = lax.axis_size("row")
    window = col_count // 2
    in_gain, in_bias = in_gain.reshape(1, channels), in_bias.reshape(1, channels)
    params = pltpu.CompilerParams(vmem_limit_bytes=VMEM_LIMIT)
    smem, vmem = whole(pltpu.SMEM), whole()

    chunks = pl.pallas_call(
        right_kernel,
        out_shape=[jax.ShapeDtypeStruct((CHUNK, columns, hidden), jnp.bfloat16)] * (rows // CHUNK),
        in_specs=[smem] + [vmem] * 4,
        out_specs=[vmem] * (rows // CHUNK),
        compiler_params=params,
        cost_estimate=pl.CostEstimate(
            flops=4 * tokens * channels * hidden, bytes_accessed=4 * tokens * channels, transcendentals=0
        ),
        name="right",
    )(token_count, pair_state, in_gain, in_bias, in_weights)

    left, gate = pl.pallas_call(
        left_kernel,
        out_shape=[
            jax.ShapeDtypeStruct((rows, columns, hidden), jnp.bfloat16),
            jax.ShapeDtypeStruct((rows, columns, channels), jnp.float32),
        ],
        in_specs=[smem] + [vmem] * 5,
        out_specs=[vmem] * 2,
        compiler_params=params,
        cost_estimate=pl.CostEstimate(
            flops=6 * tokens * channels * hidden, bytes_accessed=8 * tokens * channels, transcendentals=0
        ),
        name="left_and_gate",
    )(token_count, pair_state, in_gain, in_bias, in_weights, gate_weights)

    if row_count == 4 and col_count == 4:
        bands, picks = band_by_hops(chunks)
    else:
        bands, picks = band_by_sums(chunks, window, row_count, col_count)
    lefts = [left]
    for _ in range(window - 1):
        lefts.append(shifted(lefts[-1], "col", -1))

    depth = window * columns
    width = -(-depth // LANES) * LANES
    turned_left = pl.pallas_call(
        turn_kernel,
        out_shape=jax.ShapeDtypeStruct((hidden, rows, width), jnp.bfloat16),
        in_specs=[vmem] * window,
        out_specs=vmem,
        scratch_shapes=[pltpu.VMEM((width // LANES, hidden * rows, LANES), jnp.float32)],
        compiler_params=params,
        cost_estimate=pl.CostEstimate(
            flops=2 * rows * width * hidden * hidden,
            bytes_accessed=4 * rows * width * hidden,
            transcendentals=0,
        ),
        name="turn_left",
    )(*lefts)

    update = []
    for at, band in enumerate(bands):
        chunk_of = pl.BlockSpec((rows, CHUNK, channels), lambda step, at=at: (0, at, 0))
        filled = pl.pallas_call(
            functools.partial(product_kernel, picks, len(band)),
            grid=(1,),
            out_shape=jax.ShapeDtypeStruct((rows, columns, channels), jnp.bfloat16),
            in_specs=[whole(pl.ANY)] * len(band)
            + [vmem, chunk_of, smem, smem, vmem]
            + [whole(pl.ANY)] * len(update),
            out_specs=chunk_of,
            scratch_shapes=[
                pltpu.VMEM((window, CHUNK, columns, hidden), jnp.bfloat16),
                pltpu.SemaphoreType.DMA((window,)),
                pltpu.VMEM((width // LANES, hidden * CHUNK, LANES), jnp.float32),
                pltpu.VMEM((hidden * CHUNK, LANES), jnp.float32),
                pltpu.VMEM((rows * CHUNK, channels), jnp.float32),
            ],
            input_output_aliases={len(band) + 5: 0} if update else {},
            compiler_params=params,
            cost_estimate=pl.CostEstimate(
                flops=2 * rows * CHUNK * depth * hidden,
                bytes_accessed=2 * rows * depth * hidden,
                transcendentals=0,
            ),
            name="product",
        )(*band, turned_left, gate, out_gain, out_bias, out_weights, *update)
        update = [filled]
    return filled


def solution(mesh):
    placed = (P(("crops", "row"), "col", None), P("crops"), P(), P(), P(), P(), P(), P(), P())
    return jax.shard_map(
        on_device,
        mesh=mesh,
        in_specs=placed,
        out_specs=P(("crops", "row"), "col", None),
        check_vma=False,
    )
```

```python
import functools

import jax
import jax.numpy as jnp
from jax import lax
from jax.experimental import pallas as pl
from jax.experimental.pallas import tpu as pltpu
from jax.sharding import PartitionSpec as P

CHUNK = 16
LANES = 128
MIB = 1024 * 1024


def params(*sizes):
    return pltpu.CompilerParams(vmem_limit_bytes=min(6 * MIB + 2 * sum(sizes), 56 * MIB))


def whole(memory_space=pltpu.VMEM):
    return pl.BlockSpec(memory_space=memory_space)


def shifted(array, axis, by):
    devices = lax.axis_size(axis)
    return lax.ppermute(array, axis, [(i, (i + by) % devices) for i in range(devices)])


def from_root(array, axis, root):
    mine = lax.axis_index(axis) == root
    return lax.psum(jnp.where(mine, array, jnp.zeros_like(array)), axis)


def layer_norm(values, gain, offset):
    average = jnp.mean(values, axis=-1, keepdims=True)
    centered = values - average
    variance = jnp.mean(centered * centered, axis=-1, keepdims=True)
    return centered * lax.rsqrt(variance + 1e-05) * gain + offset


def normed_rows(pair_ref, gain_ref, bias_ref, first, count):
    _, columns, channels = pair_ref.shape
    values = pair_ref[pl.ds(first, count)].reshape(count * columns, channels)
    return layer_norm(values.astype(jnp.float32), gain_ref[...], bias_ref[...]).astype(jnp.bfloat16)


def gated(normed, weights_ref, start, hidden):
    both = jnp.dot(
        normed, weights_ref[:, start : start + 2 * hidden], preferred_element_type=jnp.float32
    )
    return jax.nn.sigmoid(both[:, :hidden]) * both[:, hidden:]


def masked(values, tokens_ref, first, count, rows, columns):
    tokens = tokens_ref[0]
    row_start = lax.axis_index("row") * rows + first
    col_start = lax.axis_index("col") * columns
    valid_columns = tokens - col_start
    position = lax.broadcasted_iota(jnp.int32, (columns, values.shape[-1]), 0)
    parts = []
    for row in range(count):
        limit = jnp.where(row_start + row < tokens, valid_columns, 0)
        part = values[row * columns : (row + 1) * columns]
        parts.append(jnp.where(position < limit, part, 0.0))
    return parts


def right_kernel(tokens_ref, pair_ref, gain_ref, bias_ref, weights_ref, *outs):
    rows, columns, _ = pair_ref.shape
    hidden = outs[0].shape[2]
    step = 4
    for first in range(0, rows, step):
        normed = normed_rows(pair_ref, gain_ref, bias_ref, first, step)
        right = gated(normed, weights_ref, 2 * hidden, hidden)
        for row, part in enumerate(masked(right, tokens_ref, first, step, rows, columns)):
            outs[(first + row) // CHUNK][(first + row) % CHUNK] = part.astype(jnp.bfloat16)


def left_kernel(
    tokens_ref, pair_ref, gain_ref, bias_ref, weights_ref, gate_weights_ref, left_ref, gate_ref
):
    rows, columns, _ = pair_ref.shape
    hidden = left_ref.shape[2]
    channels = gate_ref.shape[2]
    step = 4
    for first in range(0, rows, step):
        normed = normed_rows(pair_ref, gain_ref, bias_ref, first, step)
        left = gated(normed, weights_ref, 0, hidden)
        for row, part in enumerate(masked(left, tokens_ref, first, step, rows, columns)):
            left_ref[first + row] = part.astype(jnp.bfloat16)
        gate = jax.nn.sigmoid(
            jnp.dot(normed, gate_weights_ref[...], preferred_element_type=jnp.float32)
        )
        gate_ref[pl.ds(first, step)] = gate.reshape(step, columns, channels)


def turned(pieces, width):
    rows = sum(piece.shape[0] for piece in pieces)
    hidden = pieces[0].shape[1]
    if width > rows:
        pieces = pieces + [jnp.zeros((width - rows, hidden), pieces[0].dtype)]
    stacked = jnp.concatenate(pieces, axis=0)
    row = lax.broadcasted_iota(jnp.int32, (hidden, hidden), 0)
    column = lax.broadcasted_iota(jnp.int32, (hidden, hidden), 1)
    identity = (row == column).astype(jnp.float32).astype(jnp.bfloat16)
    return lax.dot_general(
        identity, stacked, (((1,), (1,)), ((), ())), preferred_element_type=jnp.float32
    )


def turn_kernel(*refs):
    pieces, (out_ref, scratch) = refs[:-2], refs[-2:]
    rows, _, hidden = pieces[0].shape
    width = out_ref.shape[2]
    for row in range(rows):
        one = turned([ref[row] for ref in pieces], width)
        for at in range(0, width, LANES):
            scratch[at // LANES, pl.ds(row, hidden, stride=rows), :] = one[:, at : at + LANES]
    for channel in range(hidden):
        for at in range(0, width, LANES):
            one = scratch[at // LANES, pl.ds(channel * rows, rows), :]
            out_ref[channel, :, at : at + LANES] = one.astype(jnp.bfloat16)


def product_kernel(picks, rights, *refs):
    right_refs, refs = refs[:rights], refs[rights:]
    left_ref, gate_ref, gain_ref, bias_ref, weights_ref, *_, out_ref = refs[:-5]
    held, arrived, right, product, updates = refs[-5:]
    hidden, rows, width = left_ref.shape
    even = (lax.axis_index("row") + lax.axis_index("col")) % 2 == 0

    def fetch(source, at):
        return pltpu.make_async_copy(right_refs[source], held.at[at], arrived.at[at])

    for at, (at_even, at_odd) in enumerate(picks):
        if at_even == at_odd:
            fetch(at_even, at).start()
        else:
            pl.when(even)(fetch(at_even, at).start)
            pl.when(jnp.logical_not(even))(fetch(at_odd, at).start)
    for at, (at_even, _) in enumerate(picks):
        fetch(at_even, at).wait()

    for token in range(CHUNK):
        pieces = [held[at, token] for at in range(len(picks))]
        one = turned(pieces, width)
        for at in range(0, width, LANES):
            right[at // LANES, pl.ds(token, hidden, stride=CHUNK), :] = one[:, at : at + LANES]

    total = jnp.zeros((CHUNK, rows), jnp.float32)
    for channel in range(hidden):
        one = 0.0
        for at in range(0, width, LANES):
            one += lax.dot_general(
                right[at // LANES, pl.ds(channel * CHUNK, CHUNK), :].astype(jnp.bfloat16),
                left_ref[channel, :, at : at + LANES],
                (((1,), (1,)), ((), ())),
                preferred_element_type=jnp.float32,
            )
        product[pl.ds(channel * CHUNK, CHUNK), :rows] = one
        total += one
    average = total / hidden
    total = jnp.zeros((CHUNK, rows), jnp.float32)
    for channel in range(hidden):
        centered = product[pl.ds(channel * CHUNK, CHUNK), :rows] - average
        total += centered * centered
    scale = lax.rsqrt(total / hidden + 1e-05)
    for channel in range(hidden):
        place = pl.ds(channel * CHUNK, CHUNK)
        centered = product[place, :rows] - average
        product[place, :rows] = centered * scale * gain_ref[channel] + bias_ref[channel]
    for token in range(CHUNK):
        mixed = product[pl.ds(token, hidden, stride=CHUNK), :][:, :rows].astype(jnp.bfloat16)
        updates[pl.ds(token, rows, stride=CHUNK), :] = lax.dot_general(
            mixed, weights_ref[...], (((0,), (0,)), ((), ())), preferred_element_type=jnp.float32
        )
    step = 8
    for first in range(0, rows, step):
        gate = gate_ref[pl.ds(first, step)]
        update = updates[pl.ds(first * CHUNK, step * CHUNK), :].reshape(gate.shape)
        out_ref[pl.ds(first, step)] = (gate * update).astype(jnp.bfloat16)


def band_by_sums(chunks, window, row_count, col_count):
    blocks_per_row = col_count // row_count
    col_pos = lax.axis_index("col")
    per_block = len(chunks) // blocks_per_row
    stacked = jnp.stack(chunks)
    pieces = []
    for offset in range(window):
        block_id = (col_pos - offset) % col_count
        start = block_id % blocks_per_row * per_block
        received = from_root(
            lax.dynamic_slice_in_dim(stacked, start, per_block, 0), "row", block_id // blocks_per_row
        )
        pieces.append(received if offset == 0 else shifted(received, "col", -offset))
    bands = [[piece[at] for piece in pieces] for at in range(per_block)]
    return bands, [(offset, offset) for offset in range(window)]


def band_by_hops(chunks):
    row_pos = lax.axis_index("row")
    col_pos = lax.axis_index("col")

    def at(r, c):
        return r % 4 * 4 + c % 4

    def move(array, pairs):
        return lax.ppermute(array, ("row", "col"), pairs)

    everyone = [(r, c) for r in range(4) for c in range(4)]
    roots = [(r, c) for r, c in everyone if (c - r) % 4 < 2]
    is_root = (col_pos - row_pos) % 4 < 2
    bands = []
    for chunk in chunks:
        far = move(chunk, [(at(r, c), at(r ^ 2, c)) for r, c in roots])
        held = jnp.where(is_root, chunk, far)
        near = move(
            held,
            [
                (at(r, c), at(r ^ 1, c) if (r + c) % 2 == 0 else at(r, c - 1))
                for r, c in everyone
            ],
        )
        cross = move(
            held, [(at(r, c), at(r ^ 1, c - 1)) for r, c in everyone if (r + c) % 2 == 1]
        )
        bands.append([held, near, cross])
    return bands, [(0, 1), (1, 2)]


def on_device(
    pair_state,
    token_count,
    in_gain,
    in_bias,
    in_weights,
    gate_weights,
    out_gain,
    out_bias,
    out_weights,
):
    rows, columns, channels = pair_state.shape
    hidden = out_weights.shape[0]
    tokens = rows * columns
    col_count = lax.axis_size("col")
    row_count = lax.axis_size("row")
    window = col_count // 2
    in_gain, in_bias = in_gain.reshape(1, channels), in_bias.reshape(1, channels)
    block = 2 * tokens * max(channels, hidden)
    smem, vmem = whole(pltpu.SMEM), whole()

    chunks = pl.pallas_call(
        right_kernel,
        out_shape=[jax.ShapeDtypeStruct((CHUNK, columns, hidden), jnp.bfloat16)] * (rows // CHUNK),
        in_specs=[smem] + [vmem] * 4,
        out_specs=[vmem] * (rows // CHUNK),
        compiler_params=params(2 * block),
        cost_estimate=pl.CostEstimate(
            flops=4 * tokens * channels * hidden, bytes_accessed=4 * tokens * channels, transcendentals=0
        ),
        name="right",
    )(token_count, pair_state, in_gain, in_bias, in_weights)

    left, gate = pl.pallas_call(
        left_kernel,
        out_shape=[
            jax.ShapeDtypeStruct((rows, columns, hidden), jnp.bfloat16),
            jax.ShapeDtypeStruct((rows, columns, channels), jnp.float32),
        ],
        in_specs=[smem] + [vmem] * 5,
        out_specs=[vmem] * 2,
        compiler_params=params(4 * block),
        cost_estimate=pl.CostEstimate(
            flops=6 * tokens * channels * hidden, bytes_accessed=8 * tokens * channels, transcendentals=0
        ),
        name="left_and_gate",
    )(token_count, pair_state, in_gain, in_bias, in_weights, gate_weights)

    if row_count == 4 and col_count == 4:
        bands, picks = band_by_hops(chunks)
    else:
        bands, picks = band_by_sums(chunks, window, row_count, col_count)
    lefts = [left]
    for _ in range(window - 1):
        lefts.append(shifted(lefts[-1], "col", -1))

    depth = window * columns
    width = -(-depth // LANES) * LANES
    turned_left = pl.pallas_call(
        turn_kernel,
        out_shape=jax.ShapeDtypeStruct((hidden, rows, width), jnp.bfloat16),
        in_specs=[vmem] * window,
        out_specs=vmem,
        scratch_shapes=[pltpu.VMEM((width // LANES, hidden * rows, LANES), jnp.float32)],
        compiler_params=params(window * block, 6 * hidden * rows * width),
        cost_estimate=pl.CostEstimate(
            flops=2 * rows * width * hidden * hidden,
            bytes_accessed=4 * rows * width * hidden,
            transcendentals=0,
        ),
        name="turn_left",
    )(*lefts)

    update = []
    for at, band in enumerate(bands):
        chunk_of = pl.BlockSpec((rows, CHUNK, channels), lambda step, at=at: (0, at, 0))
        filled = pl.pallas_call(
            functools.partial(product_kernel, picks, len(band)),
            grid=(1,),
            out_shape=jax.ShapeDtypeStruct((rows, columns, channels), jnp.bfloat16),
            in_specs=[whole(pl.ANY)] * len(band)
            + [vmem, chunk_of, smem, smem, vmem]
            + [whole(pl.ANY)] * len(update),
            out_specs=chunk_of,
            scratch_shapes=[
                pltpu.VMEM((window, CHUNK, columns, hidden), jnp.bfloat16),
                pltpu.SemaphoreType.DMA((window,)),
                pltpu.VMEM((width // LANES, hidden * CHUNK, LANES), jnp.float32),
                pltpu.VMEM((hidden * CHUNK, LANES), jnp.float32),
                pltpu.VMEM((rows * CHUNK, channels), jnp.float32),
            ],
            input_output_aliases={len(band) + 5: 0} if update else {},
            compiler_params=params(2 * block, 2 * hidden * (rows + 2 * CHUNK) * width),
            cost_estimate=pl.CostEstimate(
                flops=2 * rows * CHUNK * depth * hidden,
                bytes_accessed=2 * rows * depth * hidden,
                transcendentals=0,
            ),
            name="product",
        )(*band, turned_left, gate, out_gain, out_bias, out_weights, *update)
        update = [filled]
    return filled


def solution(mesh):
    placed = (P(("crops", "row"), "col", None), P("crops"), P(), P(), P(), P(), P(), P(), P())
    return jax.shard_map(
        on_device,
        mesh=mesh,
        in_specs=placed,
        out_specs=P(("crops", "row"), "col", None),
        check_vma=False,
    )
```

```python
import functools

import jax
import jax.numpy as jnp
from jax import lax
from jax.experimental import pallas as pl
from jax.experimental.pallas import tpu as pltpu
from jax.sharding import PartitionSpec as P

LANES = 128
MIB = 1024 * 1024


def params(*sizes):
    return pltpu.CompilerParams(vmem_limit_bytes=min(6 * MIB + 2 * sum(sizes), 56 * MIB))


def cost(flops, bytes_accessed):
    return pl.CostEstimate(flops=flops, bytes_accessed=bytes_accessed, transcendentals=0)


VMEM = pl.BlockSpec(memory_space=pltpu.VMEM)
SMEM = pl.BlockSpec(memory_space=pltpu.SMEM)
ANY = pl.BlockSpec(memory_space=pl.ANY)


def shifted(array, axis, by):
    devices = lax.axis_size(axis)
    return lax.ppermute(array, axis, [(i, (i + by) % devices) for i in range(devices)])


def from_root(array, axis, root):
    mine = lax.axis_index(axis) == root
    return lax.psum(jnp.where(mine, array, jnp.zeros_like(array)), axis)


def layer_norm(values, gain, offset):
    average = jnp.mean(values, axis=-1, keepdims=True)
    centered = values - average
    variance = jnp.mean(centered * centered, axis=-1, keepdims=True)
    return centered * lax.rsqrt(variance + 1e-05) * gain + offset


def normed_rows(block, gain_ref, bias_ref):
    rows, columns, channels = block.shape
    values = block.reshape(rows * columns, channels).astype(jnp.float32)
    return layer_norm(values, gain_ref[...], bias_ref[...]).astype(jnp.bfloat16)


def right_kernel(hops, first, tokens_ref, pair_ref, gain_ref, bias_ref, weights_ref, *refs):
    out_ref = refs[-1]
    count, columns, hidden = out_ref.shape
    row_pos, col_pos = lax.axis_index("row"), lax.axis_index("col")
    tokens = tokens_ref[0]
    block_row = row_pos
    if hops:
        is_root = (col_pos - row_pos + 4) % 4 < 2
        block_row = jnp.where((row_pos + col_pos) % 2 == 0, col_pos, (col_pos + 3) % 4)
    row_start = block_row * pair_ref.shape[0] + first
    valid_columns = tokens - col_pos * columns
    position = lax.broadcasted_iota(jnp.int32, (columns, hidden), 0)
    step = 4
    for at in range(0, count, step):
        block = pair_ref[pl.ds(first + at, step)]
        if hops:
            block = jnp.where(is_root, block, refs[0][pl.ds(at, step)])
        normed = normed_rows(block, gain_ref, bias_ref)
        both = jnp.dot(
            normed, weights_ref[...], preferred_element_type=jnp.float32
        )
        right = jax.nn.sigmoid(both[:, :hidden]) * both[:, hidden:]
        for row in range(step):
            limit = jnp.where(row_start + at + row < tokens, valid_columns, 0)
            part = right[row * columns : (row + 1) * columns]
            out_ref[at + row] = jnp.where(position < limit, part, 0.0).astype(jnp.bfloat16)


def left_kernel(blocks, tokens_ref, *refs):
    pair_refs, refs = refs[:blocks], refs[blocks:]
    gain_ref, bias_ref, weights_ref, gate_weights_ref, *passed, scratch = refs
    passed, (left_ref, gate_ref), handed = passed[:4], passed[4:6], passed[6:]
    for source, target in zip(passed, handed):
        target[...] = source[...]
    rows, columns, channels = pair_refs[0].shape
    hidden, _, width = left_ref.shape
    tokens = tokens_ref[0]
    row_start = lax.axis_index("row") * rows
    col_pos, col_count = lax.axis_index("col"), lax.axis_size("col")
    lane = lax.broadcasted_iota(jnp.int32, (1, width), 1)
    keep = jnp.zeros((1, width), jnp.float32)
    for at in range(blocks):
        end = at * columns + jnp.minimum(tokens - (col_pos + at) % col_count * columns, columns)
        keep += jnp.where((lane >= at * columns) & (lane < end), 1.0, 0.0)
    padding = [jnp.zeros((width - blocks * columns, channels), jnp.bfloat16)]
    if width == blocks * columns:
        padding = []
    step = 4
    for first in range(0, rows, step):
        normed = [normed_rows(ref[pl.ds(first, step)], gain_ref, bias_ref) for ref in pair_refs]
        gate = jnp.dot(normed[0], gate_weights_ref[...], preferred_element_type=jnp.float32)
        gate_ref[pl.ds(first, step)] = jax.nn.sigmoid(gate).reshape(step, columns, channels)
        for row in range(step):
            thirds = [piece[row * columns : (row + 1) * columns] for piece in normed]
            both = lax.dot_general(
                weights_ref[...],
                jnp.concatenate(thirds + padding, axis=0),
                (((1,), (1,)), ((), ())),
                preferred_element_type=jnp.float32,
            )
            left = jax.nn.sigmoid(both[:hidden]) * both[hidden:]
            valid = jnp.where(row_start + first + row < tokens, keep, 0.0)
            left = jnp.where(valid > 0.0, left, 0.0)
            for at in range(0, width, LANES):
                scratch[at // LANES, pl.ds(first + row, hidden, stride=rows), :] = left[
                    :, at : at + LANES
                ]
    for channel in range(hidden):
        for at in range(0, width, LANES):
            one = scratch[at // LANES, pl.ds(channel * rows, rows), :]
            left_ref[channel, :, at : at + LANES] = one.astype(jnp.bfloat16)


def turned(pieces, width):
    rows = sum(piece.shape[0] for piece in pieces)
    hidden = pieces[0].shape[1]
    if width > rows:
        pieces = pieces + [jnp.zeros((width - rows, hidden), pieces[0].dtype)]
    row = lax.broadcasted_iota(jnp.int32, (hidden, hidden), 0)
    column = lax.broadcasted_iota(jnp.int32, (hidden, hidden), 1)
    identity = (row == column).astype(jnp.float32).astype(jnp.bfloat16)
    return lax.dot_general(
        identity,
        jnp.concatenate(pieces, axis=0),
        (((1,), (1,)), ((), ())),
        preferred_element_type=jnp.float32,
    )


def product_kernel(picks, rights, first, *refs):
    right_refs, refs = refs[:rights], refs[rights:]
    left_ref, gate_ref, gain_ref, bias_ref, weights_ref, *_, out_ref = refs[:-5]
    right, product, updates, result, sent = refs[-5:]
    hidden, rows, width = left_ref.shape
    count = right_refs[0].shape[0]
    even = (lax.axis_index("row") + lax.axis_index("col")) % 2 == 0

    for token in range(count):
        pieces = []
        for at_even, at_odd in picks:
            piece = right_refs[at_even][token]
            if at_odd != at_even:
                piece = jnp.where(even, piece, right_refs[at_odd][token])
            pieces.append(piece)
        one = turned(pieces, width)
        for at in range(0, width, LANES):
            right[at // LANES, pl.ds(token, hidden, stride=count), :] = one[:, at : at + LANES]

    total = jnp.zeros((count, rows), jnp.float32)
    for channel in range(hidden):
        one = 0.0
        for at in range(0, width, LANES):
            one += lax.dot_general(
                right[at // LANES, pl.ds(channel * count, count), :].astype(jnp.bfloat16),
                left_ref[channel, :, at : at + LANES],
                (((1,), (1,)), ((), ())),
                preferred_element_type=jnp.float32,
            )
        product[pl.ds(channel * count, count), :rows] = one
        total += one
    average = total / hidden
    total = jnp.zeros((count, rows), jnp.float32)
    for channel in range(hidden):
        centered = product[pl.ds(channel * count, count), :rows] - average
        total += centered * centered
    scale = lax.rsqrt(total / hidden + 1e-05)
    for channel in range(hidden):
        place = pl.ds(channel * count, count)
        centered = product[place, :rows] - average
        product[place, :rows] = centered * scale * gain_ref[channel] + bias_ref[channel]
    for token in range(count):
        mixed = product[pl.ds(token, hidden, stride=count), :][:, :rows].astype(jnp.bfloat16)
        updates[pl.ds(token, rows, stride=count), :] = lax.dot_general(
            mixed, weights_ref[...], (((0,), (0,)), ((), ())), preferred_element_type=jnp.float32
        )
    step = 8
    for at in range(0, rows, step):
        gate = gate_ref[pl.ds(at, step), pl.ds(first, count)]
        update = updates[pl.ds(at * count, step * count), :].reshape(gate.shape)
        result[pl.ds(at, step)] = (gate * update).astype(jnp.bfloat16)
    copy = pltpu.make_async_copy(result, out_ref.at[:, pl.ds(first, count)], sent)
    copy.start()
    copy.wait()


def band_by_sums(right, spans, window, row_count, col_count, columns):
    blocks_per_row = col_count // row_count
    col_pos = lax.axis_index("col")
    pieces = []
    for offset in range(window):
        block_id = (col_pos - offset) % col_count
        start = block_id % blocks_per_row * columns
        received = from_root(
            lax.dynamic_slice_in_dim(right, start, columns, 0), "row", block_id // blocks_per_row
        )
        pieces.append(received if offset == 0 else shifted(received, "col", -offset))
    bands = [[piece[first : first + count] for piece in pieces] for first, count in spans]
    return bands, [(offset, offset) for offset in range(window)]


def band_by_hops(pair_state, right_of, spans):
    def at(r, c):
        return r % 4 * 4 + c % 4

    def move(array, pairs):
        return lax.ppermute(array, ("row", "col"), pairs)

    everyone = [(r, c) for r in range(4) for c in range(4)]
    roots = [(r, c) for r, c in everyone if (c - r) % 4 < 2]
    fars = [
        move(pair_state[first : first + count], [(at(r, c), at(r ^ 2, c)) for r, c in roots])
        for first, count in spans
    ]
    bands = []
    for (first, count), far in zip(spans, fars):
        held = right_of(first, count, far)
        near = move(
            held,
            [
                (at(r, c), at(r ^ 1, c) if (r + c) % 2 == 0 else at(r, c - 1))
                for r, c in everyone
            ],
        )
        cross = move(
            held, [(at(r, c), at(r ^ 1, c - 1)) for r, c in everyone if (r + c) % 2 == 1]
        )
        bands.append([held, near, cross])
    return bands, [(0, 1), (1, 2)]


def on_device(
    pair_state,
    token_count,
    in_gain,
    in_bias,
    in_weights,
    gate_weights,
    out_gain,
    out_bias,
    out_weights,
):
    rows, columns, channels = pair_state.shape
    hidden = out_weights.shape[0]
    tokens = rows * columns
    col_count = lax.axis_size("col")
    row_count = lax.axis_size("row")
    window = col_count // 2
    depth = window * columns
    width = -(-depth // LANES) * LANES
    in_gain, in_bias = in_gain.reshape(1, channels), in_bias.reshape(1, channels)
    block = 2 * tokens * max(channels, hidden)
    hops = row_count == 4 and col_count == 4
    last = 16
    spans = [(0, columns - last), (columns - last, last)]

    pairs = [pair_state]
    for _ in range(window - 1):
        pairs.append(shifted(pairs[-1], "col", -1))
    passed = [in_gain, in_bias, in_weights[:, 2 * hidden :], out_weights]
    left, gate, *handed = pl.pallas_call(
        functools.partial(left_kernel, window),
        out_shape=[
            jax.ShapeDtypeStruct((hidden, rows, width), jnp.bfloat16),
            jax.ShapeDtypeStruct((rows, columns, channels), jnp.float32),
        ]
        + [jax.ShapeDtypeStruct(array.shape, array.dtype) for array in passed],
        in_specs=[SMEM] + [VMEM] * (window + 8),
        out_specs=[VMEM] * 6,
        scratch_shapes=[pltpu.VMEM((width // LANES, hidden * rows, LANES), jnp.float32)],
        compiler_params=params((window + 2) * block, 6 * hidden * rows * width),
        cost_estimate=cost(
            4 * window * tokens * channels * hidden, 6 * rows * width * hidden
        ),
        name="left_and_gate",
    )(token_count, *pairs, in_gain, in_bias, in_weights[:, : 2 * hidden].T, gate_weights, *passed)
    in_gain, in_bias, right_weights, out_weights = handed

    def right_of(first, count, *far):
        return pl.pallas_call(
            functools.partial(right_kernel, hops, first),
            out_shape=jax.ShapeDtypeStruct((count, columns, hidden), jnp.bfloat16),
            in_specs=[SMEM] + [VMEM] * (4 + len(far)),
            out_specs=VMEM,
            compiler_params=params(2 * block),
            cost_estimate=cost(4 * count * columns * channels * hidden, 6 * count * columns * channels),
            name="right",
        )(token_count, pair_state, in_gain, in_bias, right_weights, *far)

    if hops:
        bands, picks = band_by_hops(pair_state, right_of, spans)
    else:
        bands, picks = band_by_sums(
            right_of(0, rows), spans, window, row_count, col_count, columns
        )

    update = []
    for (first, count), band in zip(spans, bands):
        filled = pl.pallas_call(
            functools.partial(product_kernel, picks, len(band), first),
            out_shape=jax.ShapeDtypeStruct((rows, columns, channels), jnp.bfloat16),
            in_specs=[VMEM] * (len(band) + 2) + [SMEM, SMEM, VMEM] + [ANY] * len(update),
            out_specs=ANY,
            scratch_shapes=[
                pltpu.VMEM((width // LANES, hidden * count, LANES), jnp.float32),
                pltpu.VMEM((hidden * count, LANES), jnp.float32),
                pltpu.VMEM((rows * count, channels), jnp.float32),
                pltpu.VMEM((rows, count, channels), jnp.bfloat16),
                pltpu.SemaphoreType.DMA,
            ],
            input_output_aliases={len(band) + 5: 0} if update else {},
            compiler_params=params(2 * block, 2 * hidden * (rows + 2 * count) * width),
            cost_estimate=cost(
                2 * rows * count * depth * hidden, 4 * rows * depth * hidden
            ),
            name="product",
        )(*band, left, gate, out_gain, out_bias, out_weights, *update)
        update = [filled]
    return filled


def solution(mesh):
    placed = (P(("crops", "row"), "col", None), P("crops"), P(), P(), P(), P(), P(), P(), P())
    return jax.shard_map(
        on_device,
        mesh=mesh,
        in_specs=placed,
        out_specs=P(("crops", "row"), "col", None),
        check_vma=False,
    )
```

```python
import functools

import jax
import jax.numpy as jnp
from jax import lax
from jax.experimental import pallas as pl
from jax.experimental.pallas import tpu as pltpu
from jax.sharding import PartitionSpec as P

LANES = 128
MIB = 1024 * 1024


def params(*sizes):
    return pltpu.CompilerParams(vmem_limit_bytes=min(6 * MIB + 2 * sum(sizes), 56 * MIB))


def cost(flops, bytes_accessed):
    return pl.CostEstimate(flops=flops, bytes_accessed=bytes_accessed, transcendentals=0)


VMEM = pl.BlockSpec(memory_space=pltpu.VMEM)
SMEM = pl.BlockSpec(memory_space=pltpu.SMEM)
ANY = pl.BlockSpec(memory_space=pl.ANY)


def shifted(array, axis, by):
    devices = lax.axis_size(axis)
    return lax.ppermute(array, axis, [(i, (i + by) % devices) for i in range(devices)])


def from_root(array, axis, root):
    mine = lax.axis_index(axis) == root
    return lax.psum(jnp.where(mine, array, jnp.zeros_like(array)), axis)


def layer_norm(values, gain, offset):
    average = jnp.mean(values, axis=-1, keepdims=True)
    centered = values - average
    variance = jnp.mean(centered * centered, axis=-1, keepdims=True)
    return centered * lax.rsqrt(variance + 1e-05) * gain + offset


def normed_rows(block, gain_ref, bias_ref):
    rows, columns, channels = block.shape
    values = block.reshape(rows * columns, channels).astype(jnp.float32)
    return layer_norm(values, gain_ref[...], bias_ref[...]).astype(jnp.bfloat16)


def right_kernel(origin, tokens_ref, pair_ref, gain_ref, bias_ref, weights_ref, *outs):
    columns, hidden = outs[0].shape[1:]
    row_block, third_block = origin()
    tokens = tokens_ref[0]
    row_start = row_block * pair_ref.shape[0]
    valid_columns = tokens - third_block * columns
    position = lax.broadcasted_iota(jnp.int32, (columns, hidden), 0)
    step = 4
    first = 0
    for out_ref in outs:
        for at in range(0, out_ref.shape[0], step):
            normed = normed_rows(pair_ref[pl.ds(first + at, step)], gain_ref, bias_ref)
            both = jnp.dot(normed, weights_ref[...], preferred_element_type=jnp.float32)
            right = jax.nn.sigmoid(both[:, :hidden]) * both[:, hidden:]
            for row in range(step):
                limit = jnp.where(row_start + first + at + row < tokens, valid_columns, 0)
                part = right[row * columns : (row + 1) * columns]
                out_ref[at + row] = jnp.where(position < limit, part, 0.0).astype(jnp.bfloat16)
        first += out_ref.shape[0]


def left_kernel(blocks, tokens_ref, *refs):
    pair_refs, refs = refs[:blocks], refs[blocks:]
    gain_ref, bias_ref, weights_ref, gate_weights_ref, *passed, scratch = refs
    passed, (left_ref, gate_ref), handed = passed[:4], passed[4:6], passed[6:]
    for source, target in zip(passed, handed):
        target[...] = source[...]
    rows, columns, channels = pair_refs[0].shape
    hidden, _, width = left_ref.shape
    tokens = tokens_ref[0]
    row_start = lax.axis_index("row") * rows
    col_pos, col_count = lax.axis_index("col"), lax.axis_size("col")
    lane = lax.broadcasted_iota(jnp.int32, (1, width), 1)
    keep = jnp.zeros((1, width), jnp.float32)
    for at in range(blocks):
        end = at * columns + jnp.minimum(tokens - (col_pos + at) % col_count * columns, columns)
        keep += jnp.where((lane >= at * columns) & (lane < end), 1.0, 0.0)
    padding = [jnp.zeros((width - blocks * columns, channels), jnp.bfloat16)]
    if width == blocks * columns:
        padding = []
    step = 4
    for first in range(0, rows, step):
        normed = [normed_rows(ref[pl.ds(first, step)], gain_ref, bias_ref) for ref in pair_refs]
        gate = jnp.dot(normed[0], gate_weights_ref[...], preferred_element_type=jnp.float32)
        gate_ref[pl.ds(first, step)] = jax.nn.sigmoid(gate).reshape(step, columns, channels)
        for row in range(step):
            thirds = [piece[row * columns : (row + 1) * columns] for piece in normed]
            both = lax.dot_general(
                weights_ref[...],
                jnp.concatenate(thirds + padding, axis=0),
                (((1,), (1,)), ((), ())),
                preferred_element_type=jnp.float32,
            )
            left = jax.nn.sigmoid(both[:hidden]) * both[hidden:]
            valid = jnp.where(row_start + first + row < tokens, keep, 0.0)
            left = jnp.where(valid > 0.0, left, 0.0)
            for at in range(0, width, LANES):
                scratch[at // LANES, pl.ds(first + row, hidden, stride=rows), :] = left[
                    :, at : at + LANES
                ]
    for channel in range(hidden):
        for at in range(0, width, LANES):
            one = scratch[at // LANES, pl.ds(channel * rows, rows), :]
            left_ref[channel, :, at : at + LANES] = one.astype(jnp.bfloat16)


def turned(pieces, width):
    rows = sum(piece.shape[0] for piece in pieces)
    hidden = pieces[0].shape[1]
    if width > rows:
        pieces = pieces + [jnp.zeros((width - rows, hidden), pieces[0].dtype)]
    row = lax.broadcasted_iota(jnp.int32, (hidden, hidden), 0)
    column = lax.broadcasted_iota(jnp.int32, (hidden, hidden), 1)
    identity = (row == column).astype(jnp.float32).astype(jnp.bfloat16)
    return lax.dot_general(
        identity,
        jnp.concatenate(pieces, axis=0),
        (((1,), (1,)), ((), ())),
        preferred_element_type=jnp.float32,
    )


def product_kernel(picks, place, rights, first, count, *refs):
    right_refs, refs = refs[:rights], refs[rights:]
    left_ref, gate_ref, gain_ref, bias_ref, weights_ref, *_, out_ref = refs[:-5]
    right, product, updates, result, sent = refs[-5:]
    hidden, rows, width = left_ref.shape
    mine = place()

    def row_of(source, token):
        ref = right_refs[source]
        return ref[token if ref.shape[0] == count else first + token]

    for token in range(count):
        pieces = []
        for sources in picks:
            piece = row_of(sources[0], token)
            for at, source in enumerate(sources[1:], 1):
                piece = jnp.where(mine == at, row_of(source, token), piece)
            pieces.append(piece)
        one = turned(pieces, width)
        for at in range(0, width, LANES):
            right[at // LANES, pl.ds(token, hidden, stride=count), :] = one[:, at : at + LANES]

    total = jnp.zeros((count, rows), jnp.float32)
    for channel in range(hidden):
        one = 0.0
        for at in range(0, width, LANES):
            one += lax.dot_general(
                right[at // LANES, pl.ds(channel * count, count), :].astype(jnp.bfloat16),
                left_ref[channel, :, at : at + LANES],
                (((1,), (1,)), ((), ())),
                preferred_element_type=jnp.float32,
            )
        product[pl.ds(channel * count, count), :rows] = one
        total += one
    average = total / hidden
    total = jnp.zeros((count, rows), jnp.float32)
    for channel in range(hidden):
        centered = product[pl.ds(channel * count, count), :rows] - average
        total += centered * centered
    scale = lax.rsqrt(total / hidden + 1e-05)
    for channel in range(hidden):
        place = pl.ds(channel * count, count)
        centered = product[place, :rows] - average
        product[place, :rows] = centered * scale * gain_ref[channel] + bias_ref[channel]
    for token in range(count):
        mixed = product[pl.ds(token, hidden, stride=count), :][:, :rows].astype(jnp.bfloat16)
        updates[pl.ds(token, rows, stride=count), :] = lax.dot_general(
            mixed, weights_ref[...], (((0,), (0,)), ((), ())), preferred_element_type=jnp.float32
        )
    step = 8
    for at in range(0, rows, step):
        gate = gate_ref[pl.ds(at, step), pl.ds(first, count)]
        update = updates[pl.ds(at * count, step * count), :].reshape(gate.shape)
        result[pl.ds(at, step)] = (gate * update).astype(jnp.bfloat16)
    copy = pltpu.make_async_copy(result, out_ref.at[:, pl.ds(first, count)], sent)
    copy.start()
    copy.wait()


def band_by_sums(right, window, row_count, col_count, columns):
    blocks_per_row = col_count // row_count
    col_pos = lax.axis_index("col")
    pieces = []
    for offset in range(window):
        block_id = (col_pos - offset) % col_count
        start = block_id % blocks_per_row * columns
        received = from_root(
            lax.dynamic_slice_in_dim(right, start, columns, 0), "row", block_id // blocks_per_row
        )
        pieces.append(received if offset == 0 else shifted(received, "col", -offset))
    return pieces


def hop_place():
    return lax.axis_index("row") ^ lax.axis_index("col")


def far_origin():
    row_pos, col_pos = lax.axis_index("row"), lax.axis_index("col")
    diagonal = hop_place() == 2
    row_block = jnp.where(diagonal, col_pos, jnp.where(col_pos == 2, row_pos - 2, 3 - row_pos))
    return row_block, jnp.where(diagonal, col_pos, (row_block + 1) % 4)


def hops():
    relay = {0: (2, 2), 1: (3, 2), 2: (1, 0), 3: (0, 0)}
    column = range(4)
    out, near, near_more, far, far_more = [], [], [], [], []
    for c in column:
        out += [((c, c), (c ^ 2, c)), ((c, (c + 1) % 4), relay[c])]
        near += [((c, c), (c ^ 1, c)), ((c, (c + 1) % 4), (c, c))]
        near_more += [((c, (c + 1) % 4), (c ^ 1, c))]
        far += [((c ^ 2, c), (c ^ 3, c)), (relay[c], (c ^ 2, c))]
        far_more += [(relay[c], (c ^ 3, c))]
    return out, near, near_more, far, far_more


def move(array, pairs):
    return lax.ppermute(
        array, ("row", "col"), [(r * 4 + c, to_r * 4 + to_c) for (r, c), (to_r, to_c) in pairs]
    )


def on_device(
    pair_state,
    token_count,
    in_gain,
    in_bias,
    in_weights,
    gate_weights,
    out_gain,
    out_bias,
    out_weights,
):
    rows, columns, channels = pair_state.shape
    hidden = out_weights.shape[0]
    tokens = rows * columns
    col_count = lax.axis_size("col")
    row_count = lax.axis_size("row")
    window = col_count // 2
    depth = window * columns
    width = -(-depth // LANES) * LANES
    in_gain, in_bias = in_gain.reshape(1, channels), in_bias.reshape(1, channels)
    block = 2 * tokens * max(channels, hidden)
    by_hops = row_count == 4 and col_count == 4
    last = 16
    spans = [(0, columns - last), (columns - last, last)]

    def right_of(origin, pair, parts):
        return pl.pallas_call(
            functools.partial(right_kernel, origin),
            out_shape=[
                jax.ShapeDtypeStruct((count, columns, hidden), jnp.bfloat16) for count in parts
            ],
            in_specs=[SMEM] + [VMEM] * 4,
            out_specs=[VMEM] * len(parts),
            compiler_params=params(2 * block),
            cost_estimate=cost(4 * tokens * channels * hidden, 6 * tokens * channels),
            name="right",
        )(token_count, pair, in_gain, in_bias, right_weights)

    def here():
        return lax.axis_index("row"), lax.axis_index("col")

    right_weights = in_weights[:, 2 * hidden :]
    if by_hops:
        out, near, near_more, far, far_more = hops()
        arrived = move(pair_state, out)
    pairs = [pair_state]
    for _ in range(window - 1):
        pairs.append(shifted(pairs[-1], "col", -1))
    (right,) = right_of(here, pair_state, [rows])
    passed = [in_gain, in_bias, right_weights, out_weights]
    left, gate, *handed = pl.pallas_call(
        functools.partial(left_kernel, window),
        out_shape=[
            jax.ShapeDtypeStruct((hidden, rows, width), jnp.bfloat16),
            jax.ShapeDtypeStruct((rows, columns, channels), jnp.float32),
        ]
        + [jax.ShapeDtypeStruct(array.shape, array.dtype) for array in passed],
        in_specs=[SMEM] + [VMEM] * (window + 8),
        out_specs=[VMEM] * 6,
        scratch_shapes=[pltpu.VMEM((width // LANES, hidden * rows, LANES), jnp.float32)],
        compiler_params=params((window + 2) * block, 6 * hidden * rows * width),
        cost_estimate=cost(
            4 * window * tokens * channels * hidden, 6 * rows * width * hidden
        ),
        name="left_and_gate",
    )(token_count, *pairs, in_gain, in_bias, in_weights[:, : 2 * hidden].T, gate_weights, *passed)
    in_gain, in_bias, right_weights, out_weights = handed

    if by_hops:
        near, near_more = move(right, near), move(right, near_more)
        bands = []
        for mine in right_of(far_origin, arrived, [count for _, count in spans]):
            bands.append([right, near, near_more, mine, move(mine, far), move(mine, far_more)])
        picks, place = [(0, 1, 3, 4), (1, 2, 4, 5)], hop_place
    else:
        bands = [band_by_sums(right, window, row_count, col_count, columns)] * len(spans)
        picks, place = [(at,) for at in range(window)], lambda: 0

    update = []
    for (first, count), band in zip(spans, bands):
        filled = pl.pallas_call(
            functools.partial(product_kernel, picks, place, len(band), first, count),
            out_shape=jax.ShapeDtypeStruct((rows, columns, channels), jnp.bfloat16),
            in_specs=[VMEM] * (len(band) + 2) + [SMEM, SMEM, VMEM] + [ANY] * len(update),
            out_specs=ANY,
            scratch_shapes=[
                pltpu.VMEM((width // LANES, hidden * count, LANES), jnp.float32),
                pltpu.VMEM((hidden * count, LANES), jnp.float32),
                pltpu.VMEM((rows * count, channels), jnp.float32),
                pltpu.VMEM((rows, count, channels), jnp.bfloat16),
                pltpu.SemaphoreType.DMA,
            ],
            input_output_aliases={len(band) + 5: 0} if update else {},
            compiler_params=params(2 * block, 2 * hidden * (rows + 2 * count) * width),
            cost_estimate=cost(
                2 * rows * count * depth * hidden, 4 * rows * depth * hidden
            ),
            name="product",
        )(*band, left, gate, out_gain, out_bias, out_weights, *update)
        update = [filled]
    return filled


def solution(mesh):
    placed = (P(("crops", "row"), "col", None), P("crops"), P(), P(), P(), P(), P(), P(), P())
    return jax.shard_map(
        on_device,
        mesh=mesh,
        in_specs=placed,
        out_specs=P(("crops", "row"), "col", None),
        check_vma=False,
    )
```

```python
import functools

import jax
import jax.numpy as jnp
from jax import lax
from jax.experimental import pallas as pl
from jax.experimental.pallas import tpu as pltpu
from jax.sharding import PartitionSpec as P

LANES = 128
MIB = 1024 * 1024


def params(*sizes):
    return pltpu.CompilerParams(vmem_limit_bytes=min(6 * MIB + 2 * sum(sizes), 56 * MIB))


def cost(flops, bytes_accessed):
    return pl.CostEstimate(flops=flops, bytes_accessed=bytes_accessed, transcendentals=0)


VMEM = pl.BlockSpec(memory_space=pltpu.VMEM)
SMEM = pl.BlockSpec(memory_space=pltpu.SMEM)
ANY = pl.BlockSpec(memory_space=pl.ANY)


def shifted(array, axis, by):
    devices = lax.axis_size(axis)
    return lax.ppermute(array, axis, [(i, (i + by) % devices) for i in range(devices)])


def from_root(array, axis, root):
    mine = lax.axis_index(axis) == root
    return lax.psum(jnp.where(mine, array, jnp.zeros_like(array)), axis)


def layer_norm(values, gain, offset):
    average = jnp.mean(values, axis=-1, keepdims=True)
    centered = values - average
    variance = jnp.mean(centered * centered, axis=-1, keepdims=True)
    return centered * lax.rsqrt(variance + 1e-05) * gain + offset


def normed_rows(block, gain_ref, bias_ref):
    rows, columns, channels = block.shape
    values = block.reshape(rows * columns, channels).astype(jnp.float32)
    return layer_norm(values, gain_ref[...], bias_ref[...]).astype(jnp.bfloat16)


def masked_right(both, tokens, row_token, third_block, columns):
    hidden = both.shape[1] // 2
    right = jax.nn.sigmoid(both[:, :hidden]) * both[:, hidden:]
    position = lax.broadcasted_iota(jnp.int32, (columns, hidden), 0)
    parts = []
    for row in range(both.shape[0] // columns):
        limit = jnp.where(row_token + row < tokens, tokens - third_block * columns, 0)
        part = right[row * columns : (row + 1) * columns]
        parts.append(jnp.where(position < limit, part, 0.0).astype(jnp.bfloat16))
    return parts


def right_kernel(origin, first, tokens_ref, pair_ref, gain_ref, bias_ref, weights_ref, out_ref):
    count, columns, _ = out_ref.shape
    row_token, third_block = origin()
    step = 4
    for at in range(0, count, step):
        normed = normed_rows(pair_ref[pl.ds(at, step)], gain_ref, bias_ref)
        both = jnp.dot(normed, weights_ref[...], preferred_element_type=jnp.float32)
        parts = masked_right(both, tokens_ref[0], row_token + first + at, third_block, columns)
        for row, part in enumerate(parts):
            out_ref[at + row] = part


def near_kernel(blocks, later, passes, tokens_ref, *refs):
    pair_refs, refs = refs[:blocks], refs[blocks:]
    left_weights_ref, gate_weights_ref, *refs = refs
    passed, refs = refs[:passes], refs[passes:]
    (left_ref, gate_ref, right_ref, later_ref), handed, scratch = refs[:4], refs[4:-1], refs[-1]
    gain_ref, bias_ref, right_weights_ref = passed[:3]
    rows, columns, channels = pair_refs[0].shape
    hidden, _, width = left_ref.shape
    for source, target in zip(passed, handed):
        target[...] = source[...]
    later_ref[...] = pair_refs[0][pl.ds(later, rows - later)]
    tokens = tokens_ref[0]
    row_start = lax.axis_index("row") * rows
    col_pos, col_count = lax.axis_index("col"), lax.axis_size("col")
    lane = lax.broadcasted_iota(jnp.int32, (1, width), 1)
    keep = jnp.zeros((1, width), jnp.float32)
    for at in range(blocks):
        end = at * columns + jnp.minimum(tokens - (col_pos + at) % col_count * columns, columns)
        keep += jnp.where((lane >= at * columns) & (lane < end), 1.0, 0.0)
    padding = [jnp.zeros((width - blocks * columns, channels), jnp.bfloat16)]
    if width == blocks * columns:
        padding = []
    step = 4
    for first in range(0, rows, step):
        normed = [normed_rows(ref[pl.ds(first, step)], gain_ref, bias_ref) for ref in pair_refs]
        gate = jnp.dot(normed[0], gate_weights_ref[...], preferred_element_type=jnp.float32)
        gate_ref[pl.ds(first, step)] = jax.nn.sigmoid(gate).reshape(step, columns, channels)
        both = jnp.dot(normed[0], right_weights_ref[...], preferred_element_type=jnp.float32)
        parts = masked_right(both, tokens, row_start + first, col_pos, columns)
        for row, part in enumerate(parts):
            right_ref[first + row] = part
        for row in range(step):
            thirds = [piece[row * columns : (row + 1) * columns] for piece in normed]
            both = lax.dot_general(
                left_weights_ref[...],
                jnp.concatenate(thirds + padding, axis=0),
                (((1,), (1,)), ((), ())),
                preferred_element_type=jnp.float32,
            )
            left = jax.nn.sigmoid(both[:hidden]) * both[hidden:]
            valid = jnp.where(row_start + first + row < tokens, keep, 0.0)
            left = jnp.where(valid > 0.0, left, 0.0)
            for at in range(0, width, LANES):
                scratch[at // LANES, pl.ds(first + row, hidden, stride=rows), :] = left[
                    :, at : at + LANES
                ]
    for channel in range(hidden):
        for at in range(0, width, LANES):
            one = scratch[at // LANES, pl.ds(channel * rows, rows), :]
            left_ref[channel, :, at : at + LANES] = one.astype(jnp.bfloat16)


def turned(pieces, width):
    rows = sum(piece.shape[0] for piece in pieces)
    hidden = pieces[0].shape[1]
    if width > rows:
        pieces = pieces + [jnp.zeros((width - rows, hidden), pieces[0].dtype)]
    row = lax.broadcasted_iota(jnp.int32, (hidden, hidden), 0)
    column = lax.broadcasted_iota(jnp.int32, (hidden, hidden), 1)
    identity = (row == column).astype(jnp.float32).astype(jnp.bfloat16)
    return lax.dot_general(
        identity,
        jnp.concatenate(pieces, axis=0),
        (((1,), (1,)), ((), ())),
        preferred_element_type=jnp.float32,
    )


def product_kernel(picks, place, rights, first, count, *refs):
    right_refs, refs = refs[:rights], refs[rights:]
    left_ref, gate_ref, gain_ref, bias_ref, weights_ref, *_, out_ref = refs[:-5]
    right, product, updates, result, sent = refs[-5:]
    hidden, rows, width = left_ref.shape
    mine = place()

    def row_of(source, token):
        ref = right_refs[source]
        return ref[token if ref.shape[0] == count else first + token]

    for token in range(count):
        pieces = []
        for sources in picks:
            piece = row_of(sources[0], token)
            for at, source in enumerate(sources[1:], 1):
                piece = jnp.where(mine == at, row_of(source, token), piece)
            pieces.append(piece)
        one = turned(pieces, width)
        for at in range(0, width, LANES):
            right[at // LANES, pl.ds(token, hidden, stride=count), :] = one[:, at : at + LANES]

    total = jnp.zeros((count, rows), jnp.float32)
    for channel in range(hidden):
        one = 0.0
        for at in range(0, width, LANES):
            one += lax.dot_general(
                right[at // LANES, pl.ds(channel * count, count), :].astype(jnp.bfloat16),
                left_ref[channel, :, at : at + LANES],
                (((1,), (1,)), ((), ())),
                preferred_element_type=jnp.float32,
            )
        product[pl.ds(channel * count, count), :rows] = one
        total += one
    average = total / hidden
    total = jnp.zeros((count, rows), jnp.float32)
    for channel in range(hidden):
        centered = product[pl.ds(channel * count, count), :rows] - average
        total += centered * centered
    scale = lax.rsqrt(total / hidden + 1e-05)
    for channel in range(hidden):
        place = pl.ds(channel * count, count)
        centered = product[place, :rows] - average
        product[place, :rows] = centered * scale * gain_ref[channel] + bias_ref[channel]
    for token in range(count):
        mixed = product[pl.ds(token, hidden, stride=count), :][:, :rows].astype(jnp.bfloat16)
        updates[pl.ds(token, rows, stride=count), :] = lax.dot_general(
            mixed, weights_ref[...], (((0,), (0,)), ((), ())), preferred_element_type=jnp.float32
        )
    step = 8
    for at in range(0, rows, step):
        gate = gate_ref[pl.ds(at, step), pl.ds(first, count)]
        update = updates[pl.ds(at * count, step * count), :].reshape(gate.shape)
        result[pl.ds(at, step)] = (gate * update).astype(jnp.bfloat16)
    copy = pltpu.make_async_copy(result, out_ref.at[:, pl.ds(first, count)], sent)
    copy.start()
    copy.wait()


def band_by_sums(right, window, row_count, col_count, columns):
    blocks_per_row = col_count // row_count
    col_pos = lax.axis_index("col")
    pieces = []
    for offset in range(window):
        block_id = (col_pos - offset) % col_count
        start = block_id % blocks_per_row * columns
        received = from_root(
            lax.dynamic_slice_in_dim(right, start, columns, 0), "row", block_id // blocks_per_row
        )
        pieces.append(received if offset == 0 else shifted(received, "col", -offset))
    return pieces


def hop_place():
    return lax.axis_index("row") ^ lax.axis_index("col")


def hops():
    out, near, near_more, far, far_more = [], [], [], [], []
    for c in range(4):
        after = (c + 1) % 4
        out += [((c, c), (c ^ 2, c)), ((c, after), (c ^ 2, after))]
        near += [((c, c), (c ^ 1, c)), ((c, after), (c, c))]
        near_more += [((c, after), (c ^ 1, c))]
        far += [((c ^ 2, c), (c ^ 3, c)), ((c ^ 2, after), (c ^ 2, c))]
        far_more += [((c ^ 2, after), (c ^ 3, c))]
    return out, near, near_more, far, far_more


def move(array, pairs):
    return lax.ppermute(
        array, ("row", "col"), [(r * 4 + c, to_r * 4 + to_c) for (r, c), (to_r, to_c) in pairs]
    )


def on_device(
    pair_state,
    token_count,
    in_gain,
    in_bias,
    in_weights,
    gate_weights,
    out_gain,
    out_bias,
    out_weights,
):
    rows, columns, channels = pair_state.shape
    hidden = out_weights.shape[0]
    tokens = rows * columns
    col_count = lax.axis_size("col")
    row_count = lax.axis_size("row")
    window = col_count // 2
    depth = window * columns
    width = -(-depth // LANES) * LANES
    in_gain, in_bias = in_gain.reshape(1, channels), in_bias.reshape(1, channels)
    block = 2 * tokens * max(channels, hidden)
    by_hops = row_count == 4 and col_count == 4
    last = 16
    spans = [(0, columns - last), (columns - last, last)]

    def right_of(origin, first, pair):
        count = pair.shape[0]
        return pl.pallas_call(
            functools.partial(right_kernel, origin, first),
            out_shape=jax.ShapeDtypeStruct((count, columns, hidden), jnp.bfloat16),
            in_specs=[SMEM] + [VMEM] * 4,
            out_specs=VMEM,
            compiler_params=params(2 * block),
            cost_estimate=cost(
                4 * count * columns * channels * hidden, 4 * count * columns * channels
            ),
            name="right",
        )(token_count, pair, in_gain, in_bias, right_weights)

    def far_origin():
        col_pos = lax.axis_index("col")
        row_block = jnp.where(hop_place() == 2, col_pos, (col_pos + 3) % 4)
        return row_block * rows, col_pos

    arrived = []
    if by_hops:
        out, near, near_more, far, far_more = hops()
        arrived.append(move(pair_state[: spans[0][1]], out))
    pairs = [pair_state]
    for _ in range(window - 1):
        pairs.append(shifted(pairs[-1], "col", -1))
    later = spans[1][0]
    passed = [in_gain, in_bias, in_weights[:, 2 * hidden :], out_weights]
    left, gate, right, later_pair, *handed = pl.pallas_call(
        functools.partial(near_kernel, window, later, len(passed)),
        out_shape=[
            jax.ShapeDtypeStruct((hidden, rows, width), jnp.bfloat16),
            jax.ShapeDtypeStruct((rows, columns, channels), jnp.float32),
            jax.ShapeDtypeStruct((rows, columns, hidden), jnp.bfloat16),
            jax.ShapeDtypeStruct((rows - later, columns, channels), jnp.bfloat16),
        ]
        + [jax.ShapeDtypeStruct(array.shape, array.dtype) for array in passed],
        in_specs=[SMEM] + [VMEM] * (window + 2 + len(passed)),
        out_specs=[VMEM] * (4 + len(passed)),
        scratch_shapes=[pltpu.VMEM((width // LANES, hidden * rows, LANES), jnp.float32)],
        compiler_params=params((window + 4) * block, 6 * hidden * rows * width),
        cost_estimate=cost(
            4 * (window + 1) * tokens * channels * hidden, 6 * rows * width * hidden
        ),
        name="near",
    )(token_count, *pairs, in_weights[:, : 2 * hidden].T, gate_weights, *passed)
    in_gain, in_bias, right_weights, out_weights = handed

    if by_hops:
        arrived.append(move(later_pair, out))
        near, near_more = move(right, near), move(right, near_more)
        bands = []
        for (first, _), pair in zip(spans, arrived):
            mine = right_of(far_origin, first, pair)
            bands.append([right, near, near_more, mine, move(mine, far), move(mine, far_more)])
        picks, place = [(0, 1, 3, 4), (1, 2, 4, 5)], hop_place
    else:
        bands = [band_by_sums(right, window, row_count, col_count, columns)] * len(spans)
        picks, place = [(at,) for at in range(window)], lambda: 0

    update = []
    for (first, count), band in zip(spans, bands):
        filled = pl.pallas_call(
            functools.partial(product_kernel, picks, place, len(band), first, count),
            out_shape=jax.ShapeDtypeStruct((rows, columns, channels), jnp.bfloat16),
            in_specs=[VMEM] * (len(band) + 2) + [SMEM, SMEM, VMEM] + [ANY] * len(update),
            out_specs=ANY,
            scratch_shapes=[
                pltpu.VMEM((width // LANES, hidden * count, LANES), jnp.float32),
                pltpu.VMEM((hidden * count, LANES), jnp.float32),
                pltpu.VMEM((rows * count, channels), jnp.float32),
                pltpu.VMEM((rows, count, channels), jnp.bfloat16),
                pltpu.SemaphoreType.DMA,
            ],
            input_output_aliases={len(band) + 5: 0} if update else {},
            compiler_params=params(2 * block, 2 * hidden * (rows + 2 * count) * width),
            cost_estimate=cost(
                2 * rows * count * depth * hidden, 4 * rows * depth * hidden
            ),
            name="product",
        )(*band, left, gate, out_gain, out_bias, out_weights, *update)
        update = [filled]
    return filled


def solution(mesh):
    placed = (P(("crops", "row"), "col", None), P("crops"), P(), P(), P(), P(), P(), P(), P())
    return jax.shard_map(
        on_device,
        mesh=mesh,
        in_specs=placed,
        out_specs=P(("crops", "row"), "col", None),
        check_vma=False,
    )
```

```python
import functools

import jax
import jax.numpy as jnp
from jax import lax
from jax.experimental import pallas as pl
from jax.experimental.pallas import tpu as pltpu
from jax.sharding import PartitionSpec as P

LANES = 128
MIB = 1024 * 1024


def params(*sizes):
    return pltpu.CompilerParams(vmem_limit_bytes=min(6 * MIB + 2 * sum(sizes), 56 * MIB))


def cost(flops, bytes_accessed):
    return pl.CostEstimate(flops=flops, bytes_accessed=bytes_accessed, transcendentals=0)


VMEM = pl.BlockSpec(memory_space=pltpu.VMEM)
SMEM = pl.BlockSpec(memory_space=pltpu.SMEM)
ANY = pl.BlockSpec(memory_space=pl.ANY)


def shifted(array, axis, by):
    devices = lax.axis_size(axis)
    return lax.ppermute(array, axis, [(i, (i + by) % devices) for i in range(devices)])


def from_root(array, axis, root):
    mine = lax.axis_index(axis) == root
    return lax.psum(jnp.where(mine, array, jnp.zeros_like(array)), axis)


def layer_norm(values, gain, offset):
    average = jnp.mean(values, axis=-1, keepdims=True)
    centered = values - average
    variance = jnp.mean(centered * centered, axis=-1, keepdims=True)
    return centered * lax.rsqrt(variance + 1e-05) * gain + offset


def normed_rows(block, gain_ref, bias_ref):
    rows, columns, channels = block.shape
    values = block.reshape(rows * columns, channels).astype(jnp.float32)
    return layer_norm(values, gain_ref[...], bias_ref[...]).astype(jnp.bfloat16)


def masked_right(both, tokens, row_token, third_block, columns):
    hidden = both.shape[1] // 2
    right = jax.nn.sigmoid(both[:, :hidden]) * both[:, hidden:]
    position = lax.broadcasted_iota(jnp.int32, (columns, hidden), 0)
    parts = []
    for row in range(both.shape[0] // columns):
        limit = jnp.where(row_token + row < tokens, tokens - third_block * columns, 0)
        part = right[row * columns : (row + 1) * columns]
        parts.append(jnp.where(position < limit, part, 0.0).astype(jnp.bfloat16))
    return parts


def right_kernel(origin, tokens_ref, pair_ref, gain_ref, bias_ref, weights_ref, *outs):
    columns = pair_ref.shape[1]
    row_token, third_block = origin()
    step = 4
    first = 0
    for out_ref in outs:
        for at in range(0, out_ref.shape[0], step):
            normed = normed_rows(pair_ref[pl.ds(first + at, step)], gain_ref, bias_ref)
            both = jnp.dot(normed, weights_ref[...], preferred_element_type=jnp.float32)
            parts = masked_right(both, tokens_ref[0], row_token + first + at, third_block, columns)
            for row, part in enumerate(parts):
                out_ref[at + row] = part
        first += out_ref.shape[0]


def own_kernel(passes, tokens_ref, pair_ref, gate_weights_ref, *refs):
    passed, (right_ref, gate_ref), handed = refs[:passes], refs[passes : passes + 2], refs[passes + 2 :]
    gain_ref, bias_ref, right_weights_ref = passed[:3]
    rows, columns, channels = pair_ref.shape
    for source, target in zip(passed, handed):
        target[...] = source[...]
    row_start = lax.axis_index("row") * rows
    step = 4
    for first in range(0, rows, step):
        normed = normed_rows(pair_ref[pl.ds(first, step)], gain_ref, bias_ref)
        gate = jnp.dot(normed, gate_weights_ref[...], preferred_element_type=jnp.float32)
        gate_ref[pl.ds(first, step)] = jax.nn.sigmoid(gate).reshape(step, columns, channels)
        both = jnp.dot(normed, right_weights_ref[...], preferred_element_type=jnp.float32)
        parts = masked_right(
            both, tokens_ref[0], row_start + first, lax.axis_index("col"), columns
        )
        for row, part in enumerate(parts):
            right_ref[first + row] = part


def left_kernel(blocks, tokens_ref, *refs):
    pair_refs, (gain_ref, bias_ref, weights_ref, left_ref, scratch) = refs[:blocks], refs[blocks:]
    rows, columns, channels = pair_refs[0].shape
    hidden, _, width = left_ref.shape
    tokens = tokens_ref[0]
    row_start = lax.axis_index("row") * rows
    col_pos, col_count = lax.axis_index("col"), lax.axis_size("col")
    lane = lax.broadcasted_iota(jnp.int32, (1, width), 1)
    keep = jnp.zeros((1, width), jnp.float32)
    for at in range(blocks):
        end = at * columns + jnp.minimum(tokens - (col_pos + at) % col_count * columns, columns)
        keep += jnp.where((lane >= at * columns) & (lane < end), 1.0, 0.0)
    padding = [jnp.zeros((width - blocks * columns, channels), jnp.bfloat16)]
    if width == blocks * columns:
        padding = []
    step = 4
    for first in range(0, rows, step):
        normed = [normed_rows(ref[pl.ds(first, step)], gain_ref, bias_ref) for ref in pair_refs]
        for row in range(step):
            thirds = [piece[row * columns : (row + 1) * columns] for piece in normed]
            both = lax.dot_general(
                weights_ref[...],
                jnp.concatenate(thirds + padding, axis=0),
                (((1,), (1,)), ((), ())),
                preferred_element_type=jnp.float32,
            )
            left = jax.nn.sigmoid(both[:hidden]) * both[hidden:]
            valid = jnp.where(row_start + first + row < tokens, keep, 0.0)
            left = jnp.where(valid > 0.0, left, 0.0)
            for at in range(0, width, LANES):
                scratch[at // LANES, pl.ds(first + row, hidden, stride=rows), :] = left[
                    :, at : at + LANES
                ]
    for channel in range(hidden):
        for at in range(0, width, LANES):
            one = scratch[at // LANES, pl.ds(channel * rows, rows), :]
            left_ref[channel, :, at : at + LANES] = one.astype(jnp.bfloat16)


def turned(pieces, width):
    rows = sum(piece.shape[0] for piece in pieces)
    hidden = pieces[0].shape[1]
    if width > rows:
        pieces = pieces + [jnp.zeros((width - rows, hidden), pieces[0].dtype)]
    row = lax.broadcasted_iota(jnp.int32, (hidden, hidden), 0)
    column = lax.broadcasted_iota(jnp.int32, (hidden, hidden), 1)
    identity = (row == column).astype(jnp.float32).astype(jnp.bfloat16)
    return lax.dot_general(
        identity,
        jnp.concatenate(pieces, axis=0),
        (((1,), (1,)), ((), ())),
        preferred_element_type=jnp.float32,
    )


def product_kernel(picks, place, rights, first, count, *refs):
    right_refs, refs = refs[:rights], refs[rights:]
    left_ref, gate_ref, gain_ref, bias_ref, weights_ref, *_, out_ref = refs[:-5]
    right, product, updates, result, sent = refs[-5:]
    hidden, rows, width = left_ref.shape
    mine = place()

    def row_of(source, token):
        ref = right_refs[source]
        return ref[token if ref.shape[0] == count else first + token]

    for token in range(count):
        pieces = []
        for sources in picks:
            piece = row_of(sources[0], token)
            for at, source in enumerate(sources[1:], 1):
                piece = jnp.where(mine == at, row_of(source, token), piece)
            pieces.append(piece)
        one = turned(pieces, width)
        for at in range(0, width, LANES):
            right[at // LANES, pl.ds(token, hidden, stride=count), :] = one[:, at : at + LANES]

    group = max(1, LANES // rows)
    share, lanes = hidden // group, group * rows
    low = [lax.broadcasted_iota(jnp.int32, (count, lanes), 1) < rows * at for at in range(group)]

    def per_lane(values_ref, channel):
        values = jnp.full((count, lanes), values_ref[channel + (group - 1) * share], jnp.float32)
        for at in range(group - 1, 0, -1):
            values = jnp.where(low[at], values_ref[channel + (at - 1) * share], values)
        return values

    def folded(total):
        mean = sum(total[:, at * rows : (at + 1) * rows] for at in range(group)) / hidden
        return jnp.concatenate([mean] * group, axis=1)

    total = jnp.zeros((count, lanes), jnp.float32)
    nothing = jnp.zeros((rows, LANES), jnp.bfloat16)
    for channel in range(share):
        one = 0.0
        for at in range(0, width, LANES):
            rights = [
                right[at // LANES, pl.ds((channel + member * share) * count, count), :].astype(jnp.bfloat16)
                for member in range(group)
            ]
            lefts = [
                jnp.concatenate(
                    [
                        left_ref[channel + member * share, :, at : at + LANES] if here == member else nothing
                        for here in range(group)
                    ],
                    axis=1,
                )
                for member in range(group)
            ]
            one += lax.dot_general(
                jnp.concatenate(rights, axis=1),
                jnp.concatenate(lefts, axis=0),
                (((1,), (1,)), ((), ())),
                preferred_element_type=jnp.float32,
            )
        product[pl.ds(channel * count, count), :lanes] = one
        total += one
    average = folded(total)
    total = jnp.zeros((count, lanes), jnp.float32)
    for channel in range(share):
        centered = product[pl.ds(channel * count, count), :lanes] - average
        total += centered * centered
    scale = lax.rsqrt(folded(total) + 1e-05)
    for channel in range(share):
        place = pl.ds(channel * count, count)
        centered = product[place, :lanes] - average
        product[place, :lanes] = centered * scale * per_lane(gain_ref, channel) + per_lane(bias_ref, channel)
    for token in range(count):
        mixed = product[pl.ds(token, share, stride=count), :].T.astype(jnp.bfloat16)
        updates[pl.ds(token, rows, stride=count), :] = sum(
            jnp.dot(
                mixed[member * rows : (member + 1) * rows],
                weights_ref[pl.ds(member * share, share)],
                preferred_element_type=jnp.float32,
            )
            for member in range(group)
        )
    step = 8
    for at in range(0, rows, step):
        gate = gate_ref[pl.ds(at, step), pl.ds(first, count)]
        update = updates[pl.ds(at * count, step * count), :].reshape(gate.shape)
        result[pl.ds(at, step)] = (gate * update).astype(jnp.bfloat16)
    copy = pltpu.make_async_copy(result, out_ref.at[:, pl.ds(first, count)], sent)
    copy.start()
    copy.wait()


def band_by_sums(right, window, row_count, col_count, columns):
    blocks_per_row = col_count // row_count
    col_pos = lax.axis_index("col")
    pieces = []
    for offset in range(window):
        block_id = (col_pos - offset) % col_count
        start = block_id % blocks_per_row * columns
        received = from_root(
            lax.dynamic_slice_in_dim(right, start, columns, 0), "row", block_id // blocks_per_row
        )
        pieces.append(received if offset == 0 else shifted(received, "col", -offset))
    return pieces


def hop_place():
    col_pos = lax.axis_index("col")
    place = lax.axis_index("row") ^ col_pos
    return jnp.where((place > 1) & (col_pos % 2 == 1), place + 2, place)


def hops():
    out, near, near_more, direct, swap = [], [], [], [], []
    for c in range(4):
        first, second = (c, c), (c, (c + 1) % 4)
        out += [(first, (c ^ 2, c)), (second, (c ^ 3, c))]
        near += [(first, (c ^ 1, c)), (second, (c, c))]
        near_more += [(second, (c ^ 1, c))]
        swap += [((c ^ 2, c), (c ^ 3, c))]
        if c % 2:
            direct += [(second, (c ^ 2, c))]
        else:
            swap += [((c ^ 3, c), (c ^ 2, c))]
    return out, near, near_more, direct, swap


def move(array, pairs):
    return lax.ppermute(
        array, ("row", "col"), [(r * 4 + c, to_r * 4 + to_c) for (r, c), (to_r, to_c) in pairs]
    )


def on_device(
    pair_state,
    token_count,
    in_gain,
    in_bias,
    in_weights,
    gate_weights,
    out_gain,
    out_bias,
    out_weights,
):
    rows, columns, channels = pair_state.shape
    hidden = out_weights.shape[0]
    tokens = rows * columns
    col_count = lax.axis_size("col")
    row_count = lax.axis_size("row")
    window = col_count // 2
    depth = window * columns
    width = -(-depth // LANES) * LANES
    in_gain, in_bias = in_gain.reshape(1, channels), in_bias.reshape(1, channels)
    block = 2 * tokens * max(channels, hidden)
    by_hops = row_count == 4 and col_count == 4
    last = 16
    spans = [(0, columns - last), (columns - last, last)]

    def right_of(origin, pair, counts):
        return pl.pallas_call(
            functools.partial(right_kernel, origin),
            out_shape=[
                jax.ShapeDtypeStruct((count, columns, hidden), jnp.bfloat16) for count in counts
            ],
            in_specs=[SMEM] + [VMEM] * 4,
            out_specs=[VMEM] * len(counts),
            compiler_params=params(2 * block),
            cost_estimate=cost(4 * tokens * channels * hidden, 4 * tokens * channels),
            name="right",
        )(token_count, pair, in_gain, in_bias, right_weights)

    def far_origin():
        col_pos = lax.axis_index("col")
        return col_pos * rows, jnp.where(hop_place() % 2 == 0, col_pos, (col_pos + 1) % 4)

    if by_hops:
        out, near, near_more, direct, swap = hops()
        arrived = move(pair_state, out)
    pairs = [pair_state]
    for _ in range(window - 1):
        pairs.append(shifted(pairs[-1], "col", -1))
    passed = [in_gain, in_bias, in_weights[:, 2 * hidden :], out_weights]
    right, gate, *handed = pl.pallas_call(
        functools.partial(own_kernel, len(passed)),
        out_shape=[
            jax.ShapeDtypeStruct((rows, columns, hidden), jnp.bfloat16),
            jax.ShapeDtypeStruct((rows, columns, channels), jnp.float32),
        ]
        + [jax.ShapeDtypeStruct(array.shape, array.dtype) for array in passed],
        in_specs=[SMEM] + [VMEM] * (2 + len(passed)),
        out_specs=[VMEM] * (2 + len(passed)),
        compiler_params=params(4 * block),
        cost_estimate=cost(6 * tokens * channels * hidden, 8 * tokens * channels),
        name="own",
    )(token_count, pair_state, gate_weights, *passed)
    in_gain, in_bias, right_weights, out_weights = handed
    if by_hops:
        near, direct = move(right, near), move(right, direct)
    left = pl.pallas_call(
        functools.partial(left_kernel, window),
        out_shape=jax.ShapeDtypeStruct((hidden, rows, width), jnp.bfloat16),
        in_specs=[SMEM] + [VMEM] * (window + 3),
        out_specs=VMEM,
        scratch_shapes=[pltpu.VMEM((width // LANES, hidden * rows, LANES), jnp.float32)],
        compiler_params=params((window + 2) * block, 6 * hidden * rows * width),
        cost_estimate=cost(4 * window * tokens * channels * hidden, 6 * rows * width * hidden),
        name="left",
    )(token_count, *pairs, in_gain, in_bias, in_weights[:, : 2 * hidden].T)

    if by_hops:
        mine = right_of(far_origin, arrived, [count for _, count in spans])
        later, *mine = lax.optimization_barrier((right, *mine))
        near_more = move(later, near_more)
        bands = []
        for piece in mine:
            bands.append([right, near, near_more, piece, move(piece, swap), direct])
        picks, place = [(0, 1, 3, 4, 3, 4), (1, 2, 4, 3, 5, 3)], hop_place
    else:
        bands = [band_by_sums(right, window, row_count, col_count, columns)] * len(spans)
        picks, place = [(at,) for at in range(window)], lambda: 0

    update = []
    for (first, count), band in zip(spans, bands):
        filled = pl.pallas_call(
            functools.partial(product_kernel, picks, place, len(band), first, count),
            out_shape=jax.ShapeDtypeStruct((rows, columns, channels), jnp.bfloat16),
            in_specs=[VMEM] * (len(band) + 2) + [SMEM, SMEM, VMEM] + [ANY] * len(update),
            out_specs=ANY,
            scratch_shapes=[
                pltpu.VMEM((width // LANES, hidden * count, LANES), jnp.float32),
                pltpu.VMEM((hidden // max(1, LANES // rows) * count, LANES), jnp.float32),
                pltpu.VMEM((rows * count, channels), jnp.float32),
                pltpu.VMEM((rows, count, channels), jnp.bfloat16),
                pltpu.SemaphoreType.DMA,
            ],
            input_output_aliases={len(band) + 5: 0} if update else {},
            compiler_params=params(2 * block, 2 * hidden * (rows + 2 * count) * width),
            cost_estimate=cost(
                2 * rows * count * depth * hidden, 4 * rows * depth * hidden
            ),
            name="product",
        )(*band, left, gate, out_gain, out_bias, out_weights, *update)
        update = [filled]
    return filled


def solution(mesh):
    placed = (P(("crops", "row"), "col", None), P("crops"), P(), P(), P(), P(), P(), P(), P())
    return jax.shard_map(
        on_device,
        mesh=mesh,
        in_specs=placed,
        out_specs=P(("crops", "row"), "col", None),
        check_vma=False,
    )
```

```python
import functools

import jax
import jax.numpy as jnp
from jax import lax
from jax.experimental import pallas as pl
from jax.experimental.pallas import tpu as pltpu
from jax.sharding import PartitionSpec as P

LANES = 128
MIB = 1024 * 1024


def params(*sizes):
    return pltpu.CompilerParams(vmem_limit_bytes=min(6 * MIB + 2 * sum(sizes), 56 * MIB))


def cost(flops, bytes_accessed):
    return pl.CostEstimate(flops=flops, bytes_accessed=bytes_accessed, transcendentals=0)


VMEM = pl.BlockSpec(memory_space=pltpu.VMEM)
SMEM = pl.BlockSpec(memory_space=pltpu.SMEM)
ANY = pl.BlockSpec(memory_space=pl.ANY)


def pitch(rows):
    return (rows // 8 | 1) * 8


def shifted(array, axis, by):
    devices = lax.axis_size(axis)
    return lax.ppermute(array, axis, [(i, (i + by) % devices) for i in range(devices)])


def from_root(array, axis, root):
    mine = lax.axis_index(axis) == root
    return lax.psum(jnp.where(mine, array, jnp.zeros_like(array)), axis)


def layer_norm(values, gain, offset):
    average = jnp.mean(values, axis=-1, keepdims=True)
    centered = values - average
    variance = jnp.mean(centered * centered, axis=-1, keepdims=True)
    return centered * lax.rsqrt(variance + 1e-05) * gain + offset


def normed_rows(block, gain_ref, bias_ref):
    rows, columns, channels = block.shape
    values = block.reshape(rows * columns, channels).astype(jnp.float32)
    return layer_norm(values, gain_ref[...], bias_ref[...]).astype(jnp.bfloat16)


def right_kernel(hops, first, tokens_ref, pair_ref, gain_ref, bias_ref, weights_ref, *refs):
    out_ref = refs[-1]
    count, columns, hidden = out_ref.shape
    row_pos, col_pos = lax.axis_index("row"), lax.axis_index("col")
    tokens = tokens_ref[0]
    block_row = row_pos
    if hops:
        is_root = (col_pos - row_pos + 4) % 4 < 2
        block_row = jnp.where((row_pos + col_pos) % 2 == 0, col_pos, (col_pos + 3) % 4)
    row_start = block_row * pair_ref.shape[0] + first
    valid_columns = tokens - col_pos * columns
    position = lax.broadcasted_iota(jnp.int32, (columns, hidden), 0)
    step = 4
    for at in range(0, count, step):
        block = pair_ref[pl.ds(first + at, step)]
        if hops:
            block = jnp.where(is_root, block, refs[0][pl.ds(at, step)])
        normed = normed_rows(block, gain_ref, bias_ref)
        both = jnp.dot(
            normed, weights_ref[...], preferred_element_type=jnp.float32
        )
        right = jax.nn.sigmoid(both[:, :hidden]) * both[:, hidden:]
        for row in range(step):
            limit = jnp.where(row_start + at + row < tokens, valid_columns, 0)
            part = right[row * columns : (row + 1) * columns]
            out_ref[at + row] = jnp.where(position < limit, part, 0.0).astype(jnp.bfloat16)


def left_kernel(blocks, later, tokens_ref, *refs):
    pair_refs, refs = refs[:blocks], refs[blocks:]
    gain_ref, bias_ref, weights_ref, gate_weights_ref, *passed, scratch = refs
    passed, (left_ref, gate_ref, later_ref), handed = passed[:4], passed[4:7], passed[7:]
    later_ref[...] = pair_refs[0][pl.ds(later, later_ref.shape[0])]
    for source, target in zip(passed, handed):
        target[...] = source[...]
    rows, columns, channels = pair_refs[0].shape
    hidden, _, width = left_ref.shape
    tokens = tokens_ref[0]
    row_start = lax.axis_index("row") * rows
    col_pos, col_count = lax.axis_index("col"), lax.axis_size("col")
    lane = lax.broadcasted_iota(jnp.int32, (1, width), 1)
    keep = jnp.zeros((1, width), jnp.float32)
    for at in range(blocks):
        end = at * columns + jnp.minimum(tokens - (col_pos + at) % col_count * columns, columns)
        keep += jnp.where((lane >= at * columns) & (lane < end), 1.0, 0.0)
    padding = [jnp.zeros((width - blocks * columns, channels), jnp.bfloat16)]
    if width == blocks * columns:
        padding = []
    step = 4
    for first in range(0, rows, step):
        normed = [normed_rows(ref[pl.ds(first, step)], gain_ref, bias_ref) for ref in pair_refs]
        gate = jnp.dot(normed[0], gate_weights_ref[...], preferred_element_type=jnp.float32)
        gate_ref[pl.ds(first, step)] = jax.nn.sigmoid(gate).reshape(step, columns, channels)
        for row in range(step):
            thirds = [piece[row * columns : (row + 1) * columns] for piece in normed]
            both = lax.dot_general(
                weights_ref[...],
                jnp.concatenate(thirds + padding, axis=0),
                (((1,), (1,)), ((), ())),
                preferred_element_type=jnp.float32,
            )
            left = jax.nn.sigmoid(both[:hidden]) * both[hidden:]
            valid = jnp.where(row_start + first + row < tokens, keep, 0.0)
            left = jnp.where(valid > 0.0, left, 0.0)
            for at in range(0, width, LANES):
                scratch[at // LANES, pl.ds(first + row, hidden, stride=pitch(rows)), :] = left[
                    :, at : at + LANES
                ]
    for channel in range(hidden):
        for at in range(0, width, LANES):
            one = scratch[at // LANES, pl.ds(channel * pitch(rows), rows), :]
            left_ref[channel, :, at : at + LANES] = one.astype(jnp.bfloat16)


def turned(pieces, width):
    rows = sum(piece.shape[0] for piece in pieces)
    hidden = pieces[0].shape[1]
    if width > rows:
        pieces = pieces + [jnp.zeros((width - rows, hidden), pieces[0].dtype)]
    row = lax.broadcasted_iota(jnp.int32, (hidden, hidden), 0)
    column = lax.broadcasted_iota(jnp.int32, (hidden, hidden), 1)
    identity = (row == column).astype(jnp.float32).astype(jnp.bfloat16)
    return lax.dot_general(
        identity,
        jnp.concatenate(pieces, axis=0),
        (((1,), (1,)), ((), ())),
        preferred_element_type=jnp.float32,
    )


def product_kernel(picks, rights, first, *refs):
    right_refs, refs = refs[:rights], refs[rights:]
    left_ref, gate_ref, gain_ref, bias_ref, weights_ref, *_, out_ref = refs[:-5]
    right, product, updates, result, sent = refs[-5:]
    hidden, rows, width = left_ref.shape
    count = right_refs[0].shape[0]
    apart = pitch(count)
    even = (lax.axis_index("row") + lax.axis_index("col")) % 2 == 0

    for token in range(count):
        pieces = []
        for at_even, at_odd in picks:
            piece = right_refs[at_even][token]
            if at_odd != at_even:
                piece = jnp.where(even, piece, right_refs[at_odd][token])
            pieces.append(piece)
        one = turned(pieces, width)
        for at in range(0, width, LANES):
            right[at // LANES, pl.ds(token, hidden, stride=apart), :] = one[:, at : at + LANES]

    total = jnp.zeros((count, rows), jnp.float32)
    for channel in range(hidden):
        one = 0.0
        for at in range(0, width, LANES):
            one += lax.dot_general(
                right[at // LANES, pl.ds(channel * apart, count), :].astype(jnp.bfloat16),
                left_ref[channel, :, at : at + LANES],
                (((1,), (1,)), ((), ())),
                preferred_element_type=jnp.float32,
            )
        product[pl.ds(channel * apart, count), :rows] = one
        total += one
    average = total / hidden
    total = jnp.zeros((count, rows), jnp.float32)
    for channel in range(hidden):
        centered = product[pl.ds(channel * apart, count), :rows] - average
        total += centered * centered
    scale = lax.rsqrt(total / hidden + 1e-05)
    for channel in range(hidden):
        place = pl.ds(channel * apart, count)
        centered = product[place, :rows] - average
        product[place, :rows] = centered * scale * gain_ref[channel] + bias_ref[channel]
    for token in range(count):
        mixed = product[pl.ds(token, hidden, stride=apart), :][:, :rows].astype(jnp.bfloat16)
        updates[pl.ds(token, rows, stride=apart), :] = lax.dot_general(
            mixed, weights_ref[...], (((0,), (0,)), ((), ())), preferred_element_type=jnp.float32
        )
    step = 8
    for at in range(0, rows, step):
        gate = gate_ref[pl.ds(at, step), pl.ds(first, count)]
        for row in range(step):
            update = updates[pl.ds((at + row) * apart, count), :]
            result[at + row] = (gate[row] * update).astype(jnp.bfloat16)
    copy = pltpu.make_async_copy(result, out_ref.at[:, pl.ds(first, count)], sent)
    copy.start()
    copy.wait()


def band_by_sums(right, spans, window, row_count, col_count, columns):
    blocks_per_row = col_count // row_count
    col_pos = lax.axis_index("col")
    pieces = []
    for offset in range(window):
        block_id = (col_pos - offset) % col_count
        start = block_id % blocks_per_row * columns
        received = from_root(
            lax.dynamic_slice_in_dim(right, start, columns, 0), "row", block_id // blocks_per_row
        )
        pieces.append(received if offset == 0 else shifted(received, "col", -offset))
    bands = [[piece[first : first + count] for piece in pieces] for first, count in spans]
    return bands, [(offset, offset) for offset in range(window)]


def hops():
    out, near, cross = [], [], []
    for r in range(4):
        for c in range(4):
            before = (c - 1) % 4
            if (c - r) % 4 < 2:
                out.append(((r, c), (r ^ 2, c)))
            if (r + c) % 2 == 0:
                near.append(((r, c), (r ^ 1, c)))
            else:
                near.append(((r, c), (r, before)))
                cross.append(((r, c), (r ^ 1, before)))
    return out, near, cross


def move(array, pairs):
    return lax.ppermute(
        array, ("row", "col"), [(r * 4 + c, to_r * 4 + to_c) for (r, c), (to_r, to_c) in pairs]
    )


def on_device(
    pair_state,
    token_count,
    in_gain,
    in_bias,
    in_weights,
    gate_weights,
    out_gain,
    out_bias,
    out_weights,
):
    rows, columns, channels = pair_state.shape
    hidden = out_weights.shape[0]
    tokens = rows * columns
    col_count = lax.axis_size("col")
    row_count = lax.axis_size("row")
    window = col_count // 2
    depth = window * columns
    width = -(-depth // LANES) * LANES
    in_gain, in_bias = in_gain.reshape(1, channels), in_bias.reshape(1, channels)
    block = 2 * tokens * max(channels, hidden)
    by_hops = row_count == 4 and col_count == 4
    last = 16
    spans = [(0, columns - last), (columns - last, last)]

    arrived = []
    if by_hops:
        out, near, cross = hops()
        arrived.append(move(pair_state[: spans[0][1]], out))
    pairs = [pair_state]
    for _ in range(window - 1):
        pairs.append(shifted(pairs[-1], "col", -1))
    passed = [in_gain, in_bias, in_weights[:, 2 * hidden :], out_weights]
    later = spans[1][0]
    left, gate, later_pair, *handed = pl.pallas_call(
        functools.partial(left_kernel, window, later),
        out_shape=[
            jax.ShapeDtypeStruct((hidden, rows, width), jnp.bfloat16),
            jax.ShapeDtypeStruct((rows, columns, channels), jnp.float32),
            jax.ShapeDtypeStruct((rows - later, columns, channels), jnp.bfloat16),
        ]
        + [jax.ShapeDtypeStruct(array.shape, array.dtype) for array in passed],
        in_specs=[SMEM] + [VMEM] * (window + 8),
        out_specs=[VMEM] * 7,
        scratch_shapes=[pltpu.VMEM((width // LANES, hidden * pitch(rows), LANES), jnp.float32)],
        compiler_params=params((window + 2) * block, 6 * hidden * rows * width),
        cost_estimate=cost(
            4 * window * tokens * channels * hidden, 6 * rows * width * hidden
        ),
        name="left_and_gate",
    )(token_count, *pairs, in_gain, in_bias, in_weights[:, : 2 * hidden].T, gate_weights, *passed)
    in_gain, in_bias, right_weights, out_weights = handed

    def right_of(first, count, *far):
        return pl.pallas_call(
            functools.partial(right_kernel, by_hops, first),
            out_shape=jax.ShapeDtypeStruct((count, columns, hidden), jnp.bfloat16),
            in_specs=[SMEM] + [VMEM] * (4 + len(far)),
            out_specs=VMEM,
            compiler_params=params(2 * block),
            cost_estimate=cost(4 * count * columns * channels * hidden, 6 * count * columns * channels),
            name="right",
        )(token_count, pair_state, in_gain, in_bias, right_weights, *far)

    if by_hops:
        arrived.append(move(later_pair, out))
        bands = []
        for (first, count), far in zip(spans, arrived):
            held = right_of(first, count, far)
            bands.append([held, move(held, near), move(held, cross)])
        picks = [(0, 1), (1, 2)]
    else:
        bands, picks = band_by_sums(
            right_of(0, rows), spans, window, row_count, col_count, columns
        )

    update = []
    for (first, count), band in zip(spans, bands):
        filled = pl.pallas_call(
            functools.partial(product_kernel, picks, len(band), first),
            out_shape=jax.ShapeDtypeStruct((rows, columns, channels), jnp.bfloat16),
            in_specs=[VMEM] * (len(band) + 2) + [SMEM, SMEM, VMEM] + [ANY] * len(update),
            out_specs=ANY,
            scratch_shapes=[
                pltpu.VMEM((width // LANES, hidden * pitch(count), LANES), jnp.float32),
                pltpu.VMEM((hidden * pitch(count), LANES), jnp.float32),
                pltpu.VMEM((rows * pitch(count), channels), jnp.float32),
                pltpu.VMEM((rows, count, channels), jnp.bfloat16),
                pltpu.SemaphoreType.DMA,
            ],
            input_output_aliases={len(band) + 5: 0} if update else {},
            compiler_params=params(2 * block, 2 * hidden * (rows + 2 * count) * width),
            cost_estimate=cost(
                2 * rows * count * depth * hidden, 4 * rows * depth * hidden
            ),
            name="product",
        )(*band, left, gate, out_gain, out_bias, out_weights, *update)
        update = [filled]
    return filled


def solution(mesh):
    placed = (P(("crops", "row"), "col", None), P("crops"), P(), P(), P(), P(), P(), P(), P())
    return jax.shard_map(
        on_device,
        mesh=mesh,
        in_specs=placed,
        out_specs=P(("crops", "row"), "col", None),
        check_vma=False,
    )
```

```python
import functools

import jax
import jax.numpy as jnp
from jax import lax
from jax.experimental import pallas as pl
from jax.experimental.pallas import tpu as pltpu
from jax.sharding import PartitionSpec as P

LANES = 128
MIB = 1024 * 1024


def params(*sizes):
    return pltpu.CompilerParams(vmem_limit_bytes=min(6 * MIB + 2 * sum(sizes), 56 * MIB))


def cost(flops, bytes_accessed):
    return pl.CostEstimate(flops=flops, bytes_accessed=bytes_accessed, transcendentals=0)


VMEM = pl.BlockSpec(memory_space=pltpu.VMEM)
SMEM = pl.BlockSpec(memory_space=pltpu.SMEM)
ANY = pl.BlockSpec(memory_space=pl.ANY)


def pitch(rows):
    return (rows // 8 | 1) * 8


def shifted(array, axis, by):
    devices = lax.axis_size(axis)
    return lax.ppermute(array, axis, [(i, (i + by) % devices) for i in range(devices)])


def from_root(array, axis, root):
    mine = lax.axis_index(axis) == root
    return lax.psum(jnp.where(mine, array, jnp.zeros_like(array)), axis)


def layer_norm(values, gain, offset):
    average = jnp.mean(values, axis=-1, keepdims=True)
    centered = values - average
    variance = jnp.mean(centered * centered, axis=-1, keepdims=True)
    return centered * lax.rsqrt(variance + 1e-05) * gain + offset


def normed_rows(block, gain_ref, bias_ref):
    rows, columns, channels = block.shape
    values = block.reshape(rows * columns, channels).astype(jnp.float32)
    return layer_norm(values, gain_ref[...], bias_ref[...]).astype(jnp.bfloat16)


def right_kernel(hops, first, tokens_ref, pair_ref, gain_ref, bias_ref, weights_ref, *refs):
    out_ref = refs[-1]
    count, columns, hidden = out_ref.shape
    row_pos, col_pos = lax.axis_index("row"), lax.axis_index("col")
    tokens = tokens_ref[0]
    block_row = row_pos
    if hops:
        is_root = (col_pos - row_pos + 4) % 4 < 2
        block_row = jnp.where((row_pos + col_pos) % 2 == 0, col_pos, (col_pos + 3) % 4)
    row_start = block_row * pair_ref.shape[0] + first
    valid_columns = tokens - col_pos * columns
    position = lax.broadcasted_iota(jnp.int32, (columns, hidden), 0)
    step = 4
    for at in range(0, count, step):
        block = pair_ref[pl.ds(first + at, step)]
        if hops:
            block = jnp.where(is_root, block, refs[0][pl.ds(first + at, step)])
        normed = normed_rows(block, gain_ref, bias_ref)
        both = jnp.dot(
            normed, weights_ref[...], preferred_element_type=jnp.float32
        )
        right = jax.nn.sigmoid(both[:, :hidden]) * both[:, hidden:]
        for row in range(step):
            limit = jnp.where(row_start + at + row < tokens, valid_columns, 0)
            part = right[row * columns : (row + 1) * columns]
            out_ref[at + row] = jnp.where(position < limit, part, 0.0).astype(jnp.bfloat16)


def gate_kernel(passes, pair_ref, weights_ref, *refs):
    passed, gate_ref, handed = refs[:passes], refs[passes], refs[passes + 1 :]
    for source, target in zip(passed, handed):
        target[...] = source[...]
    rows, columns, channels = pair_ref.shape
    step = 4
    for first in range(0, rows, step):
        normed = normed_rows(pair_ref[pl.ds(first, step)], passed[0], passed[1])
        gate = jnp.dot(normed, weights_ref[...], preferred_element_type=jnp.float32)
        gate_ref[pl.ds(first, step)] = jax.nn.sigmoid(gate).reshape(step, columns, channels)


def left_kernel(blocks, tokens_ref, *refs):
    pair_refs, (gain_ref, bias_ref, weights_ref, left_ref, scratch) = refs[:blocks], refs[blocks:]
    rows, columns, channels = pair_refs[0].shape
    hidden, _, width = left_ref.shape
    tokens = tokens_ref[0]
    row_start = lax.axis_index("row") * rows
    col_pos, col_count = lax.axis_index("col"), lax.axis_size("col")
    lane = lax.broadcasted_iota(jnp.int32, (1, width), 1)
    keep = jnp.zeros((1, width), jnp.float32)
    for at in range(blocks):
        end = at * columns + jnp.minimum(tokens - (col_pos + at) % col_count * columns, columns)
        keep += jnp.where((lane >= at * columns) & (lane < end), 1.0, 0.0)
    padding = [jnp.zeros((width - blocks * columns, channels), jnp.bfloat16)]
    if width == blocks * columns:
        padding = []
    step = 4
    for first in range(0, rows, step):
        normed = [normed_rows(ref[pl.ds(first, step)], gain_ref, bias_ref) for ref in pair_refs]
        for row in range(step):
            thirds = [piece[row * columns : (row + 1) * columns] for piece in normed]
            both = lax.dot_general(
                weights_ref[...],
                jnp.concatenate(thirds + padding, axis=0),
                (((1,), (1,)), ((), ())),
                preferred_element_type=jnp.float32,
            )
            left = jax.nn.sigmoid(both[:hidden]) * both[hidden:]
            valid = jnp.where(row_start + first + row < tokens, keep, 0.0)
            left = jnp.where(valid > 0.0, left, 0.0)
            for at in range(0, width, LANES):
                scratch[at // LANES, pl.ds(first + row, hidden, stride=pitch(rows)), :] = left[
                    :, at : at + LANES
                ]
    for channel in range(hidden):
        for at in range(0, width, LANES):
            one = scratch[at // LANES, pl.ds(channel * pitch(rows), rows), :]
            left_ref[channel, :, at : at + LANES] = one.astype(jnp.bfloat16)


def turned(pieces, width):
    rows = sum(piece.shape[0] for piece in pieces)
    hidden = pieces[0].shape[1]
    if width > rows:
        pieces = pieces + [jnp.zeros((width - rows, hidden), pieces[0].dtype)]
    row = lax.broadcasted_iota(jnp.int32, (hidden, hidden), 0)
    column = lax.broadcasted_iota(jnp.int32, (hidden, hidden), 1)
    identity = (row == column).astype(jnp.float32).astype(jnp.bfloat16)
    return lax.dot_general(
        identity,
        jnp.concatenate(pieces, axis=0),
        (((1,), (1,)), ((), ())),
        preferred_element_type=jnp.float32,
    )


def product_kernel(picks, rights, first, last, *refs):
    right_refs, refs = refs[:rights], refs[rights:]
    left_ref, gate_ref, gain_ref, bias_ref, weights_ref, *done, out_ref = refs[: -5 if last else -3]
    right, product, updates = refs[-5:-2] if last else refs[-3:]
    result, sent = refs[-2:] if last else (out_ref, None)
    hidden, rows, width = left_ref.shape
    count = right_refs[0].shape[0]
    apart = pitch(count)
    even = (lax.axis_index("row") + lax.axis_index("col")) % 2 == 0

    copies, start = [], 0
    for at, ref in enumerate(done):
        columns = pl.ds(start, ref.shape[1])
        copies.append(pltpu.make_async_copy(ref, out_ref.at[:, columns], sent.at[at]))
        copies[-1].start()
        start += ref.shape[1]

    for token in range(count):
        pieces = []
        for at_even, at_odd in picks:
            piece = right_refs[at_even][token]
            if at_odd != at_even:
                piece = jnp.where(even, piece, right_refs[at_odd][token])
            pieces.append(piece)
        one = turned(pieces, width)
        for at in range(0, width, LANES):
            right[at // LANES, pl.ds(token, hidden, stride=apart), :] = one[:, at : at + LANES]

    ways = 4
    totals = [jnp.zeros((count, rows), jnp.float32)] * ways
    for channel in range(hidden):
        one = 0.0
        for at in range(0, width, LANES):
            one += lax.dot_general(
                right[at // LANES, pl.ds(channel * apart, count), :].astype(jnp.bfloat16),
                left_ref[channel, :, at : at + LANES],
                (((1,), (1,)), ((), ())),
                preferred_element_type=jnp.float32,
            )
        product[pl.ds(channel * apart, count), :rows] = one
        totals[channel % ways] += one
    average = sum(totals) / hidden
    totals = [jnp.zeros((count, rows), jnp.float32)] * ways
    for channel in range(hidden):
        centered = product[pl.ds(channel * apart, count), :rows] - average
        totals[channel % ways] += centered * centered
    scale = lax.rsqrt(sum(totals) / hidden + 1e-05)
    for channel in range(hidden):
        place = pl.ds(channel * apart, count)
        centered = product[place, :rows] - average
        product[place, :rows] = centered * scale * gain_ref[channel] + bias_ref[channel]
    for token in range(count):
        mixed = product[pl.ds(token, hidden, stride=apart), :][:, :rows].astype(jnp.bfloat16)
        updates[pl.ds(token, rows, stride=apart), :] = lax.dot_general(
            mixed, weights_ref[...], (((0,), (0,)), ((), ())), preferred_element_type=jnp.float32
        )
    step = 16
    for at in range(0, rows, step):
        gate = gate_ref[pl.ds(at, step), pl.ds(first, count)]
        for row in range(step):
            update = updates[pl.ds((at + row) * apart, count), :]
            result[at + row] = (gate[row] * update).astype(jnp.bfloat16)
        if last:
            target = out_ref.at[pl.ds(at, step), pl.ds(first, count)]
            place = sent.at[len(done) + at // step]
            copies.append(pltpu.make_async_copy(result.at[pl.ds(at, step)], target, place))
            copies[-1].start()
    for copy in copies:
        copy.wait()


def band_by_sums(right, spans, window, row_count, col_count, columns):
    blocks_per_row = col_count // row_count
    col_pos = lax.axis_index("col")
    pieces = []
    for offset in range(window):
        block_id = (col_pos - offset) % col_count
        start = block_id % blocks_per_row * columns
        received = from_root(
            lax.dynamic_slice_in_dim(right, start, columns, 0), "row", block_id // blocks_per_row
        )
        pieces.append(received if offset == 0 else shifted(received, "col", -offset))
    bands = [[piece[first : first + count] for piece in pieces] for first, count in spans]
    return bands, [(offset, offset) for offset in range(window)]


def hops():
    out, near, cross = [], [], []
    for r in range(4):
        for c in range(4):
            before = (c - 1) % 4
            if (c - r) % 4 < 2:
                out.append(((r, c), (r ^ 2, c)))
            if (r + c) % 2 == 0:
                near.append(((r, c), (r ^ 1, c)))
            else:
                near.append(((r, c), (r, before)))
                cross.append(((r, c), (r ^ 1, before)))
    return out, near, cross


def move(array, pairs):
    return lax.ppermute(
        array, ("row", "col"), [(r * 4 + c, to_r * 4 + to_c) for (r, c), (to_r, to_c) in pairs]
    )


def on_device(
    pair_state,
    token_count,
    in_gain,
    in_bias,
    in_weights,
    gate_weights,
    out_gain,
    out_bias,
    out_weights,
):
    rows, columns, channels = pair_state.shape
    hidden = out_weights.shape[0]
    tokens = rows * columns
    col_count = lax.axis_size("col")
    row_count = lax.axis_size("row")
    window = col_count // 2
    depth = window * columns
    width = -(-depth // LANES) * LANES
    in_gain, in_bias = in_gain.reshape(1, channels), in_bias.reshape(1, channels)
    block = 2 * tokens * max(channels, hidden)
    by_hops = row_count == 4 and col_count == 4
    few = 16
    spans = [(0, few), (few, columns - few)]

    if by_hops:
        out, near, cross = hops()
        arrived = move(pair_state, out)
    left_weights, right_weights = in_weights[:, : 2 * hidden].T, in_weights[:, 2 * hidden :]
    passed = [in_gain, in_bias, left_weights, right_weights, out_weights, pair_state]
    gate, *handed = pl.pallas_call(
        functools.partial(gate_kernel, len(passed)),
        out_shape=[jax.ShapeDtypeStruct((rows, columns, channels), jnp.float32)]
        + [jax.ShapeDtypeStruct(array.shape, array.dtype) for array in passed],
        in_specs=[VMEM] * (2 + len(passed)),
        out_specs=[VMEM] * (1 + len(passed)),
        compiler_params=params(5 * block),
        cost_estimate=cost(2 * tokens * channels * channels, 6 * tokens * channels),
        name="gate",
    )(pair_state, gate_weights, *passed)
    in_gain, in_bias, left_weights, right_weights, out_weights, own = handed

    def right_of(first, count, *far):
        return pl.pallas_call(
            functools.partial(right_kernel, by_hops, first),
            out_shape=jax.ShapeDtypeStruct((count, columns, hidden), jnp.bfloat16),
            in_specs=[SMEM] + [VMEM] * (4 + len(far)),
            out_specs=VMEM,
            compiler_params=params(2 * block),
            cost_estimate=cost(4 * count * columns * channels * hidden, 6 * count * columns * channels),
            name="right",
        )(token_count, own, in_gain, in_bias, right_weights, *far)

    pairs = [pair_state]
    for _ in range(window - 1):
        pairs.append(shifted(pairs[-1], "col", -1))
    pairs[0] = own
    if by_hops:
        out, near, cross = hops()
        arrived = move(pair_state, out)
        held = [right_of(first, count, arrived) for first, count in spans]
        *held, pairs[-1] = lax.optimization_barrier((*held, pairs[-1]))
        bands = [[piece, move(piece, near), move(piece, cross)] for piece in held]
        picks = [(0, 1), (1, 2)]
    else:
        bands, picks = band_by_sums(
            right_of(0, rows), spans, window, row_count, col_count, columns
        )
    left = pl.pallas_call(
        functools.partial(left_kernel, window),
        out_shape=jax.ShapeDtypeStruct((hidden, rows, width), jnp.bfloat16),
        in_specs=[SMEM] + [VMEM] * (window + 3),
        out_specs=VMEM,
        scratch_shapes=[pltpu.VMEM((width // LANES, hidden * pitch(rows), LANES), jnp.float32)],
        compiler_params=params((window + 2) * block, 6 * hidden * rows * width),
        cost_estimate=cost(4 * window * tokens * channels * hidden, 6 * rows * width * hidden),
        name="left",
    )(token_count, *pairs, in_gain, in_bias, left_weights)

    done = []
    for (first, count), band in zip(spans, bands):
        last = first + count == columns
        scratch = [
            pltpu.VMEM((width // LANES, hidden * pitch(count), LANES), jnp.float32),
            pltpu.VMEM((hidden * pitch(count), LANES), jnp.float32),
            pltpu.VMEM((rows * pitch(count), channels), jnp.float32),
        ]
        if last:
            scratch += [
                pltpu.VMEM((rows, count, channels), jnp.bfloat16),
                pltpu.SemaphoreType.DMA((len(done) + rows // 16,)),
            ]
        filled = pl.pallas_call(
            functools.partial(product_kernel, picks, len(band), first, last),
            out_shape=jax.ShapeDtypeStruct(
                (rows, columns if last else count, channels), jnp.bfloat16
            ),
            in_specs=[VMEM] * (len(band) + 2) + [SMEM, SMEM, VMEM] + [VMEM] * len(done) * last,
            out_specs=ANY if last else VMEM,
            scratch_shapes=scratch,
            compiler_params=params(2 * block, 2 * hidden * (rows + 2 * count) * width),
            cost_estimate=cost(2 * rows * count * depth * hidden, 4 * rows * depth * hidden),
            name="product",
        )(*band, left, gate, out_gain, out_bias, out_weights, *(done if last else []))
        done.append(filled)
    return filled


def solution(mesh):
    placed = (P(("crops", "row"), "col", None), P("crops"), P(), P(), P(), P(), P(), P(), P())
    return jax.shard_map(
        on_device,
        mesh=mesh,
        in_specs=placed,
        out_specs=P(("crops", "row"), "col", None),
        check_vma=False,
    )
```

```python
import functools

import jax
import jax.numpy as jnp
from jax import lax
from jax.experimental import pallas as pl
from jax.experimental.pallas import tpu as pltpu
from jax.sharding import PartitionSpec as P

LANES = 128
MIB = 1024 * 1024


def params(*sizes):
    return pltpu.CompilerParams(vmem_limit_bytes=min(6 * MIB + 2 * sum(sizes), 56 * MIB))


def cost(flops, bytes_accessed):
    return pl.CostEstimate(flops=flops, bytes_accessed=bytes_accessed, transcendentals=0)


VMEM = pl.BlockSpec(memory_space=pltpu.VMEM)
SMEM = pl.BlockSpec(memory_space=pltpu.SMEM)
ANY = pl.BlockSpec(memory_space=pl.ANY)


def pitch(rows):
    return (rows // 8 | 1) * 8


def shifted(array, axis, by):
    devices = lax.axis_size(axis)
    return lax.ppermute(array, axis, [(i, (i + by) % devices) for i in range(devices)])


def from_root(array, axis, root):
    mine = lax.axis_index(axis) == root
    return lax.psum(jnp.where(mine, array, jnp.zeros_like(array)), axis)


def layer_norm(values, gain, offset):
    average = jnp.mean(values, axis=-1, keepdims=True)
    centered = values - average
    variance = jnp.mean(centered * centered, axis=-1, keepdims=True)
    return centered * lax.rsqrt(variance + 1e-05) * gain + offset


def normed_rows(block, gain_ref, bias_ref):
    rows, columns, channels = block.shape
    values = block.reshape(rows * columns, channels).astype(jnp.float32)
    return layer_norm(values, gain_ref[...], bias_ref[...]).astype(jnp.bfloat16)


def right_kernel(hops, first, tokens_ref, pair_ref, gain_ref, bias_ref, weights_ref, *refs):
    out_ref = refs[-1]
    count, columns, hidden = out_ref.shape
    row_pos, col_pos = lax.axis_index("row"), lax.axis_index("col")
    tokens = tokens_ref[0]
    block_row = row_pos
    if hops:
        is_root = (col_pos - row_pos + 4) % 4 < 2
        block_row = jnp.where((row_pos + col_pos) % 2 == 0, col_pos, (col_pos + 3) % 4)
    row_start = block_row * pair_ref.shape[0] + first
    valid_columns = tokens - col_pos * columns
    position = lax.broadcasted_iota(jnp.int32, (columns, hidden), 0)
    step = 4
    for at in range(0, count, step):
        block = pair_ref[pl.ds(first + at, step)]
        if hops:
            block = jnp.where(is_root, block, refs[0][pl.ds(at, step)])
        normed = normed_rows(block, gain_ref, bias_ref)
        both = jnp.dot(
            normed, weights_ref[...], preferred_element_type=jnp.float32
        )
        right = jax.nn.sigmoid(both[:, :hidden]) * both[:, hidden:]
        for row in range(step):
            limit = jnp.where(row_start + at + row < tokens, valid_columns, 0)
            part = right[row * columns : (row + 1) * columns]
            out_ref[at + row] = jnp.where(position < limit, part, 0.0).astype(jnp.bfloat16)


def left_kernel(blocks, later, tokens_ref, *refs):
    pair_refs, refs = refs[:blocks], refs[blocks:]
    gain_ref, bias_ref, weights_ref, gate_weights_ref, *passed, scratch = refs
    passed, (left_ref, gate_ref, later_ref), handed = passed[:4], passed[4:7], passed[7:]
    later_ref[...] = pair_refs[0][pl.ds(later, later_ref.shape[0])]
    for source, target in zip(passed, handed):
        target[...] = source[...]
    rows, columns, channels = pair_refs[0].shape
    hidden, _, width = left_ref.shape
    tokens = tokens_ref[0]
    row_start = lax.axis_index("row") * rows
    col_pos, col_count = lax.axis_index("col"), lax.axis_size("col")
    lane = lax.broadcasted_iota(jnp.int32, (1, width), 1)
    keep = jnp.zeros((1, width), jnp.float32)
    for at in range(blocks):
        end = at * columns + jnp.minimum(tokens - (col_pos + at) % col_count * columns, columns)
        keep += jnp.where((lane >= at * columns) & (lane < end), 1.0, 0.0)
    padding = [jnp.zeros((width - blocks * columns, channels), jnp.bfloat16)]
    if width == blocks * columns:
        padding = []
    step = 4
    for first in range(0, rows, step):
        normed = [normed_rows(ref[pl.ds(first, step)], gain_ref, bias_ref) for ref in pair_refs]
        gate = jnp.dot(normed[0], gate_weights_ref[...], preferred_element_type=jnp.float32)
        gate_ref[pl.ds(first, step)] = jax.nn.sigmoid(gate).reshape(step, columns, channels)
        for row in range(step):
            thirds = [piece[row * columns : (row + 1) * columns] for piece in normed]
            both = lax.dot_general(
                weights_ref[...],
                jnp.concatenate(thirds + padding, axis=0),
                (((1,), (1,)), ((), ())),
                preferred_element_type=jnp.float32,
            )
            left = jax.nn.sigmoid(both[:hidden]) * both[hidden:]
            valid = jnp.where(row_start + first + row < tokens, keep, 0.0)
            left = jnp.where(valid > 0.0, left, 0.0)
            for at in range(0, width, LANES):
                scratch[at // LANES, pl.ds(first + row, hidden, stride=pitch(rows)), :] = left[
                    :, at : at + LANES
                ]
    for channel in range(hidden):
        for at in range(0, width, LANES):
            one = scratch[at // LANES, pl.ds(channel * pitch(rows), rows), :]
            left_ref[channel, :, at : at + LANES] = one.astype(jnp.bfloat16)


def turned(pieces, width):
    rows = sum(piece.shape[0] for piece in pieces)
    hidden = pieces[0].shape[1]
    if width > rows:
        pieces = pieces + [jnp.zeros((width - rows, hidden), pieces[0].dtype)]
    row = lax.broadcasted_iota(jnp.int32, (hidden, hidden), 0)
    column = lax.broadcasted_iota(jnp.int32, (hidden, hidden), 1)
    identity = (row == column).astype(jnp.float32).astype(jnp.bfloat16)
    return lax.dot_general(
        identity,
        jnp.concatenate(pieces, axis=0),
        (((1,), (1,)), ((), ())),
        preferred_element_type=jnp.float32,
    )


def product_kernel(picks, rights, first, last, *refs):
    right_refs, refs = refs[:rights], refs[rights:]
    left_ref, gate_ref, gain_ref, bias_ref, weights_ref, *done, out_ref = refs[: -5 if last else -3]
    right, product, updates = refs[-5:-2] if last else refs[-3:]
    result, sent = refs[-2:] if last else (out_ref, None)
    hidden, rows, width = left_ref.shape
    count = right_refs[0].shape[0]
    apart = pitch(count)
    even = (lax.axis_index("row") + lax.axis_index("col")) % 2 == 0

    copies, start = [], 0
    for at, ref in enumerate(done):
        columns = pl.ds(start, ref.shape[1])
        copies.append(pltpu.make_async_copy(ref, out_ref.at[:, columns], sent.at[at]))
        copies[-1].start()
        start += ref.shape[1]

    for token in range(count):
        pieces = []
        for at_even, at_odd in picks:
            piece = right_refs[at_even][token]
            if at_odd != at_even:
                piece = jnp.where(even, piece, right_refs[at_odd][token])
            pieces.append(piece)
        one = turned(pieces, width)
        for at in range(0, width, LANES):
            right[at // LANES, pl.ds(token, hidden, stride=apart), :] = one[:, at : at + LANES]

    ways = 4
    totals = [jnp.zeros((count, rows), jnp.float32)] * ways
    for channel in range(hidden):
        one = 0.0
        for at in range(0, width, LANES):
            one += lax.dot_general(
                right[at // LANES, pl.ds(channel * apart, count), :].astype(jnp.bfloat16),
                left_ref[channel, :, at : at + LANES],
                (((1,), (1,)), ((), ())),
                preferred_element_type=jnp.float32,
            )
        product[pl.ds(channel * apart, count), :rows] = one
        totals[channel % ways] += one
    average = sum(totals) / hidden
    totals = [jnp.zeros((count, rows), jnp.float32)] * ways
    for channel in range(hidden):
        centered = product[pl.ds(channel * apart, count), :rows] - average
        totals[channel % ways] += centered * centered
    scale = lax.rsqrt(sum(totals) / hidden + 1e-05)
    for channel in range(hidden):
        place = pl.ds(channel * apart, count)
        centered = product[place, :rows] - average
        product[place, :rows] = centered * scale * gain_ref[channel] + bias_ref[channel]
    for token in range(count):
        mixed = product[pl.ds(token, hidden, stride=apart), :][:, :rows].astype(jnp.bfloat16)
        updates[pl.ds(token, rows, stride=apart), :] = lax.dot_general(
            mixed, weights_ref[...], (((0,), (0,)), ((), ())), preferred_element_type=jnp.float32
        )
    step = 16
    for at in range(0, rows, step):
        gate = gate_ref[pl.ds(at, step), pl.ds(first, count)]
        for row in range(step):
            update = updates[pl.ds((at + row) * apart, count), :]
            result[at + row] = (gate[row] * update).astype(jnp.bfloat16)
        if last:
            target = out_ref.at[pl.ds(at, step), pl.ds(first, count)]
            place = sent.at[len(done) + at // step]
            copies.append(pltpu.make_async_copy(result.at[pl.ds(at, step)], target, place))
            copies[-1].start()
    for copy in copies:
        copy.wait()


def band_by_sums(right, spans, window, row_count, col_count, columns):
    blocks_per_row = col_count // row_count
    col_pos = lax.axis_index("col")
    pieces = []
    for offset in range(window):
        block_id = (col_pos - offset) % col_count
        start = block_id % blocks_per_row * columns
        received = from_root(
            lax.dynamic_slice_in_dim(right, start, columns, 0), "row", block_id // blocks_per_row
        )
        pieces.append(received if offset == 0 else shifted(received, "col", -offset))
    bands = [[piece[first : first + count] for piece in pieces] for first, count in spans]
    return bands, [(offset, offset) for offset in range(window)]


def hops():
    out, near, cross = [], [], []
    for r in range(4):
        for c in range(4):
            before = (c - 1) % 4
            if (c - r) % 4 < 2:
                out.append(((r, c), (r ^ 2, c)))
            if (r + c) % 2 == 0:
                near.append(((r, c), (r ^ 1, c)))
            else:
                near.append(((r, c), (r, before)))
                cross.append(((r, c), (r ^ 1, before)))
    return out, near, cross


def move(array, pairs):
    return lax.ppermute(
        array, ("row", "col"), [(r * 4 + c, to_r * 4 + to_c) for (r, c), (to_r, to_c) in pairs]
    )


def on_device(
    pair_state,
    token_count,
    in_gain,
    in_bias,
    in_weights,
    gate_weights,
    out_gain,
    out_bias,
    out_weights,
):
    rows, columns, channels = pair_state.shape
    hidden = out_weights.shape[0]
    tokens = rows * columns
    col_count = lax.axis_size("col")
    row_count = lax.axis_size("row")
    window = col_count // 2
    depth = window * columns
    width = -(-depth // LANES) * LANES
    in_gain, in_bias = in_gain.reshape(1, channels), in_bias.reshape(1, channels)
    block = 2 * tokens * max(channels, hidden)
    by_hops = row_count == 4 and col_count == 4
    last = 16
    spans = [(0, columns - last), (columns - last, last)]

    arrived = []
    if by_hops:
        out, near, cross = hops()
        arrived.append(move(pair_state[: spans[0][1]], out))
    pairs = [pair_state]
    for _ in range(window - 1):
        pairs.append(shifted(pairs[-1], "col", -1))
    passed = [in_gain, in_bias, in_weights[:, 2 * hidden :], out_weights]
    later = spans[1][0]
    left, gate, later_pair, *handed = pl.pallas_call(
        functools.partial(left_kernel, window, later),
        out_shape=[
            jax.ShapeDtypeStruct((hidden, rows, width), jnp.bfloat16),
            jax.ShapeDtypeStruct((rows, columns, channels), jnp.float32),
            jax.ShapeDtypeStruct((rows - later, columns, channels), jnp.bfloat16),
        ]
        + [jax.ShapeDtypeStruct(array.shape, array.dtype) for array in passed],
        in_specs=[SMEM] + [VMEM] * (window + 8),
        out_specs=[VMEM] * 7,
        scratch_shapes=[pltpu.VMEM((width // LANES, hidden * pitch(rows), LANES), jnp.float32)],
        compiler_params=params((window + 2) * block, 6 * hidden * rows * width),
        cost_estimate=cost(
            4 * window * tokens * channels * hidden, 6 * rows * width * hidden
        ),
        name="left_and_gate",
    )(token_count, *pairs, in_gain, in_bias, in_weights[:, : 2 * hidden].T, gate_weights, *passed)
    in_gain, in_bias, right_weights, out_weights = handed

    def right_of(first, count, *far):
        return pl.pallas_call(
            functools.partial(right_kernel, by_hops, first),
            out_shape=jax.ShapeDtypeStruct((count, columns, hidden), jnp.bfloat16),
            in_specs=[SMEM] + [VMEM] * (4 + len(far)),
            out_specs=VMEM,
            compiler_params=params(2 * block),
            cost_estimate=cost(4 * count * columns * channels * hidden, 6 * count * columns * channels),
            name="right",
        )(token_count, pair_state, in_gain, in_bias, right_weights, *far)

    if by_hops:
        arrived.append(move(later_pair, out))
        bands = []
        for (first, count), far in zip(spans, arrived):
            held = right_of(first, count, far)
            bands.append([held, move(held, near), move(held, cross)])
        picks = [(0, 1), (1, 2)]
    else:
        bands, picks = band_by_sums(
            right_of(0, rows), spans, window, row_count, col_count, columns
        )

    done = []
    for (first, count), band in zip(spans, bands):
        last = first + count == columns
        scratch = [
            pltpu.VMEM((width // LANES, hidden * pitch(count), LANES), jnp.float32),
            pltpu.VMEM((hidden * pitch(count), LANES), jnp.float32),
            pltpu.VMEM((rows * pitch(count), channels), jnp.float32),
        ]
        if last:
            scratch += [
                pltpu.VMEM((rows, count, channels), jnp.bfloat16),
                pltpu.SemaphoreType.DMA((len(done) + rows // 16,)),
            ]
        filled = pl.pallas_call(
            functools.partial(product_kernel, picks, len(band), first, last),
            out_shape=jax.ShapeDtypeStruct(
                (rows, columns if last else count, channels), jnp.bfloat16
            ),
            in_specs=[VMEM] * (len(band) + 2) + [SMEM, SMEM, VMEM] + [VMEM] * len(done) * last,
            out_specs=ANY if last else VMEM,
            scratch_shapes=scratch,
            compiler_params=params(2 * block, 2 * hidden * (rows + 2 * count) * width),
            cost_estimate=cost(2 * rows * count * depth * hidden, 4 * rows * depth * hidden),
            name="product",
        )(*band, left, gate, out_gain, out_bias, out_weights, *(done if last else []))
        done.append(filled)
    return filled


def solution(mesh):
    placed = (P(("crops", "row"), "col", None), P("crops"), P(), P(), P(), P(), P(), P(), P())
    return jax.shard_map(
        on_device,
        mesh=mesh,
        in_specs=placed,
        out_specs=P(("crops", "row"), "col", None),
        check_vma=False,
    )
```

```python
import functools

import jax
import jax.numpy as jnp
from jax import lax
from jax.experimental import pallas as pl
from jax.experimental.pallas import tpu as pltpu
from jax.sharding import PartitionSpec as P

LANES = 128
MIB = 1024 * 1024


def params(*sizes):
    return pltpu.CompilerParams(vmem_limit_bytes=min(6 * MIB + 2 * sum(sizes), 56 * MIB))


def cost(flops, bytes_accessed):
    return pl.CostEstimate(flops=flops, bytes_accessed=bytes_accessed, transcendentals=0)


VMEM = pl.BlockSpec(memory_space=pltpu.VMEM)
SMEM = pl.BlockSpec(memory_space=pltpu.SMEM)
ANY = pl.BlockSpec(memory_space=pl.ANY)


def pitch(rows):
    return (rows // 8 | 1) * 8


def shifted(array, axis, by):
    devices = lax.axis_size(axis)
    return lax.ppermute(array, axis, [(i, (i + by) % devices) for i in range(devices)])


def from_root(array, axis, root):
    mine = lax.axis_index(axis) == root
    return lax.psum(jnp.where(mine, array, jnp.zeros_like(array)), axis)


def layer_norm(values, gain, offset):
    average = jnp.mean(values, axis=-1, keepdims=True)
    centered = values - average
    variance = jnp.mean(centered * centered, axis=-1, keepdims=True)
    return centered * lax.rsqrt(variance + 1e-05) * gain + offset


def normed_rows(block, gain_ref, bias_ref):
    rows, columns, channels = block.shape
    values = block.reshape(rows * columns, channels).astype(jnp.float32)
    return layer_norm(values, gain_ref[...], bias_ref[...]).astype(jnp.bfloat16)


def right_kernel(hops, first, tokens_ref, pair_ref, gain_ref, bias_ref, weights_ref, *refs):
    out_ref = refs[-1]
    count, columns, hidden = out_ref.shape
    row_pos, col_pos = lax.axis_index("row"), lax.axis_index("col")
    tokens = tokens_ref[0]
    block_row = row_pos
    if hops:
        is_root = (col_pos - row_pos + 4) % 4 < 2
        block_row = jnp.where((row_pos + col_pos) % 2 == 0, col_pos, (col_pos + 3) % 4)
    row_start = block_row * pair_ref.shape[0] + first
    step = 4
    for at in range(0, count, step):
        block = pair_ref[pl.ds(first + at, step)]
        if hops:
            block = jnp.where(is_root, block, refs[0][pl.ds(at, step)])
        normed = normed_rows(block, gain_ref, bias_ref)
        both = jnp.dot(
            normed, weights_ref[...], preferred_element_type=jnp.float32
        )
        for row, part in enumerate(masked_right(both, tokens, row_start + at, col_pos, columns)):
            out_ref[at + row] = part


def masked_right(both, tokens, row_token, third_block, columns):
    hidden = both.shape[1] // 2
    right = jax.nn.sigmoid(both[:, :hidden]) * both[:, hidden:]
    position = lax.broadcasted_iota(jnp.int32, (columns, hidden), 0)
    parts = []
    for row in range(both.shape[0] // columns):
        limit = jnp.where(row_token + row < tokens, tokens - third_block * columns, 0)
        part = right[row * columns : (row + 1) * columns]
        parts.append(jnp.where(position < limit, part, 0.0).astype(jnp.bfloat16))
    return parts


def left_kernel(blocks, later, tokens_ref, *refs):
    pair_refs, refs = refs[:blocks], refs[blocks:]
    gain_ref, bias_ref, weights_ref, gate_weights_ref, *passed, scratch = refs
    passed, (left_ref, gate_ref, right_ref, later_ref), handed = passed[:4], passed[4:8], passed[8:]
    later_ref[...] = pair_refs[0][pl.ds(later, later_ref.shape[0])]
    for source, target in zip(passed, handed):
        target[...] = source[...]
    rows, columns, channels = pair_refs[0].shape
    hidden, _, width = left_ref.shape
    tokens = tokens_ref[0]
    row_start = lax.axis_index("row") * rows
    col_pos, col_count = lax.axis_index("col"), lax.axis_size("col")
    lane = lax.broadcasted_iota(jnp.int32, (1, width), 1)
    keep = jnp.zeros((1, width), jnp.float32)
    for at in range(blocks):
        end = at * columns + jnp.minimum(tokens - (col_pos + at) % col_count * columns, columns)
        keep += jnp.where((lane >= at * columns) & (lane < end), 1.0, 0.0)
    padding = [jnp.zeros((width - blocks * columns, channels), jnp.bfloat16)]
    if width == blocks * columns:
        padding = []
    step = 4
    for first in range(0, rows, step):
        normed = [normed_rows(ref[pl.ds(first, step)], gain_ref, bias_ref) for ref in pair_refs]
        gate = jnp.dot(normed[0], gate_weights_ref[...], preferred_element_type=jnp.float32)
        gate_ref[pl.ds(first, step)] = jax.nn.sigmoid(gate).reshape(step, columns, channels)
        both = jnp.dot(normed[0], passed[2][...], preferred_element_type=jnp.float32)
        for row, part in enumerate(masked_right(both, tokens, row_start + first, col_pos, columns)):
            right_ref[first + row] = part
        for row in range(step):
            thirds = [piece[row * columns : (row + 1) * columns] for piece in normed]
            both = lax.dot_general(
                weights_ref[...],
                jnp.concatenate(thirds + padding, axis=0),
                (((1,), (1,)), ((), ())),
                preferred_element_type=jnp.float32,
            )
            left = jax.nn.sigmoid(both[:hidden]) * both[hidden:]
            valid = jnp.where(row_start + first + row < tokens, keep, 0.0)
            left = jnp.where(valid > 0.0, left, 0.0)
            for at in range(0, width, LANES):
                scratch[at // LANES, pl.ds(first + row, hidden, stride=pitch(rows)), :] = left[
                    :, at : at + LANES
                ]
    for channel in range(hidden):
        for at in range(0, width, LANES):
            one = scratch[at // LANES, pl.ds(channel * pitch(rows), rows), :]
            left_ref[channel, :, at : at + LANES] = one.astype(jnp.bfloat16)


def turned(pieces, width):
    rows = sum(piece.shape[0] for piece in pieces)
    hidden = pieces[0].shape[1]
    if width > rows:
        pieces = pieces + [jnp.zeros((width - rows, hidden), pieces[0].dtype)]
    row = lax.broadcasted_iota(jnp.int32, (hidden, hidden), 0)
    column = lax.broadcasted_iota(jnp.int32, (hidden, hidden), 1)
    identity = (row == column).astype(jnp.float32).astype(jnp.bfloat16)
    return lax.dot_general(
        identity,
        jnp.concatenate(pieces, axis=0),
        (((1,), (1,)), ((), ())),
        preferred_element_type=jnp.float32,
    )


def product_kernel(picks, place, rights, first, last, *refs):
    right_refs, refs = refs[:rights], refs[rights:]
    left_ref, gate_ref, gain_ref, bias_ref, weights_ref, *done, out_ref = refs[: -5 if last else -3]
    right, product, updates = refs[-5:-2] if last else refs[-3:]
    result, sent = refs[-2:] if last else (out_ref, None)
    hidden, rows, width = left_ref.shape
    count = right_refs[0].shape[0]
    apart = pitch(count)
    mine = place()

    def row_of(source, token):
        ref = right_refs[source]
        return ref[token if ref.shape[0] == count else first + token]

    copies, start = [], 0
    for at, ref in enumerate(done):
        columns = pl.ds(start, ref.shape[1])
        copies.append(pltpu.make_async_copy(ref, out_ref.at[:, columns], sent.at[at]))
        copies[-1].start()
        start += ref.shape[1]

    for token in range(count):
        pieces = []
        for sources in picks:
            piece = row_of(sources[0], token)
            for at, source in enumerate(sources[1:], 1):
                if source != sources[at - 1]:
                    piece = jnp.where(mine >= at, row_of(source, token), piece)
            pieces.append(piece)
        one = turned(pieces, width)
        for at in range(0, width, LANES):
            right[at // LANES, pl.ds(token, hidden, stride=apart), :] = one[:, at : at + LANES]

    ways = 4
    totals = [jnp.zeros((count, rows), jnp.float32)] * ways
    for channel in range(hidden):
        one = 0.0
        for at in range(0, width, LANES):
            one += lax.dot_general(
                right[at // LANES, pl.ds(channel * apart, count), :].astype(jnp.bfloat16),
                left_ref[channel, :, at : at + LANES],
                (((1,), (1,)), ((), ())),
                preferred_element_type=jnp.float32,
            )
        product[pl.ds(channel * apart, count), :rows] = one
        totals[channel % ways] += one
    average = sum(totals) / hidden
    totals = [jnp.zeros((count, rows), jnp.float32)] * ways
    for channel in range(hidden):
        centered = product[pl.ds(channel * apart, count), :rows] - average
        totals[channel % ways] += centered * centered
    scale = lax.rsqrt(sum(totals) / hidden + 1e-05)
    for channel in range(hidden):
        place = pl.ds(channel * apart, count)
        centered = product[place, :rows] - average
        product[place, :rows] = centered * scale * gain_ref[channel] + bias_ref[channel]
    for token in range(count):
        mixed = product[pl.ds(token, hidden, stride=apart), :][:, :rows].astype(jnp.bfloat16)
        updates[pl.ds(token, rows, stride=apart), :] = lax.dot_general(
            mixed, weights_ref[...], (((0,), (0,)), ((), ())), preferred_element_type=jnp.float32
        )
    step = 16
    for at in range(0, rows, step):
        gate = gate_ref[pl.ds(at, step), pl.ds(first, count)]
        for row in range(step):
            update = updates[pl.ds((at + row) * apart, count), :]
            result[at + row] = (gate[row] * update).astype(jnp.bfloat16)
        if last:
            target = out_ref.at[pl.ds(at, step), pl.ds(first, count)]
            place = sent.at[len(done) + at // step]
            copies.append(pltpu.make_async_copy(result.at[pl.ds(at, step)], target, place))
            copies[-1].start()
    for copy in copies:
        copy.wait()


def band_by_sums(right, spans, window, row_count, col_count, columns):
    blocks_per_row = col_count // row_count
    col_pos = lax.axis_index("col")
    pieces = []
    for offset in range(window):
        block_id = (col_pos - offset) % col_count
        start = block_id % blocks_per_row * columns
        received = from_root(
            lax.dynamic_slice_in_dim(right, start, columns, 0), "row", block_id // blocks_per_row
        )
        pieces.append(received if offset == 0 else shifted(received, "col", -offset))
    bands = [[piece[first : first + count] for piece in pieces] for first, count in spans]
    return bands, [(offset, offset) for offset in range(window)]


def hops():
    out, near, cross, early = [], [], [], []
    for r in range(4):
        for c in range(4):
            before = (c - 1) % 4
            if (c - r) % 4 < 2:
                out.append(((r, c), (r ^ 2, c)))
            if (r + c) % 2 == 0:
                near.append(((r, c), (r ^ 1, c)))
            else:
                near.append(((r, c), (r, before)))
                (early if (r, c) in ((0, 1), (1, 2)) else cross).append(((r, c), (r ^ 1, before)))
    return out, near, cross, early


def hop_place():
    row_pos, col_pos = lax.axis_index("row"), lax.axis_index("col")
    odd = (row_pos + col_pos) % 2
    return jnp.where((row_pos < 2) & (col_pos < 2), 2 * odd, odd)


def move(array, pairs):
    return lax.ppermute(
        array, ("row", "col"), [(r * 4 + c, to_r * 4 + to_c) for (r, c), (to_r, to_c) in pairs]
    )


def on_device(
    pair_state,
    token_count,
    in_gain,
    in_bias,
    in_weights,
    gate_weights,
    out_gain,
    out_bias,
    out_weights,
):
    rows, columns, channels = pair_state.shape
    hidden = out_weights.shape[0]
    tokens = rows * columns
    col_count = lax.axis_size("col")
    row_count = lax.axis_size("row")
    window = col_count // 2
    depth = window * columns
    width = -(-depth // LANES) * LANES
    in_gain, in_bias = in_gain.reshape(1, channels), in_bias.reshape(1, channels)
    block = 2 * tokens * max(channels, hidden)
    by_hops = row_count == 4 and col_count == 4
    last = 16
    spans = [(0, columns - last), (columns - last, last)]

    arrived = []
    if by_hops:
        out, near, cross, early = hops()
        arrived.append(move(pair_state[: spans[0][1]], out))
    pairs = [pair_state]
    for _ in range(window - 1):
        pairs.append(shifted(pairs[-1], "col", -1))
    passed = [in_gain, in_bias, in_weights[:, 2 * hidden :], out_weights]
    later = spans[1][0]
    left, gate, right, later_pair, *handed = pl.pallas_call(
        functools.partial(left_kernel, window, later),
        out_shape=[
            jax.ShapeDtypeStruct((hidden, rows, width), jnp.bfloat16),
            jax.ShapeDtypeStruct((rows, columns, channels), jnp.float32),
            jax.ShapeDtypeStruct((rows, columns, hidden), jnp.bfloat16),
            jax.ShapeDtypeStruct((rows - later, columns, channels), jnp.bfloat16),
        ]
        + [jax.ShapeDtypeStruct(array.shape, array.dtype) for array in passed],
        in_specs=[SMEM] + [VMEM] * (window + 8),
        out_specs=[VMEM] * 8,
        scratch_shapes=[pltpu.VMEM((width // LANES, hidden * pitch(rows), LANES), jnp.float32)],
        compiler_params=params((window + 4) * block, 6 * hidden * rows * width),
        cost_estimate=cost(
            4 * window * tokens * channels * hidden, 6 * rows * width * hidden
        ),
        name="left_and_gate",
    )(token_count, *pairs, in_gain, in_bias, in_weights[:, : 2 * hidden].T, gate_weights, *passed)
    in_gain, in_bias, right_weights, out_weights = handed

    def right_of(first, count, *far):
        return pl.pallas_call(
            functools.partial(right_kernel, by_hops, first),
            out_shape=jax.ShapeDtypeStruct((count, columns, hidden), jnp.bfloat16),
            in_specs=[SMEM] + [VMEM] * (4 + len(far)),
            out_specs=VMEM,
            compiler_params=params(2 * block),
            cost_estimate=cost(4 * count * columns * channels * hidden, 6 * count * columns * channels),
            name="right",
        )(token_count, pair_state, in_gain, in_bias, right_weights, *far)

    if by_hops:
        early = move(right, early)
        arrived.append(move(later_pair, out))
        bands = []
        for (first, count), far in zip(spans, arrived):
            held = right_of(first, count, far)
            bands.append([held, move(held, near), move(held, cross), early])
        picks, place = [(0, 1, 1), (1, 2, 3)], hop_place
    else:
        bands, picks = band_by_sums(right, spans, window, row_count, col_count, columns)
        place = lambda: 0

    done = []
    for (first, count), band in zip(spans, bands):
        last = first + count == columns
        scratch = [
            pltpu.VMEM((width // LANES, hidden * pitch(count), LANES), jnp.float32),
            pltpu.VMEM((hidden * pitch(count), LANES), jnp.float32),
            pltpu.VMEM((rows * pitch(count), channels), jnp.float32),
        ]
        if last:
            scratch += [
                pltpu.VMEM((rows, count, channels), jnp.bfloat16),
                pltpu.SemaphoreType.DMA((len(done) + rows // 16,)),
            ]
        filled = pl.pallas_call(
            functools.partial(product_kernel, picks, place, len(band), first, last),
            out_shape=jax.ShapeDtypeStruct(
                (rows, columns if last else count, channels), jnp.bfloat16
            ),
            in_specs=[VMEM] * (len(band) + 2) + [SMEM, SMEM, VMEM] + [VMEM] * len(done) * last,
            out_specs=ANY if last else VMEM,
            scratch_shapes=scratch,
            compiler_params=params(2 * block, 2 * hidden * (rows + 2 * count) * width),
            cost_estimate=cost(2 * rows * count * depth * hidden, 4 * rows * depth * hidden),
            name="product",
        )(*band, left, gate, out_gain, out_bias, out_weights, *(done if last else []))
        done.append(filled)
    return filled


def solution(mesh):
    placed = (P(("crops", "row"), "col", None), P("crops"), P(), P(), P(), P(), P(), P(), P())
    return jax.shard_map(
        on_device,
        mesh=mesh,
        in_specs=placed,
        out_specs=P(("crops", "row"), "col", None),
        check_vma=False,
    )
```

```python
import functools

import jax
import jax.numpy as jnp
from jax import lax
from jax.experimental import pallas as pl
from jax.experimental.pallas import tpu as pltpu
from jax.sharding import PartitionSpec as P

LANES = 128
MIB = 1024 * 1024


def params(*sizes):
    return pltpu.CompilerParams(vmem_limit_bytes=min(6 * MIB + 2 * sum(sizes), 56 * MIB))


def cost(flops, bytes_accessed):
    return pl.CostEstimate(flops=flops, bytes_accessed=bytes_accessed, transcendentals=0)


VMEM = pl.BlockSpec(memory_space=pltpu.VMEM)
SMEM = pl.BlockSpec(memory_space=pltpu.SMEM)
ANY = pl.BlockSpec(memory_space=pl.ANY)


def pitch(rows):
    return (rows // 8 | 1) * 8


def shifted(array, axis, by):
    devices = lax.axis_size(axis)
    return lax.ppermute(array, axis, [(i, (i + by) % devices) for i in range(devices)])


def from_root(array, axis, root):
    mine = lax.axis_index(axis) == root
    return lax.psum(jnp.where(mine, array, jnp.zeros_like(array)), axis)


def layer_norm(values, gain, offset):
    average = jnp.mean(values, axis=-1, keepdims=True)
    centered = values - average
    variance = jnp.mean(centered * centered, axis=-1, keepdims=True)
    return centered * lax.rsqrt(variance + 1e-05) * gain + offset


def normed_rows(block, gain_ref, bias_ref):
    rows, columns, channels = block.shape
    values = block.reshape(rows * columns, channels).astype(jnp.float32)
    return layer_norm(values, gain_ref[...], bias_ref[...]).astype(jnp.bfloat16)


def mine_kernel(first, tokens_ref, far_ref, near_ref, gain_ref, bias_ref, weights_ref, out_ref):
    count, columns, _ = out_ref.shape
    col_pos, place = lax.axis_index("col"), hop_place()
    third_block = jnp.where((place == 0) | (place == 3), (col_pos + 1) % 4, col_pos)
    row_token = col_pos * columns + first
    step = 4
    for at in range(0, count, step):
        block = jnp.where(place < 2, near_ref[pl.ds(at, step)], far_ref[pl.ds(at, step)])
        normed = normed_rows(block, gain_ref, bias_ref)
        both = jnp.dot(normed, weights_ref[...], preferred_element_type=jnp.float32)
        parts = masked_right(both, tokens_ref[0], row_token + at, third_block, columns)
        for row, part in enumerate(parts):
            out_ref[at + row] = part


def masked_right(both, tokens, row_token, third_block, columns):
    hidden = both.shape[1] // 2
    right = jax.nn.sigmoid(both[:, :hidden]) * both[:, hidden:]
    position = lax.broadcasted_iota(jnp.int32, (columns, hidden), 0)
    parts = []
    for row in range(both.shape[0] // columns):
        limit = jnp.where(row_token + row < tokens, tokens - third_block * columns, 0)
        part = right[row * columns : (row + 1) * columns]
        parts.append(jnp.where(position < limit, part, 0.0).astype(jnp.bfloat16))
    return parts


def left_kernel(blocks, later, tokens_ref, *refs):
    pair_refs, refs = refs[:blocks], refs[blocks:]
    gain_ref, bias_ref, weights_ref, gate_weights_ref, *passed, scratch = refs
    passed, (left_ref, gate_ref, right_ref, later_ref), handed = passed[:4], passed[4:8], passed[8:]
    later_ref[...] = pair_refs[0][pl.ds(later, later_ref.shape[0])]
    for source, target in zip(passed, handed):
        target[...] = source[...]
    rows, columns, channels = pair_refs[0].shape
    hidden, _, width = left_ref.shape
    tokens = tokens_ref[0]
    row_start = lax.axis_index("row") * rows
    col_pos, col_count = lax.axis_index("col"), lax.axis_size("col")
    lane = lax.broadcasted_iota(jnp.int32, (1, width), 1)
    keep = jnp.zeros((1, width), jnp.float32)
    for at in range(blocks):
        end = at * columns + jnp.minimum(tokens - (col_pos + at) % col_count * columns, columns)
        keep += jnp.where((lane >= at * columns) & (lane < end), 1.0, 0.0)
    padding = [jnp.zeros((width - blocks * columns, channels), jnp.bfloat16)]
    if width == blocks * columns:
        padding = []
    step = 4
    for first in range(0, rows, step):
        normed = [normed_rows(ref[pl.ds(first, step)], gain_ref, bias_ref) for ref in pair_refs]
        gate = jnp.dot(normed[0], gate_weights_ref[...], preferred_element_type=jnp.float32)
        gate_ref[pl.ds(first, step)] = jax.nn.sigmoid(gate).reshape(step, columns, channels)
        both = jnp.dot(normed[0], passed[2][...], preferred_element_type=jnp.float32)
        for row, part in enumerate(masked_right(both, tokens, row_start + first, col_pos, columns)):
            right_ref[first + row] = part
        for row in range(step):
            thirds = [piece[row * columns : (row + 1) * columns] for piece in normed]
            both = lax.dot_general(
                weights_ref[...],
                jnp.concatenate(thirds + padding, axis=0),
                (((1,), (1,)), ((), ())),
                preferred_element_type=jnp.float32,
            )
            left = jax.nn.sigmoid(both[:hidden]) * both[hidden:]
            valid = jnp.where(row_start + first + row < tokens, keep, 0.0)
            left = jnp.where(valid > 0.0, left, 0.0)
            for at in range(0, width, LANES):
                scratch[at // LANES, pl.ds(first + row, hidden, stride=pitch(rows)), :] = left[
                    :, at : at + LANES
                ]
    for channel in range(hidden):
        for at in range(0, width, LANES):
            one = scratch[at // LANES, pl.ds(channel * pitch(rows), rows), :]
            left_ref[channel, :, at : at + LANES] = one.astype(jnp.bfloat16)


def turned(pieces, width):
    rows = sum(piece.shape[0] for piece in pieces)
    hidden = pieces[0].shape[1]
    if width > rows:
        pieces = pieces + [jnp.zeros((width - rows, hidden), pieces[0].dtype)]
    row = lax.broadcasted_iota(jnp.int32, (hidden, hidden), 0)
    column = lax.broadcasted_iota(jnp.int32, (hidden, hidden), 1)
    identity = (row == column).astype(jnp.float32).astype(jnp.bfloat16)
    return lax.dot_general(
        identity,
        jnp.concatenate(pieces, axis=0),
        (((1,), (1,)), ((), ())),
        preferred_element_type=jnp.float32,
    )


def product_kernel(picks, place, rights, first, count, last, *refs):
    right_refs, refs = refs[:rights], refs[rights:]
    left_ref, gate_ref, gain_ref, bias_ref, weights_ref, *done, out_ref = refs[: -5 if last else -3]
    right, product, updates = refs[-5:-2] if last else refs[-3:]
    result, sent = refs[-2:] if last else (out_ref, None)
    hidden, rows, width = left_ref.shape
    apart = pitch(count)
    mine = place()

    def row_of(source, token):
        ref = right_refs[source]
        return ref[token if ref.shape[0] == count else first + token]

    copies, start = [], 0
    for at, ref in enumerate(done):
        columns = pl.ds(start, ref.shape[1])
        copies.append(pltpu.make_async_copy(ref, out_ref.at[:, columns], sent.at[at]))
        copies[-1].start()
        start += ref.shape[1]

    for token in range(count):
        pieces = []
        for sources in picks:
            piece = row_of(sources[0], token)
            for at, source in enumerate(sources[1:], 1):
                if source != sources[at - 1]:
                    piece = jnp.where(mine >= at, row_of(source, token), piece)
            pieces.append(piece)
        one = turned(pieces, width)
        for at in range(0, width, LANES):
            right[at // LANES, pl.ds(token, hidden, stride=apart), :] = one[:, at : at + LANES]

    ways = 4
    totals = [jnp.zeros((count, rows), jnp.float32)] * ways
    for channel in range(hidden):
        one = 0.0
        for at in range(0, width, LANES):
            one += lax.dot_general(
                right[at // LANES, pl.ds(channel * apart, count), :].astype(jnp.bfloat16),
                left_ref[channel, :, at : at + LANES],
                (((1,), (1,)), ((), ())),
                preferred_element_type=jnp.float32,
            )
        product[pl.ds(channel * apart, count), :rows] = one
        totals[channel % ways] += one
    average = sum(totals) / hidden
    totals = [jnp.zeros((count, rows), jnp.float32)] * ways
    for channel in range(hidden):
        centered = product[pl.ds(channel * apart, count), :rows] - average
        totals[channel % ways] += centered * centered
    scale = lax.rsqrt(sum(totals) / hidden + 1e-05)
    for channel in range(hidden):
        place = pl.ds(channel * apart, count)
        centered = product[place, :rows] - average
        product[place, :rows] = centered * scale * gain_ref[channel] + bias_ref[channel]
    for token in range(count):
        mixed = product[pl.ds(token, hidden, stride=apart), :][:, :rows].astype(jnp.bfloat16)
        updates[pl.ds(token, rows, stride=apart), :] = lax.dot_general(
            mixed, weights_ref[...], (((0,), (0,)), ((), ())), preferred_element_type=jnp.float32
        )
    step = 16
    for at in range(0, rows, step):
        gate = gate_ref[pl.ds(at, step), pl.ds(first, count)]
        for row in range(step):
            update = updates[pl.ds((at + row) * apart, count), :]
            result[at + row] = (gate[row] * update).astype(jnp.bfloat16)
        if last:
            target = out_ref.at[pl.ds(at, step), pl.ds(first, count)]
            place = sent.at[len(done) + at // step]
            copies.append(pltpu.make_async_copy(result.at[pl.ds(at, step)], target, place))
            copies[-1].start()
    for copy in copies:
        copy.wait()


def band_by_sums(right, spans, window, row_count, col_count, columns):
    blocks_per_row = col_count // row_count
    col_pos = lax.axis_index("col")
    pieces = []
    for offset in range(window):
        block_id = (col_pos - offset) % col_count
        start = block_id % blocks_per_row * columns
        received = from_root(
            lax.dynamic_slice_in_dim(right, start, columns, 0), "row", block_id // blocks_per_row
        )
        pieces.append(received if offset == 0 else shifted(received, "col", -offset))
    bands = [[piece[first : first + count] for piece in pieces] for first, count in spans]
    return bands, [(offset, offset) for offset in range(window)]


def hops():
    near, far, share = [], [], []
    for c in range(4):
        first, second = (c, c), (c, (c + 1) % 4)
        inner, outer = ((2, c), (3, c)) if c < 2 else ((1, c), (0, c))
        near += [(first, (c ^ 1, c)), (second, first)]
        far += [(first, inner), (second, outer)]
        share += [(inner, outer), (outer, inner), (first, (c ^ 1, c))]
    return near, far, share


def hop_place():
    row_pos = lax.axis_index("row")
    near = row_pos ^ lax.axis_index("col")
    inner = (row_pos == 1) | (row_pos == 2)
    return jnp.where(near < 2, near, jnp.where(inner, 2, 3))


def move(array, pairs):
    return lax.ppermute(
        array, ("row", "col"), [(r * 4 + c, to_r * 4 + to_c) for (r, c), (to_r, to_c) in pairs]
    )


def on_device(
    pair_state,
    token_count,
    in_gain,
    in_bias,
    in_weights,
    gate_weights,
    out_gain,
    out_bias,
    out_weights,
):
    rows, columns, channels = pair_state.shape
    hidden = out_weights.shape[0]
    tokens = rows * columns
    col_count = lax.axis_size("col")
    row_count = lax.axis_size("row")
    window = col_count // 2
    depth = window * columns
    width = -(-depth // LANES) * LANES
    in_gain, in_bias = in_gain.reshape(1, channels), in_bias.reshape(1, channels)
    block = 2 * tokens * max(channels, hidden)
    by_hops = row_count == 4 and col_count == 4
    last = 16
    spans = [(0, columns - last), (columns - last, last)]

    if by_hops:
        near, far, share = hops()
        soon = pair_state[: spans[0][1]]
        arrived = [(move(soon, far), move(soon, near))]
    pairs = [pair_state]
    for _ in range(window - 1):
        pairs.append(shifted(pairs[-1], "col", -1))
    passed = [in_gain, in_bias, in_weights[:, 2 * hidden :], out_weights]
    later = spans[1][0]
    left, gate, right, later_pair, *handed = pl.pallas_call(
        functools.partial(left_kernel, window, later),
        out_shape=[
            jax.ShapeDtypeStruct((hidden, rows, width), jnp.bfloat16),
            jax.ShapeDtypeStruct((rows, columns, channels), jnp.float32),
            jax.ShapeDtypeStruct((rows, columns, hidden), jnp.bfloat16),
            jax.ShapeDtypeStruct((rows - later, columns, channels), jnp.bfloat16),
        ]
        + [jax.ShapeDtypeStruct(array.shape, array.dtype) for array in passed],
        in_specs=[SMEM] + [VMEM] * (window + 8),
        out_specs=[VMEM] * 8,
        scratch_shapes=[pltpu.VMEM((width // LANES, hidden * pitch(rows), LANES), jnp.float32)],
        compiler_params=params((window + 4) * block, 6 * hidden * rows * width),
        cost_estimate=cost(
            4 * window * tokens * channels * hidden, 6 * rows * width * hidden
        ),
        name="left_and_gate",
    )(token_count, *pairs, in_gain, in_bias, in_weights[:, : 2 * hidden].T, gate_weights, *passed)
    in_gain, in_bias, right_weights, out_weights = handed

    def mine_of(first, far_pair, near_pair):
        count = near_pair.shape[0]
        return pl.pallas_call(
            functools.partial(mine_kernel, first),
            out_shape=jax.ShapeDtypeStruct((count, columns, hidden), jnp.bfloat16),
            in_specs=[SMEM] + [VMEM] * 5,
            out_specs=VMEM,
            compiler_params=params(2 * block),
            cost_estimate=cost(4 * count * columns * channels * hidden, 6 * count * columns * channels),
            name="mine",
        )(token_count, far_pair, near_pair, in_gain, in_bias, right_weights)

    if by_hops:
        arrived.append((move(later_pair, far), move(later_pair, near)))
        bands = []
        for (first, _), pieces in zip(spans, arrived):
            mine = mine_of(first, *pieces)
            bands.append([right, mine, move(mine, share)])
        picks, place = [(0, 1, 1, 2), (1, 2, 2, 1)], hop_place
    else:
        bands, picks = band_by_sums(right, spans, window, row_count, col_count, columns)
        place = lambda: 0

    done = []
    for (first, count), band in zip(spans, bands):
        last = first + count == columns
        scratch = [
            pltpu.VMEM((width // LANES, hidden * pitch(count), LANES), jnp.float32),
            pltpu.VMEM((hidden * pitch(count), LANES), jnp.float32),
            pltpu.VMEM((rows * pitch(count), channels), jnp.float32),
        ]
        if last:
            scratch += [
                pltpu.VMEM((rows, count, channels), jnp.bfloat16),
                pltpu.SemaphoreType.DMA((len(done) + rows // 16,)),
            ]
        filled = pl.pallas_call(
            functools.partial(product_kernel, picks, place, len(band), first, count, last),
            out_shape=jax.ShapeDtypeStruct(
                (rows, columns if last else count, channels), jnp.bfloat16
            ),
            in_specs=[VMEM] * (len(band) + 2) + [SMEM, SMEM, VMEM] + [VMEM] * len(done) * last,
            out_specs=ANY if last else VMEM,
            scratch_shapes=scratch,
            compiler_params=params(2 * block, 2 * hidden * (rows + 2 * count) * width),
            cost_estimate=cost(2 * rows * count * depth * hidden, 4 * rows * depth * hidden),
            name="product",
        )(*band, left, gate, out_gain, out_bias, out_weights, *(done if last else []))
        done.append(filled)
    return filled


def solution(mesh):
    placed = (P(("crops", "row"), "col", None), P("crops"), P(), P(), P(), P(), P(), P(), P())
    return jax.shard_map(
        on_device,
        mesh=mesh,
        in_specs=placed,
        out_specs=P(("crops", "row"), "col", None),
        check_vma=False,
    )
```

```python
import functools

import jax
import jax.numpy as jnp
from jax import lax
from jax.experimental import pallas as pl
from jax.experimental.pallas import tpu as pltpu
from jax.sharding import PartitionSpec as P

LANES = 128
MIB = 1024 * 1024


def params(*sizes):
    return pltpu.CompilerParams(vmem_limit_bytes=min(6 * MIB + 2 * sum(sizes), 56 * MIB))


def cost(flops, bytes_accessed):
    return pl.CostEstimate(flops=flops, bytes_accessed=bytes_accessed, transcendentals=0)


VMEM = pl.BlockSpec(memory_space=pltpu.VMEM)
SMEM = pl.BlockSpec(memory_space=pltpu.SMEM)
ANY = pl.BlockSpec(memory_space=pl.ANY)


def pitch(rows):
    return (rows // 8 | 1) * 8


def shifted(array, axis, by):
    devices = lax.axis_size(axis)
    return lax.ppermute(array, axis, [(i, (i + by) % devices) for i in range(devices)])


def from_root(array, axis, root):
    mine = lax.axis_index(axis) == root
    return lax.psum(jnp.where(mine, array, jnp.zeros_like(array)), axis)


def layer_norm(values, gain, offset):
    average = jnp.mean(values, axis=-1, keepdims=True)
    centered = values - average
    variance = jnp.mean(centered * centered, axis=-1, keepdims=True)
    return centered * lax.rsqrt(variance + 1e-05) * gain + offset


def normed_rows(block, gain_ref, bias_ref):
    rows, columns, channels = block.shape
    values = block.reshape(rows * columns, channels).astype(jnp.float32)
    return layer_norm(values, gain_ref[...], bias_ref[...]).astype(jnp.bfloat16)


def mine_kernel(first, tokens_ref, far_ref, near_ref, gain_ref, bias_ref, weights_ref, out_ref):
    count, columns, _ = out_ref.shape
    col_pos, place = lax.axis_index("col"), hop_place()
    third_block = jnp.where((place == 0) | (place == 3), (col_pos + 1) % 4, col_pos)
    row_token = col_pos * columns + first
    step = 4
    for at in range(0, count, step):
        block = jnp.where(place < 2, near_ref[pl.ds(at, step)], far_ref[pl.ds(at, step)])
        normed = normed_rows(block, gain_ref, bias_ref)
        both = jnp.dot(normed, weights_ref[...], preferred_element_type=jnp.float32)
        parts = masked_right(both, tokens_ref[0], row_token + at, third_block, columns)
        for row, part in enumerate(parts):
            out_ref[at + row] = part


def masked_right(both, tokens, row_token, third_block, columns):
    hidden = both.shape[1] // 2
    right = jax.nn.sigmoid(both[:, :hidden]) * both[:, hidden:]
    position = lax.broadcasted_iota(jnp.int32, (columns, hidden), 0)
    parts = []
    for row in range(both.shape[0] // columns):
        limit = jnp.where(row_token + row < tokens, tokens - third_block * columns, 0)
        part = right[row * columns : (row + 1) * columns]
        parts.append(jnp.where(position < limit, part, 0.0).astype(jnp.bfloat16))
    return parts


def own_kernel(passes, tokens_ref, pair_ref, gate_weights_ref, *refs):
    passed, (gate_ref, right_ref), handed = refs[:passes], refs[passes : passes + 2], refs[passes + 2 :]
    gain_ref, bias_ref, right_weights_ref = passed[:3]
    for source, target in zip(passed, handed):
        target[...] = source[...]
    rows, columns, channels = pair_ref.shape
    row_start = lax.axis_index("row") * rows
    step = 4
    for first in range(0, rows, step):
        normed = normed_rows(pair_ref[pl.ds(first, step)], gain_ref, bias_ref)
        gate = jnp.dot(normed, gate_weights_ref[...], preferred_element_type=jnp.float32)
        gate_ref[pl.ds(first, step)] = jax.nn.sigmoid(gate).reshape(step, columns, channels)
        both = jnp.dot(normed, right_weights_ref[...], preferred_element_type=jnp.float32)
        parts = masked_right(
            both, tokens_ref[0], row_start + first, lax.axis_index("col"), columns
        )
        for row, part in enumerate(parts):
            right_ref[first + row] = part


def left_kernel(blocks, later, tokens_ref, *refs):
    pair_refs, refs = refs[:blocks], refs[blocks:]
    gain_ref, bias_ref, weights_ref, left_ref, later_ref, scratch = refs
    later_ref[...] = pair_refs[0][pl.ds(later, later_ref.shape[0])]
    rows, columns, channels = pair_refs[0].shape
    hidden, _, width = left_ref.shape
    tokens = tokens_ref[0]
    row_start = lax.axis_index("row") * rows
    col_pos, col_count = lax.axis_index("col"), lax.axis_size("col")
    lane = lax.broadcasted_iota(jnp.int32, (1, width), 1)
    keep = jnp.zeros((1, width), jnp.float32)
    for at in range(blocks):
        end = at * columns + jnp.minimum(tokens - (col_pos + at) % col_count * columns, columns)
        keep += jnp.where((lane >= at * columns) & (lane < end), 1.0, 0.0)
    padding = [jnp.zeros((width - blocks * columns, channels), jnp.bfloat16)]
    if width == blocks * columns:
        padding = []
    step = 4
    for first in range(0, rows, step):
        normed = [normed_rows(ref[pl.ds(first, step)], gain_ref, bias_ref) for ref in pair_refs]
        for row in range(step):
            thirds = [piece[row * columns : (row + 1) * columns] for piece in normed]
            both = lax.dot_general(
                weights_ref[...],
                jnp.concatenate(thirds + padding, axis=0),
                (((1,), (1,)), ((), ())),
                preferred_element_type=jnp.float32,
            )
            left = jax.nn.sigmoid(both[:hidden]) * both[hidden:]
            valid = jnp.where(row_start + first + row < tokens, keep, 0.0)
            left = jnp.where(valid > 0.0, left, 0.0)
            for at in range(0, width, LANES):
                scratch[at // LANES, pl.ds(first + row, hidden, stride=pitch(rows)), :] = left[
                    :, at : at + LANES
                ]
    for channel in range(hidden):
        for at in range(0, width, LANES):
            one = scratch[at // LANES, pl.ds(channel * pitch(rows), rows), :]
            left_ref[channel, :, at : at + LANES] = one.astype(jnp.bfloat16)


def turned(pieces, width):
    rows = sum(piece.shape[0] for piece in pieces)
    hidden = pieces[0].shape[1]
    if width > rows:
        pieces = pieces + [jnp.zeros((width - rows, hidden), pieces[0].dtype)]
    row = lax.broadcasted_iota(jnp.int32, (hidden, hidden), 0)
    column = lax.broadcasted_iota(jnp.int32, (hidden, hidden), 1)
    identity = (row == column).astype(jnp.float32).astype(jnp.bfloat16)
    return lax.dot_general(
        identity,
        jnp.concatenate(pieces, axis=0),
        (((1,), (1,)), ((), ())),
        preferred_element_type=jnp.float32,
    )


def product_kernel(picks, place, rights, first, count, last, *refs):
    right_refs, refs = refs[:rights], refs[rights:]
    left_ref, gate_ref, gain_ref, bias_ref, weights_ref, *done, out_ref = refs[: -5 if last else -3]
    right, product, updates = refs[-5:-2] if last else refs[-3:]
    result, sent = refs[-2:] if last else (out_ref, None)
    hidden, rows, width = left_ref.shape
    apart = pitch(count)
    mine = place()

    def row_of(source, token):
        ref = right_refs[source]
        return ref[token if ref.shape[0] == count else first + token]

    copies, start = [], 0
    for at, ref in enumerate(done):
        columns = pl.ds(start, ref.shape[1])
        copies.append(pltpu.make_async_copy(ref, out_ref.at[:, columns], sent.at[at]))
        copies[-1].start()
        start += ref.shape[1]

    for token in range(count):
        pieces = []
        for sources in picks:
            piece = row_of(sources[0], token)
            for at, source in enumerate(sources[1:], 1):
                if source != sources[at - 1]:
                    piece = jnp.where(mine >= at, row_of(source, token), piece)
            pieces.append(piece)
        one = turned(pieces, width)
        for at in range(0, width, LANES):
            right[at // LANES, pl.ds(token, hidden, stride=apart), :] = one[:, at : at + LANES]

    ways = 4
    totals = [jnp.zeros((count, rows), jnp.float32)] * ways
    for channel in range(hidden):
        one = 0.0
        for at in range(0, width, LANES):
            one += lax.dot_general(
                right[at // LANES, pl.ds(channel * apart, count), :].astype(jnp.bfloat16),
                left_ref[channel, :, at : at + LANES],
                (((1,), (1,)), ((), ())),
                preferred_element_type=jnp.float32,
            )
        product[pl.ds(channel * apart, count), :rows] = one
        totals[channel % ways] += one
    average = sum(totals) / hidden
    totals = [jnp.zeros((count, rows), jnp.float32)] * ways
    for channel in range(hidden):
        centered = product[pl.ds(channel * apart, count), :rows] - average
        totals[channel % ways] += centered * centered
    scale = lax.rsqrt(sum(totals) / hidden + 1e-05)
    for channel in range(hidden):
        place = pl.ds(channel * apart, count)
        centered = product[place, :rows] - average
        product[place, :rows] = centered * scale * gain_ref[channel] + bias_ref[channel]
    for token in range(count):
        mixed = product[pl.ds(token, hidden, stride=apart), :][:, :rows].astype(jnp.bfloat16)
        updates[pl.ds(token, rows, stride=apart), :] = lax.dot_general(
            mixed, weights_ref[...], (((0,), (0,)), ((), ())), preferred_element_type=jnp.float32
        )
    step = 16
    for at in range(0, rows, step):
        gate = gate_ref[pl.ds(at, step), pl.ds(first, count)]
        for row in range(step):
            update = updates[pl.ds((at + row) * apart, count), :]
            result[at + row] = (gate[row] * update).astype(jnp.bfloat16)
        if last:
            target = out_ref.at[pl.ds(at, step), pl.ds(first, count)]
            place = sent.at[len(done) + at // step]
            copies.append(pltpu.make_async_copy(result.at[pl.ds(at, step)], target, place))
            copies[-1].start()
    for copy in copies:
        copy.wait()


def band_by_sums(right, spans, window, row_count, col_count, columns):
    blocks_per_row = col_count // row_count
    col_pos = lax.axis_index("col")
    pieces = []
    for offset in range(window):
        block_id = (col_pos - offset) % col_count
        start = block_id % blocks_per_row * columns
        received = from_root(
            lax.dynamic_slice_in_dim(right, start, columns, 0), "row", block_id // blocks_per_row
        )
        pieces.append(received if offset == 0 else shifted(received, "col", -offset))
    bands = [[piece[first : first + count] for piece in pieces] for first, count in spans]
    return bands, [(offset, offset) for offset in range(window)]


def hops():
    near, far, share = [], [], []
    for c in range(4):
        first, second = (c, c), (c, (c + 1) % 4)
        inner, outer = ((2, c), (3, c)) if c < 2 else ((1, c), (0, c))
        near += [(first, (c ^ 1, c)), (second, first)]
        far += [(first, inner), (second, outer)]
        share += [(inner, outer), (outer, inner), (first, (c ^ 1, c))]
    return near, far, share


def hop_place():
    row_pos = lax.axis_index("row")
    near = row_pos ^ lax.axis_index("col")
    inner = (row_pos == 1) | (row_pos == 2)
    return jnp.where(near < 2, near, jnp.where(inner, 2, 3))


def move(array, pairs):
    return lax.ppermute(
        array, ("row", "col"), [(r * 4 + c, to_r * 4 + to_c) for (r, c), (to_r, to_c) in pairs]
    )


def on_device(
    pair_state,
    token_count,
    in_gain,
    in_bias,
    in_weights,
    gate_weights,
    out_gain,
    out_bias,
    out_weights,
):
    rows, columns, channels = pair_state.shape
    hidden = out_weights.shape[0]
    tokens = rows * columns
    col_count = lax.axis_size("col")
    row_count = lax.axis_size("row")
    window = col_count // 2
    depth = window * columns
    width = -(-depth // LANES) * LANES
    in_gain, in_bias = in_gain.reshape(1, channels), in_bias.reshape(1, channels)
    block = 2 * tokens * max(channels, hidden)
    by_hops = row_count == 4 and col_count == 4
    last = 16
    spans = [(0, columns - last), (columns - last, last)]

    if by_hops:
        near, far, share = hops()
        soon = pair_state[: spans[0][1]]
        arrived = [(move(soon, far), move(soon, near))]
    pairs = [pair_state]
    for _ in range(window - 1):
        pairs.append(shifted(pairs[-1], "col", -1))
    left_weights, right_weights = in_weights[:, : 2 * hidden].T, in_weights[:, 2 * hidden :]
    passed = [in_gain, in_bias, right_weights, left_weights, out_weights, pair_state]
    gate, right, *handed = pl.pallas_call(
        functools.partial(own_kernel, len(passed)),
        out_shape=[
            jax.ShapeDtypeStruct((rows, columns, channels), jnp.float32),
            jax.ShapeDtypeStruct((rows, columns, hidden), jnp.bfloat16),
        ]
        + [jax.ShapeDtypeStruct(array.shape, array.dtype) for array in passed],
        in_specs=[SMEM] + [VMEM] * (2 + len(passed)),
        out_specs=[VMEM] * (2 + len(passed)),
        compiler_params=params(6 * block),
        cost_estimate=cost(6 * tokens * channels * hidden, 8 * tokens * channels),
        name="own",
    )(token_count, pair_state, gate_weights, *passed)
    in_gain, in_bias, right_weights, left_weights, out_weights, pairs[0] = handed
    later = spans[1][0]
    left, later_pair = pl.pallas_call(
        functools.partial(left_kernel, window, later),
        out_shape=[
            jax.ShapeDtypeStruct((hidden, rows, width), jnp.bfloat16),
            jax.ShapeDtypeStruct((rows - later, columns, channels), jnp.bfloat16),
        ],
        in_specs=[SMEM] + [VMEM] * (window + 3),
        out_specs=[VMEM] * 2,
        scratch_shapes=[pltpu.VMEM((width // LANES, hidden * pitch(rows), LANES), jnp.float32)],
        compiler_params=params((window + 2) * block, 6 * hidden * rows * width),
        cost_estimate=cost(4 * window * tokens * channels * hidden, 6 * rows * width * hidden),
        name="left",
    )(token_count, *pairs, in_gain, in_bias, left_weights)

    def mine_of(first, far_pair, near_pair):
        count = near_pair.shape[0]
        return pl.pallas_call(
            functools.partial(mine_kernel, first),
            out_shape=jax.ShapeDtypeStruct((count, columns, hidden), jnp.bfloat16),
            in_specs=[SMEM] + [VMEM] * 5,
            out_specs=VMEM,
            compiler_params=params(2 * block),
            cost_estimate=cost(4 * count * columns * channels * hidden, 6 * count * columns * channels),
            name="mine",
        )(token_count, far_pair, near_pair, in_gain, in_bias, right_weights)

    if by_hops:
        arrived.append((move(later_pair, far), move(later_pair, near)))
        bands = []
        for (first, _), pieces in zip(spans, arrived):
            mine = mine_of(first, *pieces)
            bands.append([right, mine, move(mine, share)])
        picks, place = [(0, 1, 1, 2), (1, 2, 2, 1)], hop_place
    else:
        bands, picks = band_by_sums(right, spans, window, row_count, col_count, columns)
        place = lambda: 0

    done = []
    for (first, count), band in zip(spans, bands):
        last = first + count == columns
        scratch = [
            pltpu.VMEM((width // LANES, hidden * pitch(count), LANES), jnp.float32),
            pltpu.VMEM((hidden * pitch(count), LANES), jnp.float32),
            pltpu.VMEM((rows * pitch(count), channels), jnp.float32),
        ]
        if last:
            scratch += [
                pltpu.VMEM((rows, count, channels), jnp.bfloat16),
                pltpu.SemaphoreType.DMA((len(done) + rows // 16,)),
            ]
        filled = pl.pallas_call(
            functools.partial(product_kernel, picks, place, len(band), first, count, last),
            out_shape=jax.ShapeDtypeStruct(
                (rows, columns if last else count, channels), jnp.bfloat16
            ),
            in_specs=[VMEM] * (len(band) + 2) + [SMEM, SMEM, VMEM] + [VMEM] * len(done) * last,
            out_specs=ANY if last else VMEM,
            scratch_shapes=scratch,
            compiler_params=params(2 * block, 2 * hidden * (rows + 2 * count) * width),
            cost_estimate=cost(2 * rows * count * depth * hidden, 4 * rows * depth * hidden),
            name="product",
        )(*band, left, gate, out_gain, out_bias, out_weights, *(done if last else []))
        done.append(filled)
    return filled


def solution(mesh):
    placed = (P(("crops", "row"), "col", None), P("crops"), P(), P(), P(), P(), P(), P(), P())
    return jax.shard_map(
        on_device,
        mesh=mesh,
        in_specs=placed,
        out_specs=P(("crops", "row"), "col", None),
        check_vma=False,
    )
```

```python
import functools

import jax
import jax.numpy as jnp
from jax import lax
from jax.experimental import pallas as pl
from jax.experimental.pallas import tpu as pltpu
from jax.sharding import PartitionSpec as P

LANES = 128
MIB = 1024 * 1024


def params(*sizes):
    return pltpu.CompilerParams(vmem_limit_bytes=min(6 * MIB + 2 * sum(sizes), 56 * MIB))


def cost(flops, bytes_accessed):
    return pl.CostEstimate(flops=flops, bytes_accessed=bytes_accessed, transcendentals=0)


VMEM = pl.BlockSpec(memory_space=pltpu.VMEM)
SMEM = pl.BlockSpec(memory_space=pltpu.SMEM)
ANY = pl.BlockSpec(memory_space=pl.ANY)


def pitch(rows):
    return (rows // 8 | 1) * 8


def shifted(array, axis, by):
    devices = lax.axis_size(axis)
    return lax.ppermute(array, axis, [(i, (i + by) % devices) for i in range(devices)])


def from_root(array, axis, root):
    mine = lax.axis_index(axis) == root
    return lax.psum(jnp.where(mine, array, jnp.zeros_like(array)), axis)


def layer_norm(values, gain, offset):
    average = jnp.mean(values, axis=-1, keepdims=True)
    centered = values - average
    variance = jnp.mean(centered * centered, axis=-1, keepdims=True)
    return centered * lax.rsqrt(variance + 1e-05) * gain + offset


def normed_rows(block, gain_ref, bias_ref):
    rows, columns, channels = block.shape
    values = block.reshape(rows * columns, channels).astype(jnp.float32)
    return layer_norm(values, gain_ref[...], bias_ref[...]).astype(jnp.bfloat16)


def mine_kernel(first, tokens_ref, far_ref, near_ref, gain_ref, bias_ref, weights_ref, out_ref):
    count, columns, _ = out_ref.shape
    col_pos, place = lax.axis_index("col"), hop_place()
    third_block = jnp.where((place == 0) | (place == 3), (col_pos + 1) % 4, col_pos)
    row_token = col_pos * columns + first
    step = 4
    for at in range(0, count, step):
        block = jnp.where(place < 2, near_ref[pl.ds(at, step)], far_ref[pl.ds(at, step)])
        normed = normed_rows(block, gain_ref, bias_ref)
        both = jnp.dot(normed, weights_ref[...], preferred_element_type=jnp.float32)
        parts = masked_right(both, tokens_ref[0], row_token + at, third_block, columns)
        for row, part in enumerate(parts):
            out_ref[at + row] = part


def masked_right(both, tokens, row_token, third_block, columns):
    hidden = both.shape[1] // 2
    right = jax.nn.sigmoid(both[:, :hidden]) * both[:, hidden:]
    position = lax.broadcasted_iota(jnp.int32, (columns, hidden), 0)
    parts = []
    for row in range(both.shape[0] // columns):
        limit = jnp.where(row_token + row < tokens, tokens - third_block * columns, 0)
        part = right[row * columns : (row + 1) * columns]
        parts.append(jnp.where(position < limit, part, 0.0).astype(jnp.bfloat16))
    return parts


def own_kernel(passes, tokens_ref, pair_ref, gate_weights_ref, *refs):
    passed, (gate_ref, right_ref), handed = refs[:passes], refs[passes : passes + 2], refs[passes + 2 :]
    gain_ref, bias_ref, right_weights_ref = passed[:3]
    for source, target in zip(passed, handed):
        target[...] = source[...]
    rows, columns, channels = pair_ref.shape
    row_start = lax.axis_index("row") * rows
    step = 4
    for first in range(0, rows, step):
        normed = normed_rows(pair_ref[pl.ds(first, step)], gain_ref, bias_ref)
        gate = jnp.dot(normed, gate_weights_ref[...], preferred_element_type=jnp.float32)
        gate_ref[pl.ds(first, step)] = jax.nn.sigmoid(gate).reshape(step, columns, channels)
        both = jnp.dot(normed, right_weights_ref[...], preferred_element_type=jnp.float32)
        parts = masked_right(
            both, tokens_ref[0], row_start + first, lax.axis_index("col"), columns
        )
        for row, part in enumerate(parts):
            right_ref[first + row] = part


def left_kernel(here, blocks, tokens_ref, *refs):
    pair_refs, refs = refs[: len(here)], refs[len(here) :]
    gain_ref, bias_ref, weights_ref, *base_refs, left_ref, scratch = refs
    if here[0] == 0:
        *base_refs, left_ref, later_ref = (*base_refs, left_ref)
        later_ref[...] = pair_refs[0][pl.ds(pair_refs[0].shape[0] - later_ref.shape[0], later_ref.shape[0])]
    rows, columns, channels = pair_refs[0].shape
    hidden, _, width = left_ref.shape
    tokens = tokens_ref[0]
    row_start = lax.axis_index("row") * rows
    col_pos, col_count = lax.axis_index("col"), lax.axis_size("col")
    lane = lax.broadcasted_iota(jnp.int32, (1, width), 1)
    keep = jnp.zeros((1, width), jnp.float32)
    for at in range(blocks):
        end = at * columns + jnp.minimum(tokens - (col_pos + at) % col_count * columns, columns)
        keep += jnp.where((lane >= at * columns) & (lane < end), 1.0, 0.0)
    padding = [jnp.zeros((width - blocks * columns, channels), jnp.bfloat16)]
    if width == blocks * columns:
        padding = []
    step = 4
    for first in range(0, rows, step):
        normed = [normed_rows(ref[pl.ds(first, step)], gain_ref, bias_ref) for ref in pair_refs]
        for row in range(step):
            thirds = [jnp.zeros((columns, channels), jnp.bfloat16)] * blocks
            for at, piece in zip(here, normed):
                thirds[at] = piece[row * columns : (row + 1) * columns]
            both = lax.dot_general(
                weights_ref[...],
                jnp.concatenate(thirds + padding, axis=0),
                (((1,), (1,)), ((), ())),
                preferred_element_type=jnp.float32,
            )
            left = jax.nn.sigmoid(both[:hidden]) * both[hidden:]
            valid = jnp.where(row_start + first + row < tokens, keep, 0.0)
            left = jnp.where(valid > 0.0, left, 0.0)
            for at in range(0, width, LANES):
                scratch[at // LANES, pl.ds(first + row, hidden, stride=pitch(rows)), :] = left[
                    :, at : at + LANES
                ]
    for channel in range(hidden):
        for at in range(0, width, LANES):
            one = scratch[at // LANES, pl.ds(channel * pitch(rows), rows), :].astype(jnp.bfloat16)
            for base_ref in base_refs:
                one += base_ref[channel, :, at : at + LANES]
            left_ref[channel, :, at : at + LANES] = one


def turned(pieces, width):
    rows = sum(piece.shape[0] for piece in pieces)
    hidden = pieces[0].shape[1]
    if width > rows:
        pieces = pieces + [jnp.zeros((width - rows, hidden), pieces[0].dtype)]
    row = lax.broadcasted_iota(jnp.int32, (hidden, hidden), 0)
    column = lax.broadcasted_iota(jnp.int32, (hidden, hidden), 1)
    identity = (row == column).astype(jnp.float32).astype(jnp.bfloat16)
    return lax.dot_general(
        identity,
        jnp.concatenate(pieces, axis=0),
        (((1,), (1,)), ((), ())),
        preferred_element_type=jnp.float32,
    )


def product_kernel(picks, place, rights, first, count, last, *refs):
    right_refs, refs = refs[:rights], refs[rights:]
    left_ref, gate_ref, gain_ref, bias_ref, weights_ref, *done, out_ref = refs[: -5 if last else -3]
    right, product, updates = refs[-5:-2] if last else refs[-3:]
    result, sent = refs[-2:] if last else (out_ref, None)
    hidden, rows, width = left_ref.shape
    apart = pitch(count)
    mine = place()

    def row_of(source, token):
        ref = right_refs[source]
        return ref[token if ref.shape[0] == count else first + token]

    copies, start = [], 0
    for at, ref in enumerate(done):
        columns = pl.ds(start, ref.shape[1])
        copies.append(pltpu.make_async_copy(ref, out_ref.at[:, columns], sent.at[at]))
        copies[-1].start()
        start += ref.shape[1]

    for token in range(count):
        pieces = []
        for sources in picks:
            piece = row_of(sources[0], token)
            for at, source in enumerate(sources[1:], 1):
                if source != sources[at - 1]:
                    piece = jnp.where(mine >= at, row_of(source, token), piece)
            pieces.append(piece)
        one = turned(pieces, width)
        for at in range(0, width, LANES):
            right[at // LANES, pl.ds(token, hidden, stride=apart), :] = one[:, at : at + LANES]

    ways = 4
    totals = [jnp.zeros((count, rows), jnp.float32)] * ways
    for channel in range(hidden):
        one = 0.0
        for at in range(0, width, LANES):
            one += lax.dot_general(
                right[at // LANES, pl.ds(channel * apart, count), :].astype(jnp.bfloat16),
                left_ref[channel, :, at : at + LANES],
                (((1,), (1,)), ((), ())),
                preferred_element_type=jnp.float32,
            )
        product[pl.ds(channel * apart, count), :rows] = one
        totals[channel % ways] += one
    average = sum(totals) / hidden
    totals = [jnp.zeros((count, rows), jnp.float32)] * ways
    for channel in range(hidden):
        centered = product[pl.ds(channel * apart, count), :rows] - average
        totals[channel % ways] += centered * centered
    scale = lax.rsqrt(sum(totals) / hidden + 1e-05)
    for channel in range(hidden):
        place = pl.ds(channel * apart, count)
        centered = product[place, :rows] - average
        product[place, :rows] = centered * scale * gain_ref[channel] + bias_ref[channel]
    for token in range(count):
        mixed = product[pl.ds(token, hidden, stride=apart), :][:, :rows].astype(jnp.bfloat16)
        updates[pl.ds(token, rows, stride=apart), :] = lax.dot_general(
            mixed, weights_ref[...], (((0,), (0,)), ((), ())), preferred_element_type=jnp.float32
        )
    step = 16
    for at in range(0, rows, step):
        gate = gate_ref[pl.ds(at, step), pl.ds(first, count)]
        for row in range(step):
            update = updates[pl.ds((at + row) * apart, count), :]
            result[at + row] = (gate[row] * update).astype(jnp.bfloat16)
        if last:
            target = out_ref.at[pl.ds(at, step), pl.ds(first, count)]
            place = sent.at[len(done) + at // step]
            copies.append(pltpu.make_async_copy(result.at[pl.ds(at, step)], target, place))
            copies[-1].start()
    for copy in copies:
        copy.wait()


def band_by_sums(right, spans, window, row_count, col_count, columns):
    blocks_per_row = col_count // row_count
    col_pos = lax.axis_index("col")
    pieces = []
    for offset in range(window):
        block_id = (col_pos - offset) % col_count
        start = block_id % blocks_per_row * columns
        received = from_root(
            lax.dynamic_slice_in_dim(right, start, columns, 0), "row", block_id // blocks_per_row
        )
        pieces.append(received if offset == 0 else shifted(received, "col", -offset))
    bands = [[piece[first : first + count] for piece in pieces] for first, count in spans]
    return bands, [(offset, offset) for offset in range(window)]


def hops():
    near, far, share = [], [], []
    for c in range(4):
        first, second = (c, c), (c, (c + 1) % 4)
        inner, outer = ((2, c), (3, c)) if c < 2 else ((1, c), (0, c))
        near += [(first, (c ^ 1, c)), (second, first)]
        far += [(first, inner), (second, outer)]
        share += [(inner, outer), (outer, inner), (first, (c ^ 1, c))]
    return near, far, share


def hop_place():
    row_pos = lax.axis_index("row")
    near = row_pos ^ lax.axis_index("col")
    inner = (row_pos == 1) | (row_pos == 2)
    return jnp.where(near < 2, near, jnp.where(inner, 2, 3))


def move(array, pairs):
    return lax.ppermute(
        array, ("row", "col"), [(r * 4 + c, to_r * 4 + to_c) for (r, c), (to_r, to_c) in pairs]
    )


def on_device(
    pair_state,
    token_count,
    in_gain,
    in_bias,
    in_weights,
    gate_weights,
    out_gain,
    out_bias,
    out_weights,
):
    rows, columns, channels = pair_state.shape
    hidden = out_weights.shape[0]
    tokens = rows * columns
    col_count = lax.axis_size("col")
    row_count = lax.axis_size("row")
    window = col_count // 2
    depth = window * columns
    width = -(-depth // LANES) * LANES
    in_gain, in_bias = in_gain.reshape(1, channels), in_bias.reshape(1, channels)
    block = 2 * tokens * max(channels, hidden)
    by_hops = row_count == 4 and col_count == 4
    last = 16
    spans = [(0, columns - last), (columns - last, last)]

    if by_hops:
        near, far, share = hops()
        soon = pair_state[: spans[0][1]]
        arrived = [(move(soon, far), move(soon, near))]
    pairs = [pair_state]
    for _ in range(window - 1):
        pairs.append(shifted(pairs[-1], "col", -1))
    left_weights, right_weights = in_weights[:, : 2 * hidden].T, in_weights[:, 2 * hidden :]
    passed = [in_gain, in_bias, right_weights, left_weights, out_weights, pair_state]
    gate, right, *handed = pl.pallas_call(
        functools.partial(own_kernel, len(passed)),
        out_shape=[
            jax.ShapeDtypeStruct((rows, columns, channels), jnp.float32),
            jax.ShapeDtypeStruct((rows, columns, hidden), jnp.bfloat16),
        ]
        + [jax.ShapeDtypeStruct(array.shape, array.dtype) for array in passed],
        in_specs=[SMEM] + [VMEM] * (2 + len(passed)),
        out_specs=[VMEM] * (2 + len(passed)),
        compiler_params=params(6 * block),
        cost_estimate=cost(6 * tokens * channels * hidden, 8 * tokens * channels),
        name="own",
    )(token_count, pair_state, gate_weights, *passed)
    in_gain, in_bias, right_weights, left_weights, out_weights, pairs[0] = handed

    def left_of(here, *base):
        shapes = [jax.ShapeDtypeStruct((hidden, rows, width), jnp.bfloat16)]
        if here[0] == 0:
            shapes.append(jax.ShapeDtypeStruct((spans[1][1], columns, channels), jnp.bfloat16))
        return pl.pallas_call(
            functools.partial(left_kernel, here, window),
            out_shape=shapes,
            in_specs=[SMEM] + [VMEM] * (len(here) + 3 + len(base)),
            out_specs=[VMEM] * len(shapes),
            scratch_shapes=[
                pltpu.VMEM((width // LANES, hidden * pitch(rows), LANES), jnp.float32)
            ],
            compiler_params=params((len(here) + 2) * block, 6 * hidden * rows * width),
            cost_estimate=cost(
                4 * len(here) * tokens * channels * hidden, 6 * rows * width * hidden
            ),
            name="left",
        )(token_count, *[pairs[at] for at in here], in_gain, in_bias, left_weights, *base)

    left, later_pair = left_of([0])

    def mine_of(first, far_pair, near_pair):
        count = near_pair.shape[0]
        return pl.pallas_call(
            functools.partial(mine_kernel, first),
            out_shape=jax.ShapeDtypeStruct((count, columns, hidden), jnp.bfloat16),
            in_specs=[SMEM] + [VMEM] * 5,
            out_specs=VMEM,
            compiler_params=params(2 * block),
            cost_estimate=cost(4 * count * columns * channels * hidden, 6 * count * columns * channels),
            name="mine",
        )(token_count, far_pair, near_pair, in_gain, in_bias, right_weights)

    if by_hops:
        arrived.append((move(later_pair, far), move(later_pair, near)))
        bands = []
        for (first, _), pieces in zip(spans, arrived):
            mine = mine_of(first, *pieces)
            bands.append([right, mine, move(mine, share)])
        left, _ = lax.optimization_barrier((left, mine))
        picks, place = [(0, 1, 1, 2), (1, 2, 2, 1)], hop_place
    else:
        bands, picks = band_by_sums(right, spans, window, row_count, col_count, columns)
        place = lambda: 0

    (left,) = left_of(list(range(1, window)), left)
    done = []
    for (first, count), band in zip(spans, bands):
        last = first + count == columns
        scratch = [
            pltpu.VMEM((width // LANES, hidden * pitch(count), LANES), jnp.float32),
            pltpu.VMEM((hidden * pitch(count), LANES), jnp.float32),
            pltpu.VMEM((rows * pitch(count), channels), jnp.float32),
        ]
        if last:
            scratch += [
                pltpu.VMEM((rows, count, channels), jnp.bfloat16),
                pltpu.SemaphoreType.DMA((len(done) + rows // 16,)),
            ]
        filled = pl.pallas_call(
            functools.partial(product_kernel, picks, place, len(band), first, count, last),
            out_shape=jax.ShapeDtypeStruct(
                (rows, columns if last else count, channels), jnp.bfloat16
            ),
            in_specs=[VMEM] * (len(band) + 2) + [SMEM, SMEM, VMEM] + [VMEM] * len(done) * last,
            out_specs=ANY if last else VMEM,
            scratch_shapes=scratch,
            compiler_params=params(2 * block, 2 * hidden * (rows + 2 * count) * width),
            cost_estimate=cost(2 * rows * count * depth * hidden, 4 * rows * depth * hidden),
            name="product",
        )(*band, left, gate, out_gain, out_bias, out_weights, *(done if last else []))
        done.append(filled)
    return filled


def solution(mesh):
    placed = (P(("crops", "row"), "col", None), P("crops"), P(), P(), P(), P(), P(), P(), P())
    return jax.shard_map(
        on_device,
        mesh=mesh,
        in_specs=placed,
        out_specs=P(("crops", "row"), "col", None),
        check_vma=False,
    )
```

```python
import functools

import jax
import jax.numpy as jnp
from jax import lax
from jax.experimental import pallas as pl
from jax.experimental.pallas import tpu as pltpu
from jax.sharding import PartitionSpec as P

LANES = 128
MIB = 1024 * 1024


def params(*sizes):
    return pltpu.CompilerParams(vmem_limit_bytes=min(6 * MIB + 2 * sum(sizes), 56 * MIB))


def cost(flops, bytes_accessed):
    return pl.CostEstimate(flops=flops, bytes_accessed=bytes_accessed, transcendentals=0)


VMEM = pl.BlockSpec(memory_space=pltpu.VMEM)
SMEM = pl.BlockSpec(memory_space=pltpu.SMEM)
ANY = pl.BlockSpec(memory_space=pl.ANY)


def pitch(rows):
    return (rows // 8 | 1) * 8


def shifted(array, axis, by):
    devices = lax.axis_size(axis)
    return lax.ppermute(array, axis, [(i, (i + by) % devices) for i in range(devices)])


def from_root(array, axis, root):
    mine = lax.axis_index(axis) == root
    return lax.psum(jnp.where(mine, array, jnp.zeros_like(array)), axis)


def layer_norm(values, gain, offset):
    average = jnp.mean(values, axis=-1, keepdims=True)
    centered = values - average
    variance = jnp.mean(centered * centered, axis=-1, keepdims=True)
    return centered * lax.rsqrt(variance + 1e-05) * gain + offset


def normed_rows(block, gain_ref, bias_ref):
    rows, columns, channels = block.shape
    values = block.reshape(rows * columns, channels).astype(jnp.float32)
    return layer_norm(values, gain_ref[...], bias_ref[...]).astype(jnp.bfloat16)


def mine_kernel(first, tokens_ref, near_ref, far_ref, gain_ref, bias_ref, weights_ref, out_ref):
    count, columns, _ = out_ref.shape
    col_pos, place = lax.axis_index("col"), hop_place()
    third_block = jnp.where((place == 0) | (place == 3), (col_pos + 1) % 4, col_pos)
    row_token = col_pos * columns + first
    step = 4
    for at in range(0, count, step):
        block = jnp.where(place < 2, near_ref[pl.ds(at, step)], far_ref[pl.ds(at, step)])
        normed = normed_rows(block, gain_ref, bias_ref)
        both = jnp.dot(normed, weights_ref[...], preferred_element_type=jnp.float32)
        parts = masked_right(both, tokens_ref[0], row_token + at, third_block, columns)
        for row, part in enumerate(parts):
            out_ref[at + row] = part


def masked_right(both, tokens, row_token, third_block, columns):
    hidden = both.shape[1] // 2
    right = jax.nn.sigmoid(both[:, :hidden]) * both[:, hidden:]
    position = lax.broadcasted_iota(jnp.int32, (columns, hidden), 0)
    parts = []
    for row in range(both.shape[0] // columns):
        limit = jnp.where(row_token + row < tokens, tokens - third_block * columns, 0)
        part = right[row * columns : (row + 1) * columns]
        parts.append(jnp.where(position < limit, part, 0.0).astype(jnp.bfloat16))
    return parts


def own_kernel(passes, tokens_ref, pair_ref, gate_weights_ref, *refs):
    passed, (gate_ref, right_ref), handed = refs[:passes], refs[passes : passes + 2], refs[passes + 2 :]
    gain_ref, bias_ref, right_weights_ref = passed[:3]
    for source, target in zip(passed, handed):
        target[...] = source[...]
    rows, columns, channels = pair_ref.shape
    row_start = lax.axis_index("row") * rows
    step = 4
    for first in range(0, rows, step):
        normed = normed_rows(pair_ref[pl.ds(first, step)], gain_ref, bias_ref)
        gate = jnp.dot(normed, gate_weights_ref[...], preferred_element_type=jnp.float32)
        gate_ref[pl.ds(first, step)] = jax.nn.sigmoid(gate).reshape(step, columns, channels)
        both = jnp.dot(normed, right_weights_ref[...], preferred_element_type=jnp.float32)
        parts = masked_right(
            both, tokens_ref[0], row_start + first, lax.axis_index("col"), columns
        )
        for row, part in enumerate(parts):
            right_ref[first + row] = part


def left_kernel(here, blocks, tokens_ref, *refs):
    pair_refs, refs = refs[: len(here)], refs[len(here) :]
    gain_ref, bias_ref, weights_ref, *base_refs, left_ref, scratch = refs
    if here[0] == 0:
        *base_refs, left_ref, later_ref = (*base_refs, left_ref)
        later_ref[...] = pair_refs[0][pl.ds(pair_refs[0].shape[0] - later_ref.shape[0], later_ref.shape[0])]
    rows, columns, channels = pair_refs[0].shape
    hidden, _, width = left_ref.shape
    tokens = tokens_ref[0]
    row_start = lax.axis_index("row") * rows
    col_pos, col_count = lax.axis_index("col"), lax.axis_size("col")
    lane = lax.broadcasted_iota(jnp.int32, (1, width), 1)
    keep = jnp.zeros((1, width), jnp.float32)
    for at in range(blocks):
        end = at * columns + jnp.minimum(tokens - (col_pos + at) % col_count * columns, columns)
        keep += jnp.where((lane >= at * columns) & (lane < end), 1.0, 0.0)
    padding = [jnp.zeros((width - blocks * columns, channels), jnp.bfloat16)]
    if width == blocks * columns:
        padding = []
    step = 4
    for first in range(0, rows, step):
        normed = [normed_rows(ref[pl.ds(first, step)], gain_ref, bias_ref) for ref in pair_refs]
        for row in range(step):
            thirds = [jnp.zeros((columns, channels), jnp.bfloat16)] * blocks
            for at, piece in zip(here, normed):
                thirds[at] = piece[row * columns : (row + 1) * columns]
            both = lax.dot_general(
                weights_ref[...],
                jnp.concatenate(thirds + padding, axis=0),
                (((1,), (1,)), ((), ())),
                preferred_element_type=jnp.float32,
            )
            left = jax.nn.sigmoid(both[:hidden]) * both[hidden:]
            valid = jnp.where(row_start + first + row < tokens, keep, 0.0)
            left = jnp.where(valid > 0.0, left, 0.0)
            for at in range(0, width, LANES):
                scratch[at // LANES, pl.ds(first + row, hidden, stride=pitch(rows)), :] = left[
                    :, at : at + LANES
                ]
    for channel in range(hidden):
        for at in range(0, width, LANES):
            one = scratch[at // LANES, pl.ds(channel * pitch(rows), rows), :].astype(jnp.bfloat16)
            for base_ref in base_refs:
                one += base_ref[channel, :, at : at + LANES]
            left_ref[channel, :, at : at + LANES] = one


def turned(pieces, width):
    rows = sum(piece.shape[0] for piece in pieces)
    hidden = pieces[0].shape[1]
    if width > rows:
        pieces = pieces + [jnp.zeros((width - rows, hidden), pieces[0].dtype)]
    row = lax.broadcasted_iota(jnp.int32, (hidden, hidden), 0)
    column = lax.broadcasted_iota(jnp.int32, (hidden, hidden), 1)
    identity = (row == column).astype(jnp.float32).astype(jnp.bfloat16)
    return lax.dot_general(
        identity,
        jnp.concatenate(pieces, axis=0),
        (((1,), (1,)), ((), ())),
        preferred_element_type=jnp.float32,
    )


def product_kernel(picks, place, rights, first, count, last, *refs):
    right_refs, refs = refs[:rights], refs[rights:]
    left_ref, gate_ref, gain_ref, bias_ref, weights_ref, *done, out_ref = refs[: -5 if last else -3]
    right, product, updates = refs[-5:-2] if last else refs[-3:]
    result, sent = refs[-2:] if last else (out_ref, None)
    hidden, rows, width = left_ref.shape
    apart = pitch(count)
    mine = place()

    def row_of(source, token):
        ref = right_refs[source]
        return ref[token if ref.shape[0] == count else first + token]

    copies, start = [], 0
    for at, ref in enumerate(done):
        columns = pl.ds(start, ref.shape[1])
        copies.append(pltpu.make_async_copy(ref, out_ref.at[:, columns], sent.at[at]))
        copies[-1].start()
        start += ref.shape[1]

    for token in range(count):
        pieces = []
        for sources in picks:
            piece = row_of(sources[0], token)
            for at, source in enumerate(sources[1:], 1):
                if source != sources[at - 1]:
                    piece = jnp.where(mine >= at, row_of(source, token), piece)
            pieces.append(piece)
        one = turned(pieces, width)
        for at in range(0, width, LANES):
            right[at // LANES, pl.ds(token, hidden, stride=apart), :] = one[:, at : at + LANES]

    ways = 4
    totals = [jnp.zeros((count, rows), jnp.float32)] * ways
    for channel in range(hidden):
        one = 0.0
        for at in range(0, width, LANES):
            one += lax.dot_general(
                right[at // LANES, pl.ds(channel * apart, count), :].astype(jnp.bfloat16),
                left_ref[channel, :, at : at + LANES],
                (((1,), (1,)), ((), ())),
                preferred_element_type=jnp.float32,
            )
        product[pl.ds(channel * apart, count), :rows] = one
        totals[channel % ways] += one
    average = sum(totals) / hidden
    totals = [jnp.zeros((count, rows), jnp.float32)] * ways
    for channel in range(hidden):
        centered = product[pl.ds(channel * apart, count), :rows] - average
        totals[channel % ways] += centered * centered
    scale = lax.rsqrt(sum(totals) / hidden + 1e-05)
    for channel in range(hidden):
        place = pl.ds(channel * apart, count)
        centered = product[place, :rows] - average
        product[place, :rows] = centered * scale * gain_ref[channel] + bias_ref[channel]
    for token in range(count):
        mixed = product[pl.ds(token, hidden, stride=apart), :][:, :rows].astype(jnp.bfloat16)
        updates[pl.ds(token, rows, stride=apart), :] = lax.dot_general(
            mixed, weights_ref[...], (((0,), (0,)), ((), ())), preferred_element_type=jnp.float32
        )
    step = 16
    for at in range(0, rows, step):
        gate = gate_ref[pl.ds(at, step), pl.ds(first, count)]
        for row in range(step):
            update = updates[pl.ds((at + row) * apart, count), :]
            result[at + row] = (gate[row] * update).astype(jnp.bfloat16)
        if last:
            target = out_ref.at[pl.ds(at, step), pl.ds(first, count)]
            place = sent.at[len(done) + at // step]
            copies.append(pltpu.make_async_copy(result.at[pl.ds(at, step)], target, place))
            copies[-1].start()
    for copy in copies:
        copy.wait()


def band_by_sums(right, spans, window, row_count, col_count, columns):
    blocks_per_row = col_count // row_count
    col_pos = lax.axis_index("col")
    pieces = []
    for offset in range(window):
        block_id = (col_pos - offset) % col_count
        start = block_id % blocks_per_row * columns
        received = from_root(
            lax.dynamic_slice_in_dim(right, start, columns, 0), "row", block_id // blocks_per_row
        )
        pieces.append(received if offset == 0 else shifted(received, "col", -offset))
    bands = [[piece[first : first + count] for piece in pieces] for first, count in spans]
    return bands, [(offset, offset) for offset in range(window)]


def hops():
    near, far, share = [], [], []
    for c in range(4):
        first, second = (c, c), (c, (c + 1) % 4)
        inner, outer = ((2, c), (3, c)) if c < 2 else ((1, c), (0, c))
        near += [(first, (c ^ 1, c)), (second, first)]
        far += [(first, inner), (second, outer)]
        share += [(inner, outer), (outer, inner), (first, (c ^ 1, c))]
    return near, far, share


def hop_place():
    row_pos = lax.axis_index("row")
    near = row_pos ^ lax.axis_index("col")
    inner = (row_pos == 1) | (row_pos == 2)
    return jnp.where(near < 2, near, jnp.where(inner, 2, 3))


def move(array, pairs):
    return lax.ppermute(
        array, ("row", "col"), [(r * 4 + c, to_r * 4 + to_c) for (r, c), (to_r, to_c) in pairs]
    )


def on_device(
    pair_state,
    token_count,
    in_gain,
    in_bias,
    in_weights,
    gate_weights,
    out_gain,
    out_bias,
    out_weights,
):
    rows, columns, channels = pair_state.shape
    hidden = out_weights.shape[0]
    tokens = rows * columns
    col_count = lax.axis_size("col")
    row_count = lax.axis_size("row")
    window = col_count // 2
    depth = window * columns
    width = -(-depth // LANES) * LANES
    in_gain, in_bias = in_gain.reshape(1, channels), in_bias.reshape(1, channels)
    block = 2 * tokens * max(channels, hidden)
    by_hops = row_count == 4 and col_count == 4
    last = 16
    spans = [(0, columns - last), (columns - last, last)]

    if by_hops:
        near, far, share = hops()
        soon = pair_state[: spans[0][1]]
        arrived = [(move(soon, near), move(soon, far))]
    pairs = [pair_state]
    for _ in range(window - 1):
        pairs.append(shifted(pairs[-1], "col", -1))
    left_weights, right_weights = in_weights[:, : 2 * hidden].T, in_weights[:, 2 * hidden :]
    passed = [in_gain, in_bias, right_weights, left_weights, out_weights, pair_state]
    gate, right, *handed = pl.pallas_call(
        functools.partial(own_kernel, len(passed)),
        out_shape=[
            jax.ShapeDtypeStruct((rows, columns, channels), jnp.float32),
            jax.ShapeDtypeStruct((rows, columns, hidden), jnp.bfloat16),
        ]
        + [jax.ShapeDtypeStruct(array.shape, array.dtype) for array in passed],
        in_specs=[SMEM] + [VMEM] * (2 + len(passed)),
        out_specs=[VMEM] * (2 + len(passed)),
        compiler_params=params(6 * block),
        cost_estimate=cost(6 * tokens * channels * hidden, 8 * tokens * channels),
        name="own",
    )(token_count, pair_state, gate_weights, *passed)
    in_gain, in_bias, right_weights, left_weights, out_weights, pairs[0] = handed

    def left_of(here, *base):
        shapes = [jax.ShapeDtypeStruct((hidden, rows, width), jnp.bfloat16)]
        if here[0] == 0:
            shapes.append(jax.ShapeDtypeStruct((spans[1][1], columns, channels), jnp.bfloat16))
        return pl.pallas_call(
            functools.partial(left_kernel, here, window),
            out_shape=shapes,
            in_specs=[SMEM] + [VMEM] * (len(here) + 3 + len(base)),
            out_specs=[VMEM] * len(shapes),
            scratch_shapes=[
                pltpu.VMEM((width // LANES, hidden * pitch(rows), LANES), jnp.float32)
            ],
            compiler_params=params((len(here) + 2) * block, 6 * hidden * rows * width),
            cost_estimate=cost(
                4 * len(here) * tokens * channels * hidden, 6 * rows * width * hidden
            ),
            name="left",
        )(token_count, *[pairs[at] for at in here], in_gain, in_bias, left_weights, *base)

    left, later_pair = left_of([0])
    rest = list(range(1, window))

    def mine_of(first, near_pair, far_pair):
        count = near_pair.shape[0]
        return pl.pallas_call(
            functools.partial(mine_kernel, first),
            out_shape=jax.ShapeDtypeStruct((count, columns, hidden), jnp.bfloat16),
            in_specs=[SMEM] + [VMEM] * 5,
            out_specs=VMEM,
            compiler_params=params(2 * block),
            cost_estimate=cost(4 * count * columns * channels * hidden, 6 * count * columns * channels),
            name="mine",
        )(token_count, near_pair, far_pair, in_gain, in_bias, right_weights)

    if by_hops:
        arrived.append((move(later_pair, near), move(later_pair, far)))
        mine = [mine_of(0, *arrived[0])]
        left, mine[0] = lax.optimization_barrier((left, mine[0]))
        (left,) = left_of(rest, left)
        left, *last = lax.optimization_barrier((left, *arrived[1]))
        mine.append(mine_of(spans[1][0], *last))
        bands = [[right, piece, move(piece, share)] for piece in mine]
        picks, place = [(0, 1, 1, 2), (1, 2, 2, 1)], hop_place
    else:
        (left,) = left_of(rest, left)
        bands, picks = band_by_sums(right, spans, window, row_count, col_count, columns)
        place = lambda: 0

    done = []
    for (first, count), band in zip(spans, bands):
        last = first + count == columns
        scratch = [
            pltpu.VMEM((width // LANES, hidden * pitch(count), LANES), jnp.float32),
            pltpu.VMEM((hidden * pitch(count), LANES), jnp.float32),
            pltpu.VMEM((rows * pitch(count), channels), jnp.float32),
        ]
        if last:
            scratch += [
                pltpu.VMEM((rows, count, channels), jnp.bfloat16),
                pltpu.SemaphoreType.DMA((len(done) + rows // 16,)),
            ]
        filled = pl.pallas_call(
            functools.partial(product_kernel, picks, place, len(band), first, count, last),
            out_shape=jax.ShapeDtypeStruct(
                (rows, columns if last else count, channels), jnp.bfloat16
            ),
            in_specs=[VMEM] * (len(band) + 2) + [SMEM, SMEM, VMEM] + [VMEM] * len(done) * last,
            out_specs=ANY if last else VMEM,
            scratch_shapes=scratch,
            compiler_params=params(2 * block, 2 * hidden * (rows + 2 * count) * width),
            cost_estimate=cost(2 * rows * count * depth * hidden, 4 * rows * depth * hidden),
            name="product",
        )(*band, left, gate, out_gain, out_bias, out_weights, *(done if last else []))
        done.append(filled)
    return filled


def solution(mesh):
    placed = (P(("crops", "row"), "col", None), P("crops"), P(), P(), P(), P(), P(), P(), P())
    return jax.shard_map(
        on_device,
        mesh=mesh,
        in_specs=placed,
        out_specs=P(("crops", "row"), "col", None),
        check_vma=False,
    )
```

```python
import functools

import jax
import jax.numpy as jnp
from jax import lax
from jax.experimental import pallas as pl
from jax.experimental.pallas import tpu as pltpu
from jax.sharding import PartitionSpec as P

LANES = 128
MIB = 1024 * 1024


def params(*sizes):
    return pltpu.CompilerParams(vmem_limit_bytes=min(6 * MIB + 2 * sum(sizes), 56 * MIB))


def cost(flops, bytes_accessed):
    return pl.CostEstimate(flops=flops, bytes_accessed=bytes_accessed, transcendentals=0)


VMEM = pl.BlockSpec(memory_space=pltpu.VMEM)
SMEM = pl.BlockSpec(memory_space=pltpu.SMEM)
ANY = pl.BlockSpec(memory_space=pl.ANY)


def pitch(rows):
    return (rows // 8 | 1) * 8


def shifted(array, axis, by):
    devices = lax.axis_size(axis)
    return lax.ppermute(array, axis, [(i, (i + by) % devices) for i in range(devices)])


def from_root(array, axis, root):
    mine = lax.axis_index(axis) == root
    return lax.psum(jnp.where(mine, array, jnp.zeros_like(array)), axis)


def layer_norm(values, gain, offset):
    average = jnp.mean(values, axis=-1, keepdims=True)
    centered = values - average
    variance = jnp.mean(centered * centered, axis=-1, keepdims=True)
    return centered * lax.rsqrt(variance + 1e-05) * gain + offset


def normed_rows(block, gain_ref, bias_ref):
    rows, columns, channels = block.shape
    values = block.reshape(rows * columns, channels).astype(jnp.float32)
    return layer_norm(values, gain_ref[...], bias_ref[...]).astype(jnp.bfloat16)


def mine_kernel(first, tokens_ref, near_ref, far_ref, gain_ref, bias_ref, weights_ref, out_ref):
    count, columns, _ = out_ref.shape
    col_pos, place = lax.axis_index("col"), hop_place()
    third_block = jnp.where((place == 0) | (place == 3), (col_pos + 1) % 4, col_pos)
    row_token = col_pos * columns + first
    step = 4
    for at in range(0, count, step):
        block = jnp.where(place < 2, near_ref[pl.ds(at, step)], far_ref[pl.ds(at, step)])
        normed = normed_rows(block, gain_ref, bias_ref)
        both = jnp.dot(normed, weights_ref[...], preferred_element_type=jnp.float32)
        parts = masked_right(both, tokens_ref[0], row_token + at, third_block, columns)
        for row, part in enumerate(parts):
            out_ref[at + row] = part


def masked_right(both, tokens, row_token, third_block, columns):
    hidden = both.shape[1] // 2
    right = jax.nn.sigmoid(both[:, :hidden]) * both[:, hidden:]
    position = lax.broadcasted_iota(jnp.int32, (columns, hidden), 0)
    parts = []
    for row in range(both.shape[0] // columns):
        limit = jnp.where(row_token + row < tokens, tokens - third_block * columns, 0)
        part = right[row * columns : (row + 1) * columns]
        parts.append(jnp.where(position < limit, part, 0.0).astype(jnp.bfloat16))
    return parts


def own_kernel(
    tokens_ref, weights_ref, pair_ref, gain_ref, bias_ref, right_ref, left_weights_ref, right_weights_ref, *handed
):
    for source, target in zip((pair_ref, gain_ref, bias_ref), handed):
        target[...] = source[...]
    rows, columns, channels = pair_ref.shape
    hidden = right_ref.shape[2]
    for at in range(0, 2 * hidden, hidden):
        left_weights_ref[pl.ds(at, hidden)] = turned(
            [weights_ref[:, at : at + hidden]], channels
        ).astype(jnp.bfloat16)
    right_weights_ref[...] = weights_ref[:, 2 * hidden :]
    row_start = lax.axis_index("row") * rows
    step = 4
    for first in range(0, rows, step):
        normed = normed_rows(pair_ref[pl.ds(first, step)], gain_ref, bias_ref)
        both = jnp.dot(normed, right_weights_ref[...], preferred_element_type=jnp.float32)
        parts = masked_right(
            both, tokens_ref[0], row_start + first, lax.axis_index("col"), columns
        )
        for row, part in enumerate(parts):
            right_ref[first + row] = part


def left_kernel(here, blocks, tokens_ref, *refs):
    pair_refs, (gain_ref, bias_ref, weights_ref, *refs) = refs[: len(here)], refs[len(here) :]
    base_ref = None
    if here[0] == 0:
        left_ref, later_ref, scratch = refs
        later_ref[...] = pair_refs[0][pl.ds(pair_refs[0].shape[0] - later_ref.shape[0], later_ref.shape[0])]
    else:
        base_ref, own_ref, gate_weights_ref, left_ref, gate_ref, scratch = refs
    rows, columns, channels = pair_refs[0].shape
    hidden, _, width = left_ref.shape
    tokens = tokens_ref[0]
    row_start = lax.axis_index("row") * rows
    col_pos, col_count = lax.axis_index("col"), lax.axis_size("col")
    lane = lax.broadcasted_iota(jnp.int32, (1, width), 1)
    keep = jnp.zeros((1, width), jnp.float32)
    for at in range(blocks):
        end = at * columns + jnp.minimum(tokens - (col_pos + at) % col_count * columns, columns)
        keep += jnp.where((lane >= at * columns) & (lane < end), 1.0, 0.0)
    padding = [jnp.zeros((width - blocks * columns, channels), jnp.bfloat16)]
    if width == blocks * columns:
        padding = []
    step = 4
    for first in range(0, rows, step):
        normed = [normed_rows(ref[pl.ds(first, step)], gain_ref, bias_ref) for ref in pair_refs]
        if base_ref is not None:
            own = normed_rows(own_ref[pl.ds(first, step)], gain_ref, bias_ref)
            gate = jnp.dot(own, gate_weights_ref[...], preferred_element_type=jnp.float32)
            gate_ref[pl.ds(first, step)] = jax.nn.sigmoid(gate).reshape(step, columns, channels)
        for row in range(step):
            thirds = [jnp.zeros((columns, channels), jnp.bfloat16)] * blocks
            for at, piece in zip(here, normed):
                thirds[at] = piece[row * columns : (row + 1) * columns]
            both = lax.dot_general(
                weights_ref[...],
                jnp.concatenate(thirds + padding, axis=0),
                (((1,), (1,)), ((), ())),
                preferred_element_type=jnp.float32,
            )
            left = jax.nn.sigmoid(both[:hidden]) * both[hidden:]
            valid = jnp.where(row_start + first + row < tokens, keep, 0.0)
            left = jnp.where(valid > 0.0, left, 0.0)
            for at in range(0, width, LANES):
                scratch[at // LANES, pl.ds(first + row, hidden, stride=pitch(rows)), :] = left[
                    :, at : at + LANES
                ]
    for channel in range(hidden):
        for at in range(0, width, LANES):
            one = scratch[at // LANES, pl.ds(channel * pitch(rows), rows), :].astype(jnp.bfloat16)
            if base_ref is not None:
                one += base_ref[channel, :, at : at + LANES]
            left_ref[channel, :, at : at + LANES] = one


def turned(pieces, width):
    rows = sum(piece.shape[0] for piece in pieces)
    hidden = pieces[0].shape[1]
    if width > rows:
        pieces = pieces + [jnp.zeros((width - rows, hidden), pieces[0].dtype)]
    row = lax.broadcasted_iota(jnp.int32, (hidden, hidden), 0)
    column = lax.broadcasted_iota(jnp.int32, (hidden, hidden), 1)
    identity = (row == column).astype(jnp.float32).astype(jnp.bfloat16)
    return lax.dot_general(
        identity,
        jnp.concatenate(pieces, axis=0),
        (((1,), (1,)), ((), ())),
        preferred_element_type=jnp.float32,
    )


def product_kernel(picks, place, rights, first, count, last, *refs):
    right_refs, refs = refs[:rights], refs[rights:]
    left_ref, gate_ref, gain_ref, bias_ref, weights_ref, *done, out_ref = refs[: -5 if last else -3]
    right, product, updates = refs[-5:-2] if last else refs[-3:]
    result, sent = refs[-2:] if last else (out_ref, None)
    hidden, rows, width = left_ref.shape
    apart = pitch(count)
    mine = place()

    def row_of(source, token):
        ref = right_refs[source]
        return ref[token if ref.shape[0] == count else first + token]

    copies, start = [], 0
    for at, ref in enumerate(done):
        columns = pl.ds(start, ref.shape[1])
        copies.append(pltpu.make_async_copy(ref, out_ref.at[:, columns], sent.at[at]))
        copies[-1].start()
        start += ref.shape[1]

    for token in range(count):
        pieces = []
        for sources in picks:
            piece = row_of(sources[0], token)
            for at, source in enumerate(sources[1:], 1):
                if source != sources[at - 1]:
                    piece = jnp.where(mine >= at, row_of(source, token), piece)
            pieces.append(piece)
        one = turned(pieces, width)
        for at in range(0, width, LANES):
            right[at // LANES, pl.ds(token, hidden, stride=apart), :] = one[:, at : at + LANES]

    ways = 4
    totals = [jnp.zeros((count, rows), jnp.float32)] * ways
    for channel in range(hidden):
        one = 0.0
        for at in range(0, width, LANES):
            one += lax.dot_general(
                right[at // LANES, pl.ds(channel * apart, count), :].astype(jnp.bfloat16),
                left_ref[channel, :, at : at + LANES],
                (((1,), (1,)), ((), ())),
                preferred_element_type=jnp.float32,
            )
        product[pl.ds(channel * apart, count), :rows] = one
        totals[channel % ways] += one
    average = sum(totals) / hidden
    totals = [jnp.zeros((count, rows), jnp.float32)] * ways
    for channel in range(hidden):
        centered = product[pl.ds(channel * apart, count), :rows] - average
        totals[channel % ways] += centered * centered
    scale = lax.rsqrt(sum(totals) / hidden + 1e-05)
    for channel in range(hidden):
        place = pl.ds(channel * apart, count)
        centered = product[place, :rows] - average
        product[place, :rows] = centered * scale * gain_ref[channel] + bias_ref[channel]
    for token in range(count):
        mixed = product[pl.ds(token, hidden, stride=apart), :][:, :rows].astype(jnp.bfloat16)
        updates[pl.ds(token, rows, stride=apart), :] = lax.dot_general(
            mixed, weights_ref[...], (((0,), (0,)), ((), ())), preferred_element_type=jnp.float32
        )
    step = 16
    for at in range(0, rows, step):
        gate = gate_ref[pl.ds(at, step), pl.ds(first, count)]
        for row in range(step):
            update = updates[pl.ds((at + row) * apart, count), :]
            result[at + row] = (gate[row] * update).astype(jnp.bfloat16)
        if last:
            target = out_ref.at[pl.ds(at, step), pl.ds(first, count)]
            place = sent.at[len(done) + at // step]
            copies.append(pltpu.make_async_copy(result.at[pl.ds(at, step)], target, place))
            copies[-1].start()
    for copy in copies:
        copy.wait()


def band_by_sums(right, spans, window, row_count, col_count, columns):
    blocks_per_row = col_count // row_count
    col_pos = lax.axis_index("col")
    pieces = []
    for offset in range(window):
        block_id = (col_pos - offset) % col_count
        start = block_id % blocks_per_row * columns
        received = from_root(
            lax.dynamic_slice_in_dim(right, start, columns, 0), "row", block_id // blocks_per_row
        )
        pieces.append(received if offset == 0 else shifted(received, "col", -offset))
    bands = [[piece[first : first + count] for piece in pieces] for first, count in spans]
    return bands, [(offset, offset) for offset in range(window)]


def hops():
    near, far, share = [], [], []
    for c in range(4):
        first, second = (c, c), (c, (c + 1) % 4)
        inner, outer = ((2, c), (3, c)) if c < 2 else ((1, c), (0, c))
        near += [(first, (c ^ 1, c)), (second, first)]
        far += [(first, inner), (second, outer)]
        share += [(inner, outer), (outer, inner), (first, (c ^ 1, c))]
    return near, far, share


def hop_place():
    row_pos = lax.axis_index("row")
    near = row_pos ^ lax.axis_index("col")
    inner = (row_pos == 1) | (row_pos == 2)
    return jnp.where(near < 2, near, jnp.where(inner, 2, 3))


def move(array, pairs):
    return lax.ppermute(
        array, ("row", "col"), [(r * 4 + c, to_r * 4 + to_c) for (r, c), (to_r, to_c) in pairs]
    )


def on_device(
    pair_state,
    token_count,
    in_gain,
    in_bias,
    in_weights,
    gate_weights,
    out_gain,
    out_bias,
    out_weights,
):
    rows, columns, channels = pair_state.shape
    hidden = out_weights.shape[0]
    tokens = rows * columns
    col_count = lax.axis_size("col")
    row_count = lax.axis_size("row")
    window = col_count // 2
    depth = window * columns
    width = -(-depth // LANES) * LANES
    in_gain, in_bias = in_gain.reshape(1, channels), in_bias.reshape(1, channels)
    block = 2 * tokens * max(channels, hidden)
    by_hops = row_count == 4 and col_count == 4
    last = 16
    spans = [(0, columns - last), (columns - last, last)]

    if by_hops:
        near, far, share = hops()
        soon = pair_state[: spans[0][1]]
        arrived = [(move(soon, near), move(soon, far))]
    pairs = [pair_state]
    for _ in range(window - 1):
        pairs.append(shifted(pairs[-1], "col", -1))
    copied = [pair_state, in_gain, in_bias]
    right, left_weights, right_weights, pairs[0], in_gain, in_bias = pl.pallas_call(
        own_kernel,
        out_shape=[
            jax.ShapeDtypeStruct((rows, columns, hidden), jnp.bfloat16),
            jax.ShapeDtypeStruct((2 * hidden, channels), jnp.bfloat16),
            jax.ShapeDtypeStruct((channels, 2 * hidden), jnp.bfloat16),
        ]
        + [jax.ShapeDtypeStruct(array.shape, array.dtype) for array in copied],
        in_specs=[SMEM] + [VMEM] * 4,
        out_specs=[VMEM] * 6,
        compiler_params=params(5 * block),
        cost_estimate=cost(6 * tokens * channels * hidden, 8 * tokens * channels),
        name="own",
    )(token_count, in_weights, *copied)

    def left_of(here, *base):
        shapes = [jax.ShapeDtypeStruct((hidden, rows, width), jnp.bfloat16)]
        if here[0] == 0:
            shapes.append(jax.ShapeDtypeStruct((spans[1][1], columns, channels), jnp.bfloat16))
        else:
            shapes.append(jax.ShapeDtypeStruct((rows, columns, channels), jnp.float32))
        return pl.pallas_call(
            functools.partial(left_kernel, here, window),
            out_shape=shapes,
            in_specs=[SMEM] + [VMEM] * (len(here) + 3 + len(base)),
            out_specs=[VMEM] * 2,
            scratch_shapes=[
                pltpu.VMEM((width // LANES, hidden * pitch(rows), LANES), jnp.float32)
            ],
            compiler_params=params((len(here) + 4) * block, 6 * hidden * rows * width),
            cost_estimate=cost(
                4 * len(here) * tokens * channels * hidden, 6 * rows * width * hidden
            ),
            name="left",
        )(token_count, *[pairs[at] for at in here], in_gain, in_bias, left_weights, *base)

    left, later_pair = left_of([0])
    rest = list(range(1, window))

    def mine_of(first, near_pair, far_pair):
        count = near_pair.shape[0]
        return pl.pallas_call(
            functools.partial(mine_kernel, first),
            out_shape=jax.ShapeDtypeStruct((count, columns, hidden), jnp.bfloat16),
            in_specs=[SMEM] + [VMEM] * 5,
            out_specs=VMEM,
            compiler_params=params(2 * block),
            cost_estimate=cost(4 * count * columns * channels * hidden, 6 * count * columns * channels),
            name="mine",
        )(token_count, near_pair, far_pair, in_gain, in_bias, right_weights)

    if by_hops:
        arrived.append((move(later_pair, near), move(later_pair, far)))
        mine = [mine_of(0, *arrived[0])]
        left, mine[0] = lax.optimization_barrier((left, mine[0]))
        left, gate = left_of(rest, left, pairs[0], gate_weights)
        left, *last = lax.optimization_barrier((left, *arrived[1]))
        mine.append(mine_of(spans[1][0], *last))
        bands = [[right, piece, move(piece, share)] for piece in mine]
        picks, place = [(0, 1, 1, 2), (1, 2, 2, 1)], hop_place
    else:
        left, gate = left_of(rest, left, pairs[0], gate_weights)
        bands, picks = band_by_sums(right, spans, window, row_count, col_count, columns)
        place = lambda: 0

    done = []
    for (first, count), band in zip(spans, bands):
        last = first + count == columns
        scratch = [
            pltpu.VMEM((width // LANES, hidden * pitch(count), LANES), jnp.float32),
            pltpu.VMEM((hidden * pitch(count), LANES), jnp.float32),
            pltpu.VMEM((rows * pitch(count), channels), jnp.float32),
        ]
        if last:
            scratch += [
                pltpu.VMEM((rows, count, channels), jnp.bfloat16),
                pltpu.SemaphoreType.DMA((len(done) + rows // 16,)),
            ]
        filled = pl.pallas_call(
            functools.partial(product_kernel, picks, place, len(band), first, count, last),
            out_shape=jax.ShapeDtypeStruct(
                (rows, columns if last else count, channels), jnp.bfloat16
            ),
            in_specs=[VMEM] * (len(band) + 2) + [SMEM, SMEM, VMEM] + [VMEM] * len(done) * last,
            out_specs=ANY if last else VMEM,
            scratch_shapes=scratch,
            compiler_params=params(2 * block, 2 * hidden * (rows + 2 * count) * width),
            cost_estimate=cost(2 * rows * count * depth * hidden, 4 * rows * depth * hidden),
            name="product",
        )(*band, left, gate, out_gain, out_bias, out_weights, *(done if last else []))
        done.append(filled)
    return filled


def solution(mesh):
    placed = (P(("crops", "row"), "col", None), P("crops"), P(), P(), P(), P(), P(), P(), P())
    return jax.shard_map(
        on_device,
        mesh=mesh,
        in_specs=placed,
        out_specs=P(("crops", "row"), "col", None),
        check_vma=False,
    )
```

```python
import functools

import jax
import jax.numpy as jnp
from jax import lax
from jax.experimental import pallas as pl
from jax.experimental.pallas import tpu as pltpu
from jax.sharding import PartitionSpec as P

LANES = 128
MIB = 1024 * 1024


def params(*sizes):
    return pltpu.CompilerParams(vmem_limit_bytes=min(6 * MIB + 2 * sum(sizes), 56 * MIB))


def cost(flops, bytes_accessed):
    return pl.CostEstimate(flops=flops, bytes_accessed=bytes_accessed, transcendentals=0)


VMEM = pl.BlockSpec(memory_space=pltpu.VMEM)
SMEM = pl.BlockSpec(memory_space=pltpu.SMEM)
ANY = pl.BlockSpec(memory_space=pl.ANY)


def pitch(rows):
    return (rows // 8 | 1) * 8


def shifted(array, axis, by):
    devices = lax.axis_size(axis)
    return lax.ppermute(array, axis, [(i, (i + by) % devices) for i in range(devices)])


def from_root(array, axis, root):
    mine = lax.axis_index(axis) == root
    return lax.psum(jnp.where(mine, array, jnp.zeros_like(array)), axis)


def layer_norm(values, gain, offset):
    average = jnp.mean(values, axis=-1, keepdims=True)
    centered = values - average
    variance = jnp.mean(centered * centered, axis=-1, keepdims=True)
    return centered * lax.rsqrt(variance + 1e-05) * gain + offset


def normed_rows(block, gain_ref, bias_ref):
    rows, columns, channels = block.shape
    values = block.reshape(rows * columns, channels).astype(jnp.float32)
    return layer_norm(values, gain_ref[...], bias_ref[...]).astype(jnp.bfloat16)


def mine_kernel(first, tokens_ref, near_ref, far_ref, gain_ref, bias_ref, weights_ref, *refs):
    out_ref = refs[-1]
    if len(refs) > 1:
        own_ref, out_ref, later_ref = refs
        later_ref[...] = own_ref[pl.ds(out_ref.shape[0], later_ref.shape[0])]
    count, columns, _ = out_ref.shape
    col_pos, place = lax.axis_index("col"), hop_place()
    third_block = jnp.where((place == 0) | (place == 3), (col_pos + 1) % 4, col_pos)
    row_token = col_pos * columns + first
    step = 4
    for at in range(0, count, step):
        block = jnp.where(place < 2, near_ref[pl.ds(at, step)], far_ref[pl.ds(at, step)])
        normed = normed_rows(block, gain_ref, bias_ref)
        both = jnp.dot(normed, weights_ref[...], preferred_element_type=jnp.float32)
        parts = masked_right(both, tokens_ref[0], row_token + at, third_block, columns)
        for row, part in enumerate(parts):
            out_ref[at + row] = part


def masked_right(both, tokens, row_token, third_block, columns):
    hidden = both.shape[1] // 2
    right = jax.nn.sigmoid(both[:, :hidden]) * both[:, hidden:]
    position = lax.broadcasted_iota(jnp.int32, (columns, hidden), 0)
    parts = []
    for row in range(both.shape[0] // columns):
        limit = jnp.where(row_token + row < tokens, tokens - third_block * columns, 0)
        part = right[row * columns : (row + 1) * columns]
        parts.append(jnp.where(position < limit, part, 0.0).astype(jnp.bfloat16))
    return parts


def own_kernel(
    tokens_ref, weights_ref, pair_ref, gain_ref, bias_ref, right_ref, left_weights_ref, right_weights_ref, *handed
):
    for source, target in zip((pair_ref, gain_ref, bias_ref), handed):
        target[...] = source[...]
    rows, columns, channels = pair_ref.shape
    hidden = right_ref.shape[2]
    for at in range(0, 2 * hidden, hidden):
        left_weights_ref[pl.ds(at, hidden)] = turned(
            [weights_ref[:, at : at + hidden]], channels
        ).astype(jnp.bfloat16)
    right_weights_ref[...] = weights_ref[:, 2 * hidden :]
    row_start = lax.axis_index("row") * rows
    step = 4
    for first in range(0, rows, step):
        normed = normed_rows(pair_ref[pl.ds(first, step)], gain_ref, bias_ref)
        both = jnp.dot(normed, right_weights_ref[...], preferred_element_type=jnp.float32)
        parts = masked_right(
            both, tokens_ref[0], row_start + first, lax.axis_index("col"), columns
        )
        for row, part in enumerate(parts):
            right_ref[first + row] = part


def left_kernel(here, blocks, tokens_ref, *refs):
    pair_refs, (gain_ref, bias_ref, weights_ref, *refs) = refs[: len(here)], refs[len(here) :]
    base_ref = None
    if here[0] == 0:
        left_ref, scratch = refs
    else:
        base_ref, own_ref, gate_weights_ref, left_ref, gate_ref, scratch = refs
    rows, columns, channels = pair_refs[0].shape
    hidden, _, width = left_ref.shape
    tokens = tokens_ref[0]
    row_start = lax.axis_index("row") * rows
    col_pos, col_count = lax.axis_index("col"), lax.axis_size("col")
    lane = lax.broadcasted_iota(jnp.int32, (1, width), 1)
    keep = jnp.zeros((1, width), jnp.float32)
    for at in range(blocks):
        end = at * columns + jnp.minimum(tokens - (col_pos + at) % col_count * columns, columns)
        keep += jnp.where((lane >= at * columns) & (lane < end), 1.0, 0.0)
    padding = [jnp.zeros((width - blocks * columns, channels), jnp.bfloat16)]
    if width == blocks * columns:
        padding = []
    step = 4
    for first in range(0, rows, step):
        normed = [normed_rows(ref[pl.ds(first, step)], gain_ref, bias_ref) for ref in pair_refs]
        if base_ref is not None:
            own = normed_rows(own_ref[pl.ds(first, step)], gain_ref, bias_ref)
            gate = jnp.dot(own, gate_weights_ref[...], preferred_element_type=jnp.float32)
            gate_ref[pl.ds(first, step)] = jax.nn.sigmoid(gate).reshape(step, columns, channels)
        for row in range(step):
            thirds = [jnp.zeros((columns, channels), jnp.bfloat16)] * blocks
            for at, piece in zip(here, normed):
                thirds[at] = piece[row * columns : (row + 1) * columns]
            both = lax.dot_general(
                weights_ref[...],
                jnp.concatenate(thirds + padding, axis=0),
                (((1,), (1,)), ((), ())),
                preferred_element_type=jnp.float32,
            )
            left = jax.nn.sigmoid(both[:hidden]) * both[hidden:]
            valid = jnp.where(row_start + first + row < tokens, keep, 0.0)
            left = jnp.where(valid > 0.0, left, 0.0)
            for at in range(0, width, LANES):
                scratch[at // LANES, pl.ds(first + row, hidden, stride=pitch(rows)), :] = left[
                    :, at : at + LANES
                ]
    for channel in range(hidden):
        for at in range(0, width, LANES):
            one = scratch[at // LANES, pl.ds(channel * pitch(rows), rows), :].astype(jnp.bfloat16)
            if base_ref is not None:
                one += base_ref[channel, :, at : at + LANES]
            left_ref[channel, :, at : at + LANES] = one


def turned(pieces, width):
    rows = sum(piece.shape[0] for piece in pieces)
    hidden = pieces[0].shape[1]
    if width > rows:
        pieces = pieces + [jnp.zeros((width - rows, hidden), pieces[0].dtype)]
    row = lax.broadcasted_iota(jnp.int32, (hidden, hidden), 0)
    column = lax.broadcasted_iota(jnp.int32, (hidden, hidden), 1)
    identity = (row == column).astype(jnp.float32).astype(jnp.bfloat16)
    return lax.dot_general(
        identity,
        jnp.concatenate(pieces, axis=0),
        (((1,), (1,)), ((), ())),
        preferred_element_type=jnp.float32,
    )


def product_kernel(picks, place, rights, first, count, last, *refs):
    right_refs, refs = refs[:rights], refs[rights:]
    left_ref, gate_ref, gain_ref, bias_ref, weights_ref, *done, out_ref = refs[: -5 if last else -3]
    right, product, updates = refs[-5:-2] if last else refs[-3:]
    result, sent = refs[-2:] if last else (out_ref, None)
    hidden, rows, width = left_ref.shape
    apart = pitch(count)
    mine = place()

    def row_of(source, token):
        ref = right_refs[source]
        return ref[token if ref.shape[0] == count else first + token]

    copies, start = [], 0
    for at, ref in enumerate(done):
        columns = pl.ds(start, ref.shape[1])
        copies.append(pltpu.make_async_copy(ref, out_ref.at[:, columns], sent.at[at]))
        copies[-1].start()
        start += ref.shape[1]

    for token in range(count):
        pieces = []
        for sources in picks:
            piece = row_of(sources[0], token)
            for at, source in enumerate(sources[1:], 1):
                if source != sources[at - 1]:
                    piece = jnp.where(mine >= at, row_of(source, token), piece)
            pieces.append(piece)
        one = turned(pieces, width)
        for at in range(0, width, LANES):
            right[at // LANES, pl.ds(token, hidden, stride=apart), :] = one[:, at : at + LANES]

    ways = 4
    totals = [jnp.zeros((count, rows), jnp.float32)] * ways
    for channel in range(hidden):
        one = 0.0
        for at in range(0, width, LANES):
            one += lax.dot_general(
                right[at // LANES, pl.ds(channel * apart, count), :].astype(jnp.bfloat16),
                left_ref[channel, :, at : at + LANES],
                (((1,), (1,)), ((), ())),
                preferred_element_type=jnp.float32,
            )
        product[pl.ds(channel * apart, count), :rows] = one
        totals[channel % ways] += one
    average = sum(totals) / hidden
    totals = [jnp.zeros((count, rows), jnp.float32)] * ways
    for channel in range(hidden):
        centered = product[pl.ds(channel * apart, count), :rows] - average
        totals[channel % ways] += centered * centered
    scale = lax.rsqrt(sum(totals) / hidden + 1e-05)
    for channel in range(hidden):
        place = pl.ds(channel * apart, count)
        centered = product[place, :rows] - average
        product[place, :rows] = centered * scale * gain_ref[channel] + bias_ref[channel]
    for token in range(count):
        mixed = product[pl.ds(token, hidden, stride=apart), :][:, :rows].astype(jnp.bfloat16)
        updates[pl.ds(token, rows, stride=apart), :] = lax.dot_general(
            mixed, weights_ref[...], (((0,), (0,)), ((), ())), preferred_element_type=jnp.float32
        )
    step = 16
    for at in range(0, rows, step):
        gate = gate_ref[pl.ds(at, step), pl.ds(first, count)]
        for row in range(step):
            update = updates[pl.ds((at + row) * apart, count), :]
            result[at + row] = (gate[row] * update).astype(jnp.bfloat16)
        if last:
            target = out_ref.at[pl.ds(at, step), pl.ds(first, count)]
            place = sent.at[len(done) + at // step]
            copies.append(pltpu.make_async_copy(result.at[pl.ds(at, step)], target, place))
            copies[-1].start()
    for copy in copies:
        copy.wait()


def band_by_sums(right, spans, window, row_count, col_count, columns):
    blocks_per_row = col_count // row_count
    col_pos = lax.axis_index("col")
    pieces = []
    for offset in range(window):
        block_id = (col_pos - offset) % col_count
        start = block_id % blocks_per_row * columns
        received = from_root(
            lax.dynamic_slice_in_dim(right, start, columns, 0), "row", block_id // blocks_per_row
        )
        pieces.append(received if offset == 0 else shifted(received, "col", -offset))
    bands = [[piece[first : first + count] for piece in pieces] for first, count in spans]
    return bands, [(offset, offset) for offset in range(window)]


def hops():
    near, far, share = [], [], []
    for c in range(4):
        first, second = (c, c), (c, (c + 1) % 4)
        inner, outer = ((2, c), (3, c)) if c < 2 else ((1, c), (0, c))
        near += [(first, (c ^ 1, c)), (second, first)]
        far += [(first, inner), (second, outer)]
        share += [(inner, outer), (outer, inner), (first, (c ^ 1, c))]
    return near, far, share


def hop_place():
    row_pos = lax.axis_index("row")
    near = row_pos ^ lax.axis_index("col")
    inner = (row_pos == 1) | (row_pos == 2)
    return jnp.where(near < 2, near, jnp.where(inner, 2, 3))


def move(array, pairs):
    return lax.ppermute(
        array, ("row", "col"), [(r * 4 + c, to_r * 4 + to_c) for (r, c), (to_r, to_c) in pairs]
    )


def on_device(
    pair_state,
    token_count,
    in_gain,
    in_bias,
    in_weights,
    gate_weights,
    out_gain,
    out_bias,
    out_weights,
):
    rows, columns, channels = pair_state.shape
    hidden = out_weights.shape[0]
    tokens = rows * columns
    col_count = lax.axis_size("col")
    row_count = lax.axis_size("row")
    window = col_count // 2
    depth = window * columns
    width = -(-depth // LANES) * LANES
    in_gain, in_bias = in_gain.reshape(1, channels), in_bias.reshape(1, channels)
    block = 2 * tokens * max(channels, hidden)
    by_hops = row_count == 4 and col_count == 4
    last = 16
    spans = [(0, columns - last), (columns - last, last)]

    if by_hops:
        near, far, share = hops()
        soon = pair_state[: spans[0][1]]
        arrived = move(soon, near), move(soon, far)
    pairs = [pair_state]
    for _ in range(window - 1):
        pairs.append(shifted(pairs[-1], "col", -1))
    copied = [pair_state, in_gain, in_bias]
    right, left_weights, right_weights, pairs[0], in_gain, in_bias = pl.pallas_call(
        own_kernel,
        out_shape=[
            jax.ShapeDtypeStruct((rows, columns, hidden), jnp.bfloat16),
            jax.ShapeDtypeStruct((2 * hidden, channels), jnp.bfloat16),
            jax.ShapeDtypeStruct((channels, 2 * hidden), jnp.bfloat16),
        ]
        + [jax.ShapeDtypeStruct(array.shape, array.dtype) for array in copied],
        in_specs=[SMEM] + [VMEM] * 4,
        out_specs=[VMEM] * 6,
        compiler_params=params(5 * block),
        cost_estimate=cost(6 * tokens * channels * hidden, 8 * tokens * channels),
        name="own",
    )(token_count, in_weights, *copied)

    def left_of(here, *base):
        shapes = [jax.ShapeDtypeStruct((hidden, rows, width), jnp.bfloat16)]
        if here[0] > 0:
            shapes.append(jax.ShapeDtypeStruct((rows, columns, channels), jnp.float32))
        return pl.pallas_call(
            functools.partial(left_kernel, here, window),
            out_shape=shapes,
            in_specs=[SMEM] + [VMEM] * (len(here) + 3 + len(base)),
            out_specs=[VMEM] * len(shapes),
            scratch_shapes=[
                pltpu.VMEM((width // LANES, hidden * pitch(rows), LANES), jnp.float32)
            ],
            compiler_params=params((len(here) + 4) * block, 6 * hidden * rows * width),
            cost_estimate=cost(
                4 * len(here) * tokens * channels * hidden, 6 * rows * width * hidden
            ),
            name="left",
        )(token_count, *[pairs[at] for at in here], in_gain, in_bias, left_weights, *base)

    (left,) = left_of([0])
    rest = list(range(1, window))

    def mine_of(first, near_pair, far_pair, *own):
        shapes = [jax.ShapeDtypeStruct(near_pair.shape, jnp.bfloat16)]
        if own:
            shapes.append(jax.ShapeDtypeStruct((spans[1][1], columns, channels), jnp.bfloat16))
        count = near_pair.shape[0]
        return pl.pallas_call(
            functools.partial(mine_kernel, first),
            out_shape=shapes,
            in_specs=[SMEM] + [VMEM] * (5 + len(own)),
            out_specs=[VMEM] * len(shapes),
            compiler_params=params(2 * block),
            cost_estimate=cost(4 * count * columns * channels * hidden, 6 * count * columns * channels),
            name="mine",
        )(token_count, near_pair, far_pair, in_gain, in_bias, right_weights, *own)

    if by_hops:
        left, *arrived = lax.optimization_barrier((left, *arrived))
        mine, later = mine_of(0, *arrived, pairs[0])
        arrived = move(later, near), move(later, far)
        left, mine = lax.optimization_barrier((left, mine))
        left, gate = left_of(rest, left, pairs[0], gate_weights)
        left, *arrived = lax.optimization_barrier((left, *arrived))
        mine = [mine, *mine_of(spans[1][0], *arrived)]
        bands = [[right, piece, move(piece, share)] for piece in mine]
        picks, place = [(0, 1, 1, 2), (1, 2, 2, 1)], hop_place
    else:
        left, gate = left_of(rest, left, pairs[0], gate_weights)
        bands, picks = band_by_sums(right, spans, window, row_count, col_count, columns)
        place = lambda: 0

    done = []
    for (first, count), band in zip(spans, bands):
        last = first + count == columns
        scratch = [
            pltpu.VMEM((width // LANES, hidden * pitch(count), LANES), jnp.float32),
            pltpu.VMEM((hidden * pitch(count), LANES), jnp.float32),
            pltpu.VMEM((rows * pitch(count), channels), jnp.float32),
        ]
        if last:
            scratch += [
                pltpu.VMEM((rows, count, channels), jnp.bfloat16),
                pltpu.SemaphoreType.DMA((len(done) + rows // 16,)),
            ]
        filled = pl.pallas_call(
            functools.partial(product_kernel, picks, place, len(band), first, count, last),
            out_shape=jax.ShapeDtypeStruct(
                (rows, columns if last else count, channels), jnp.bfloat16
            ),
            in_specs=[VMEM] * (len(band) + 2) + [SMEM, SMEM, VMEM] + [VMEM] * len(done) * last,
            out_specs=ANY if last else VMEM,
            scratch_shapes=scratch,
            compiler_params=params(2 * block, 2 * hidden * (rows + 2 * count) * width),
            cost_estimate=cost(2 * rows * count * depth * hidden, 4 * rows * depth * hidden),
            name="product",
        )(*band, left, gate, out_gain, out_bias, out_weights, *(done if last else []))
        done.append(filled)
    return filled


def solution(mesh):
    placed = (P(("crops", "row"), "col", None), P("crops"), P(), P(), P(), P(), P(), P(), P())
    return jax.shard_map(
        on_device,
        mesh=mesh,
        in_specs=placed,
        out_specs=P(("crops", "row"), "col", None),
        check_vma=False,
    )
```

```python
import functools

import jax
import jax.numpy as jnp
from jax import lax
from jax.experimental import pallas as pl
from jax.experimental.pallas import tpu as pltpu
from jax.sharding import PartitionSpec as P

LANES = 128
MIB = 1024 * 1024


def params(*sizes):
    return pltpu.CompilerParams(vmem_limit_bytes=min(6 * MIB + 2 * sum(sizes), 56 * MIB))


def cost(flops, bytes_accessed):
    return pl.CostEstimate(flops=flops, bytes_accessed=bytes_accessed, transcendentals=0)


VMEM = pl.BlockSpec(memory_space=pltpu.VMEM)
SMEM = pl.BlockSpec(memory_space=pltpu.SMEM)
ANY = pl.BlockSpec(memory_space=pl.ANY)


def pitch(rows):
    return (rows // 8 | 1) * 8


def shifted(array, axis, by):
    devices = lax.axis_size(axis)
    return lax.ppermute(array, axis, [(i, (i + by) % devices) for i in range(devices)])


def from_root(array, axis, root):
    mine = lax.axis_index(axis) == root
    return lax.psum(jnp.where(mine, array, jnp.zeros_like(array)), axis)


def layer_norm(values, gain, offset):
    average = jnp.mean(values, axis=-1, keepdims=True)
    centered = values - average
    variance = jnp.mean(centered * centered, axis=-1, keepdims=True)
    return centered * lax.rsqrt(variance + 1e-05) * gain + offset


def normed_rows(block, gain_ref, bias_ref):
    rows, columns, channels = block.shape
    values = block.reshape(rows * columns, channels).astype(jnp.float32)
    return layer_norm(values, gain_ref[...], bias_ref[...]).astype(jnp.bfloat16)


def mine_kernel(first, tokens_ref, near_ref, far_ref, gain_ref, bias_ref, weights_ref, *refs):
    out_ref = refs[-1]
    if len(refs) > 1:
        own_ref, out_ref, later_ref = refs
        later_ref[...] = own_ref[pl.ds(out_ref.shape[0], later_ref.shape[0])]
    count, columns, _ = out_ref.shape
    col_pos, place = lax.axis_index("col"), hop_place()
    third_block = jnp.where((place == 0) | (place == 3), (col_pos + 1) % 4, col_pos)
    row_token = col_pos * columns + first
    step = 4
    for at in range(0, count, step):
        block = jnp.where(place < 2, near_ref[pl.ds(at, step)], far_ref[pl.ds(at, step)])
        normed = normed_rows(block, gain_ref, bias_ref)
        both = jnp.dot(normed, weights_ref[...], preferred_element_type=jnp.float32)
        parts = masked_right(both, tokens_ref[0], row_token + at, third_block, columns)
        for row, part in enumerate(parts):
            out_ref[at + row] = part


def masked_right(both, tokens, row_token, third_block, columns):
    hidden = both.shape[1] // 2
    right = jax.nn.sigmoid(both[:, :hidden]) * both[:, hidden:]
    position = lax.broadcasted_iota(jnp.int32, (columns, hidden), 0)
    parts = []
    for row in range(both.shape[0] // columns):
        limit = jnp.where(row_token + row < tokens, tokens - third_block * columns, 0)
        part = right[row * columns : (row + 1) * columns]
        parts.append(jnp.where(position < limit, part, 0.0).astype(jnp.bfloat16))
    return parts


def own_kernel(
    tokens_ref, weights_ref, pair_ref, gain_ref, bias_ref, right_ref, left_weights_ref, right_weights_ref, *handed
):
    for source, target in zip((pair_ref, gain_ref, bias_ref), handed):
        target[...] = source[...]
    rows, columns, channels = pair_ref.shape
    hidden = right_ref.shape[2]
    for at in range(0, 2 * hidden, hidden):
        left_weights_ref[pl.ds(at, hidden)] = turned(
            [weights_ref[:, at : at + hidden]], channels
        ).astype(jnp.bfloat16)
    right_weights_ref[...] = weights_ref[:, 2 * hidden :]
    row_start = lax.axis_index("row") * rows
    step = 4
    for first in range(0, rows, step):
        normed = normed_rows(pair_ref[pl.ds(first, step)], gain_ref, bias_ref)
        both = jnp.dot(normed, right_weights_ref[...], preferred_element_type=jnp.float32)
        parts = masked_right(
            both, tokens_ref[0], row_start + first, lax.axis_index("col"), columns
        )
        for row, part in enumerate(parts):
            right_ref[first + row] = part


def left_kernel(here, blocks, tokens_ref, *refs):
    pair_refs, (gain_ref, bias_ref, weights_ref, *refs) = refs[: len(here)], refs[len(here) :]
    base_ref = None
    if here[0] == 0:
        left_ref, scratch = refs
    else:
        base_ref, own_ref, gate_weights_ref, left_ref, gate_ref, scratch = refs
    rows, columns, channels = pair_refs[0].shape
    hidden, _, width = left_ref.shape
    tokens = tokens_ref[0]
    row_start = lax.axis_index("row") * rows
    col_pos, col_count = lax.axis_index("col"), lax.axis_size("col")
    lane = lax.broadcasted_iota(jnp.int32, (1, width), 1)
    keep = jnp.zeros((1, width), jnp.float32)
    for at in range(blocks):
        end = at * columns + jnp.minimum(tokens - (col_pos + at) % col_count * columns, columns)
        keep += jnp.where((lane >= at * columns) & (lane < end), 1.0, 0.0)
    padding = [jnp.zeros((width - blocks * columns, channels), jnp.bfloat16)]
    if width == blocks * columns:
        padding = []
    step = 4
    for first in range(0, rows, step):
        normed = [normed_rows(ref[pl.ds(first, step)], gain_ref, bias_ref) for ref in pair_refs]
        if base_ref is not None:
            own = normed_rows(own_ref[pl.ds(first, step)], gain_ref, bias_ref)
            gate = jnp.dot(own, gate_weights_ref[...], preferred_element_type=jnp.float32)
            gate_ref[pl.ds(first, step)] = jax.nn.sigmoid(gate).reshape(step, columns, channels)
        for row in range(step):
            thirds = [jnp.zeros((columns, channels), jnp.bfloat16)] * blocks
            for at, piece in zip(here, normed):
                thirds[at] = piece[row * columns : (row + 1) * columns]
            both = lax.dot_general(
                weights_ref[...],
                jnp.concatenate(thirds + padding, axis=0),
                (((1,), (1,)), ((), ())),
                preferred_element_type=jnp.float32,
            )
            left = jax.nn.sigmoid(both[:hidden]) * both[hidden:]
            valid = jnp.where(row_start + first + row < tokens, keep, 0.0)
            left = jnp.where(valid > 0.0, left, 0.0)
            for at in range(0, width, LANES):
                scratch[at // LANES, pl.ds(first + row, hidden, stride=pitch(rows)), :] = left[
                    :, at : at + LANES
                ]
    for channel in range(hidden):
        for at in range(0, width, LANES):
            one = scratch[at // LANES, pl.ds(channel * pitch(rows), rows), :].astype(jnp.bfloat16)
            if base_ref is not None:
                one += base_ref[channel, :, at : at + LANES]
            left_ref[channel, :, at : at + LANES] = one


def turned(pieces, width):
    rows = sum(piece.shape[0] for piece in pieces)
    hidden = pieces[0].shape[1]
    if width > rows:
        pieces = pieces + [jnp.zeros((width - rows, hidden), pieces[0].dtype)]
    row = lax.broadcasted_iota(jnp.int32, (hidden, hidden), 0)
    column = lax.broadcasted_iota(jnp.int32, (hidden, hidden), 1)
    identity = (row == column).astype(jnp.float32).astype(jnp.bfloat16)
    return lax.dot_general(
        identity,
        jnp.concatenate(pieces, axis=0),
        (((1,), (1,)), ((), ())),
        preferred_element_type=jnp.float32,
    )


def product_kernel(picks, place, rights, first, count, last, *refs):
    right_refs, refs = refs[:rights], refs[rights:]
    left_ref, gate_ref, gain_ref, bias_ref, weights_ref, *done, out_ref = refs[: -5 if last else -3]
    right, product, updates = refs[-5:-2] if last else refs[-3:]
    result, sent = refs[-2:] if last else (out_ref, None)
    hidden, rows, width = left_ref.shape
    apart = pitch(count)
    mine = place()

    def row_of(source, token):
        ref = right_refs[source]
        return ref[token if ref.shape[0] == count else first + token]

    copies, start = [], 0
    for at, ref in enumerate(done):
        columns = pl.ds(start, ref.shape[1])
        copies.append(pltpu.make_async_copy(ref, out_ref.at[:, columns], sent.at[at]))
        copies[-1].start()
        start += ref.shape[1]

    for token in range(count):
        pieces = []
        for sources in picks:
            piece = row_of(sources[0], token)
            for at, source in enumerate(sources[1:], 1):
                if source != sources[at - 1]:
                    piece = jnp.where(mine >= at, row_of(source, token), piece)
            pieces.append(piece)
        one = turned(pieces, width)
        for at in range(0, width, LANES):
            right[at // LANES, pl.ds(token, hidden, stride=apart), :] = one[:, at : at + LANES]

    ways = 4
    totals = [jnp.zeros((count, rows), jnp.float32)] * ways
    for channel in range(hidden):
        one = 0.0
        for at in range(0, width, LANES):
            one += lax.dot_general(
                right[at // LANES, pl.ds(channel * apart, count), :].astype(jnp.bfloat16),
                left_ref[channel, :, at : at + LANES],
                (((1,), (1,)), ((), ())),
                preferred_element_type=jnp.float32,
            )
        product[pl.ds(channel * apart, count), :rows] = one
        totals[channel % ways] += one
    average = sum(totals) / hidden
    totals = [jnp.zeros((count, rows), jnp.float32)] * ways
    for channel in range(hidden):
        centered = product[pl.ds(channel * apart, count), :rows] - average
        totals[channel % ways] += centered * centered
    scale = lax.rsqrt(sum(totals) / hidden + 1e-05)
    for channel in range(hidden):
        place = pl.ds(channel * apart, count)
        centered = product[place, :rows] - average
        product[place, :rows] = centered * scale * gain_ref[channel] + bias_ref[channel]
    for token in range(count):
        mixed = product[pl.ds(token, hidden, stride=apart), :][:, :rows].astype(jnp.bfloat16)
        updates[pl.ds(token, rows, stride=apart), :] = lax.dot_general(
            mixed, weights_ref[...], (((0,), (0,)), ((), ())), preferred_element_type=jnp.float32
        )
    step = 16
    for at in range(0, rows, step):
        gate = gate_ref[pl.ds(at, step), pl.ds(first, count)]
        for row in range(step):
            update = updates[pl.ds((at + row) * apart, count), :]
            result[at + row] = (gate[row] * update).astype(jnp.bfloat16)
        if last:
            target = out_ref.at[pl.ds(at, step), pl.ds(first, count)]
            place = sent.at[len(done) + at // step]
            copies.append(pltpu.make_async_copy(result.at[pl.ds(at, step)], target, place))
            copies[-1].start()
    for copy in copies:
        copy.wait()


def band_by_sums(right, spans, window, row_count, col_count, columns):
    blocks_per_row = col_count // row_count
    col_pos = lax.axis_index("col")
    pieces = []
    for offset in range(window):
        block_id = (col_pos - offset) % col_count
        start = block_id % blocks_per_row * columns
        received = from_root(
            lax.dynamic_slice_in_dim(right, start, columns, 0), "row", block_id // blocks_per_row
        )
        pieces.append(received if offset == 0 else shifted(received, "col", -offset))
    bands = [[piece[first : first + count] for piece in pieces] for first, count in spans]
    return bands, [(offset, offset) for offset in range(window)]


def hops():
    near, far, share = [], [], []
    for c in range(4):
        first, second = (c, c), (c, (c + 1) % 4)
        inner, outer = ((2, c), (3, c)) if c < 2 else ((1, c), (0, c))
        near += [(first, (c ^ 1, c)), (second, first)]
        far += [(first, inner), (second, outer)]
        share += [(inner, outer), (outer, inner), (first, (c ^ 1, c))]
    return near, far, share


def hop_place():
    row_pos = lax.axis_index("row")
    near = row_pos ^ lax.axis_index("col")
    inner = (row_pos == 1) | (row_pos == 2)
    return jnp.where(near < 2, near, jnp.where(inner, 2, 3))


def move(array, pairs):
    return lax.ppermute(
        array, ("row", "col"), [(r * 4 + c, to_r * 4 + to_c) for (r, c), (to_r, to_c) in pairs]
    )


def on_device(
    pair_state,
    token_count,
    in_gain,
    in_bias,
    in_weights,
    gate_weights,
    out_gain,
    out_bias,
    out_weights,
):
    rows, columns, channels = pair_state.shape
    hidden = out_weights.shape[0]
    tokens = rows * columns
    col_count = lax.axis_size("col")
    row_count = lax.axis_size("row")
    window = col_count // 2
    depth = window * columns
    width = -(-depth // LANES) * LANES
    in_gain, in_bias = in_gain.reshape(1, channels), in_bias.reshape(1, channels)
    block = 2 * tokens * max(channels, hidden)
    by_hops = row_count == 4 and col_count == 4
    last = 16
    spans = [(0, columns - last), (columns - last, last)]

    if by_hops:
        near, far, share = hops()
        soon = pair_state[: spans[0][1]]
        arrived = move(soon, near), move(soon, far)
    pairs = [pair_state]
    for _ in range(window - 1):
        pairs.append(shifted(pairs[-1], "col", -1))
    copied = [pair_state, in_gain, in_bias]
    right, left_weights, right_weights, pairs[0], in_gain, in_bias = pl.pallas_call(
        own_kernel,
        out_shape=[
            jax.ShapeDtypeStruct((rows, columns, hidden), jnp.bfloat16),
            jax.ShapeDtypeStruct((2 * hidden, channels), jnp.bfloat16),
            jax.ShapeDtypeStruct((channels, 2 * hidden), jnp.bfloat16),
        ]
        + [jax.ShapeDtypeStruct(array.shape, array.dtype) for array in copied],
        in_specs=[SMEM] + [VMEM] * 4,
        out_specs=[VMEM] * 6,
        compiler_params=params(5 * block),
        cost_estimate=cost(6 * tokens * channels * hidden, 8 * tokens * channels),
        name="own",
    )(token_count, in_weights, *copied)

    def left_of(here, *base):
        shapes = [jax.ShapeDtypeStruct((hidden, rows, width), jnp.bfloat16)]
        if here[0] > 0:
            shapes.append(jax.ShapeDtypeStruct((rows, columns, channels), jnp.float32))
        return pl.pallas_call(
            functools.partial(left_kernel, here, window),
            out_shape=shapes,
            in_specs=[SMEM] + [VMEM] * (len(here) + 3 + len(base)),
            out_specs=[VMEM] * len(shapes),
            scratch_shapes=[
                pltpu.VMEM((width // LANES, hidden * pitch(rows), LANES), jnp.float32)
            ],
            compiler_params=params((len(here) + 4) * block, 6 * hidden * rows * width),
            cost_estimate=cost(
                4 * len(here) * tokens * channels * hidden, 6 * rows * width * hidden
            ),
            name="left",
        )(token_count, *[pairs[at] for at in here], in_gain, in_bias, left_weights, *base)

    (left,) = left_of([0])
    rest = list(range(1, window))

    def mine_of(first, near_pair, far_pair, *own):
        shapes = [jax.ShapeDtypeStruct(near_pair.shape, jnp.bfloat16)]
        if own:
            shapes.append(jax.ShapeDtypeStruct((spans[1][1], columns, channels), jnp.bfloat16))
        count = near_pair.shape[0]
        return pl.pallas_call(
            functools.partial(mine_kernel, first),
            out_shape=shapes,
            in_specs=[SMEM] + [VMEM] * (5 + len(own)),
            out_specs=[VMEM] * len(shapes),
            compiler_params=params(2 * block),
            cost_estimate=cost(1024, 1024),
            name="mine",
        )(token_count, near_pair, far_pair, in_gain, in_bias, right_weights, *own)

    if by_hops:
        left, *arrived = lax.optimization_barrier((left, *arrived))
        mine, later = mine_of(0, *arrived, pairs[0])
        arrived = move(later, near), move(later, far)
        left, mine = lax.optimization_barrier((left, mine))
        left, gate = left_of(rest, left, pairs[0], gate_weights)
        left, *arrived = lax.optimization_barrier((left, *arrived))
        mine = [mine, *mine_of(spans[1][0], *arrived)]
        bands = [[right, piece, move(piece, share)] for piece in mine]
        picks, place = [(0, 1, 1, 2), (1, 2, 2, 1)], hop_place
    else:
        left, gate = left_of(rest, left, pairs[0], gate_weights)
        bands, picks = band_by_sums(right, spans, window, row_count, col_count, columns)
        place = lambda: 0

    done = []
    for (first, count), band in zip(spans, bands):
        last = first + count == columns
        scratch = [
            pltpu.VMEM((width // LANES, hidden * pitch(count), LANES), jnp.float32),
            pltpu.VMEM((hidden * pitch(count), LANES), jnp.float32),
            pltpu.VMEM((rows * pitch(count), channels), jnp.float32),
        ]
        if last:
            scratch += [
                pltpu.VMEM((rows, count, channels), jnp.bfloat16),
                pltpu.SemaphoreType.DMA((len(done) + rows // 16,)),
            ]
        filled = pl.pallas_call(
            functools.partial(product_kernel, picks, place, len(band), first, count, last),
            out_shape=jax.ShapeDtypeStruct(
                (rows, columns if last else count, channels), jnp.bfloat16
            ),
            in_specs=[VMEM] * (len(band) + 2) + [SMEM, SMEM, VMEM] + [VMEM] * len(done) * last,
            out_specs=ANY if last else VMEM,
            scratch_shapes=scratch,
            compiler_params=params(2 * block, 2 * hidden * (rows + 2 * count) * width),
            cost_estimate=cost(2 * rows * count * depth * hidden, 4 * rows * depth * hidden),
            name="product",
        )(*band, left, gate, out_gain, out_bias, out_weights, *(done if last else []))
        done.append(filled)
    return filled


def solution(mesh):
    placed = (P(("crops", "row"), "col", None), P("crops"), P(), P(), P(), P(), P(), P(), P())
    return jax.shard_map(
        on_device,
        mesh=mesh,
        in_specs=placed,
        out_specs=P(("crops", "row"), "col", None),
        check_vma=False,
    )
```

```python
import functools

import jax
import jax.numpy as jnp
from jax import lax
from jax.experimental import pallas as pl
from jax.experimental.pallas import tpu as pltpu
from jax.sharding import PartitionSpec as P

LANES = 128
MIB = 1024 * 1024


def params(*sizes):
    return pltpu.CompilerParams(vmem_limit_bytes=min(6 * MIB + 2 * sum(sizes), 56 * MIB))


def cost(flops, bytes_accessed):
    return pl.CostEstimate(flops=flops, bytes_accessed=bytes_accessed, transcendentals=0)


VMEM = pl.BlockSpec(memory_space=pltpu.VMEM)
SMEM = pl.BlockSpec(memory_space=pltpu.SMEM)
ANY = pl.BlockSpec(memory_space=pl.ANY)


def pitch(rows):
    return (rows // 8 | 1) * 8


def shifted(array, axis, by):
    devices = lax.axis_size(axis)
    return lax.ppermute(array, axis, [(i, (i + by) % devices) for i in range(devices)])


def from_root(array, axis, root):
    mine = lax.axis_index(axis) == root
    return lax.psum(jnp.where(mine, array, jnp.zeros_like(array)), axis)


def layer_norm(values, gain, offset):
    average = jnp.mean(values, axis=-1, keepdims=True)
    centered = values - average
    variance = jnp.mean(centered * centered, axis=-1, keepdims=True)
    return centered * lax.rsqrt(variance + 1e-05) * gain + offset


def normed_rows(block, gain_ref, bias_ref):
    rows, columns, channels = block.shape
    values = block.reshape(rows * columns, channels).astype(jnp.float32)
    return layer_norm(values, gain_ref[...], bias_ref[...]).astype(jnp.bfloat16)


def mine_kernel(first, tokens_ref, near_ref, far_ref, gain_ref, bias_ref, weights_ref, out_ref):
    count, columns, _ = out_ref.shape
    col_pos, place = lax.axis_index("col"), hop_place()
    third_block = jnp.where((place == 0) | (place == 3), (col_pos + 1) % 4, col_pos)
    row_token = col_pos * columns + first
    step = 4
    for at in range(0, count, step):
        block = jnp.where(place < 2, near_ref[pl.ds(at, step)], far_ref[pl.ds(at, step)])
        normed = normed_rows(block, gain_ref, bias_ref)
        both = jnp.dot(normed, weights_ref[...], preferred_element_type=jnp.float32)
        parts = masked_right(both, tokens_ref[0], row_token + at, third_block, columns)
        for row, part in enumerate(parts):
            out_ref[at + row] = part


def masked_right(both, tokens, row_token, third_block, columns):
    hidden = both.shape[1] // 2
    right = jax.nn.sigmoid(both[:, :hidden]) * both[:, hidden:]
    position = lax.broadcasted_iota(jnp.int32, (columns, hidden), 0)
    parts = []
    for row in range(both.shape[0] // columns):
        limit = jnp.where(row_token + row < tokens, tokens - third_block * columns, 0)
        part = right[row * columns : (row + 1) * columns]
        parts.append(jnp.where(position < limit, part, 0.0).astype(jnp.bfloat16))
    return parts


def own_kernel(passes, tokens_ref, pair_ref, gate_weights_ref, *refs):
    passed, (gate_ref, right_ref), handed = refs[:passes], refs[passes : passes + 2], refs[passes + 2 :]
    gain_ref, bias_ref, right_weights_ref = passed[:3]
    for source, target in zip(passed, handed):
        target[...] = source[...]
    rows, columns, channels = pair_ref.shape
    row_start = lax.axis_index("row") * rows
    step = 4
    for first in range(0, rows, step):
        normed = normed_rows(pair_ref[pl.ds(first, step)], gain_ref, bias_ref)
        gate = jnp.dot(normed, gate_weights_ref[...], preferred_element_type=jnp.float32)
        gate_ref[pl.ds(first, step)] = jax.nn.sigmoid(gate).reshape(step, columns, channels)
        both = jnp.dot(normed, right_weights_ref[...], preferred_element_type=jnp.float32)
        parts = masked_right(
            both, tokens_ref[0], row_start + first, lax.axis_index("col"), columns
        )
        for row, part in enumerate(parts):
            right_ref[first + row] = part


def left_kernel(here, blocks, tokens_ref, *refs):
    pair_refs, refs = refs[: len(here)], refs[len(here) :]
    gain_ref, bias_ref, weights_ref, *base_refs, left_ref, scratch = refs
    if here[0] == 0:
        *base_refs, left_ref, later_ref = (*base_refs, left_ref)
        later_ref[...] = pair_refs[0][pl.ds(pair_refs[0].shape[0] - later_ref.shape[0], later_ref.shape[0])]
    rows, columns, channels = pair_refs[0].shape
    hidden, _, width = left_ref.shape
    tokens = tokens_ref[0]
    row_start = lax.axis_index("row") * rows
    col_pos, col_count = lax.axis_index("col"), lax.axis_size("col")
    lane = lax.broadcasted_iota(jnp.int32, (1, width), 1)
    keep = jnp.zeros((1, width), jnp.float32)
    for at in range(blocks):
        end = at * columns + jnp.minimum(tokens - (col_pos + at) % col_count * columns, columns)
        keep += jnp.where((lane >= at * columns) & (lane < end), 1.0, 0.0)
    padding = [jnp.zeros((width - blocks * columns, channels), jnp.bfloat16)]
    if width == blocks * columns:
        padding = []
    step = 4
    for first in range(0, rows, step):
        normed = [normed_rows(ref[pl.ds(first, step)], gain_ref, bias_ref) for ref in pair_refs]
        for row in range(step):
            thirds = [jnp.zeros((columns, channels), jnp.bfloat16)] * blocks
            for at, piece in zip(here, normed):
                thirds[at] = piece[row * columns : (row + 1) * columns]
            both = lax.dot_general(
                weights_ref[...],
                jnp.concatenate(thirds + padding, axis=0),
                (((1,), (1,)), ((), ())),
                preferred_element_type=jnp.float32,
            )
            left = jax.nn.sigmoid(both[:hidden]) * both[hidden:]
            valid = jnp.where(row_start + first + row < tokens, keep, 0.0)
            left = jnp.where(valid > 0.0, left, 0.0)
            for at in range(0, width, LANES):
                scratch[at // LANES, pl.ds(first + row, hidden, stride=pitch(rows)), :] = left[
                    :, at : at + LANES
                ]
    for channel in range(hidden):
        for at in range(0, width, LANES):
            one = scratch[at // LANES, pl.ds(channel * pitch(rows), rows), :].astype(jnp.bfloat16)
            for base_ref in base_refs:
                one += base_ref[channel, :, at : at + LANES]
            left_ref[channel, :, at : at + LANES] = one


def turned(pieces, width):
    rows = sum(piece.shape[0] for piece in pieces)
    hidden = pieces[0].shape[1]
    if width > rows:
        pieces = pieces + [jnp.zeros((width - rows, hidden), pieces[0].dtype)]
    row = lax.broadcasted_iota(jnp.int32, (hidden, hidden), 0)
    column = lax.broadcasted_iota(jnp.int32, (hidden, hidden), 1)
    identity = (row == column).astype(jnp.float32).astype(jnp.bfloat16)
    return lax.dot_general(
        identity,
        jnp.concatenate(pieces, axis=0),
        (((1,), (1,)), ((), ())),
        preferred_element_type=jnp.float32,
    )


def product_kernel(picks, place, rights, first, count, last, *refs):
    right_refs, refs = refs[:rights], refs[rights:]
    left_ref, gate_ref, gain_ref, bias_ref, weights_ref, *done, out_ref = refs[: -5 if last else -3]
    right, product, updates = refs[-5:-2] if last else refs[-3:]
    result, sent = refs[-2:] if last else (out_ref, None)
    hidden, rows, width = left_ref.shape
    apart = pitch(count)
    mine = place()

    def row_of(source, token):
        ref = right_refs[source]
        return ref[token if ref.shape[0] == count else first + token]

    copies, start = [], 0
    for at, ref in enumerate(done):
        columns = pl.ds(start, ref.shape[1])
        copies.append(pltpu.make_async_copy(ref, out_ref.at[:, columns], sent.at[at]))
        copies[-1].start()
        start += ref.shape[1]

    for token in range(count):
        pieces = []
        for sources in picks:
            piece = row_of(sources[0], token)
            for at, source in enumerate(sources[1:], 1):
                if source != sources[at - 1]:
                    piece = jnp.where(mine >= at, row_of(source, token), piece)
            pieces.append(piece)
        one = turned(pieces, width)
        for at in range(0, width, LANES):
            right[at // LANES, pl.ds(token, hidden, stride=apart), :] = one[:, at : at + LANES]

    ways = 4
    totals = [jnp.zeros((count, rows), jnp.float32)] * ways
    for channel in range(hidden):
        one = 0.0
        for at in range(0, width, LANES):
            one += lax.dot_general(
                right[at // LANES, pl.ds(channel * apart, count), :].astype(jnp.bfloat16),
                left_ref[channel, :, at : at + LANES],
                (((1,), (1,)), ((), ())),
                preferred_element_type=jnp.float32,
            )
        product[pl.ds(channel * apart, count), :rows] = one
        totals[channel % ways] += one
    average = sum(totals) / hidden
    totals = [jnp.zeros((count, rows), jnp.float32)] * ways
    for channel in range(hidden):
        centered = product[pl.ds(channel * apart, count), :rows] - average
        totals[channel % ways] += centered * centered
    scale = lax.rsqrt(sum(totals) / hidden + 1e-05)
    gain, bias = (
        jnp.broadcast_to(ref[...], (LANES, hidden)).T[:, :rows] for ref in (gain_ref, bias_ref)
    )
    for token in range(count):
        values = product[pl.ds(token, hidden, stride=apart), :][:, :rows]
        centered = values - average[token : token + 1]
        mixed = (centered * scale[token : token + 1] * gain + bias).astype(jnp.bfloat16)
        updates[pl.ds(token, rows, stride=apart), :] = lax.dot_general(
            mixed, weights_ref[...], (((0,), (0,)), ((), ())), preferred_element_type=jnp.float32
        )
    step = 16
    for at in range(0, rows, step):
        gate = gate_ref[pl.ds(at, step), pl.ds(first, count)]
        for row in range(step):
            update = updates[pl.ds((at + row) * apart, count), :]
            result[at + row] = (gate[row] * update).astype(jnp.bfloat16)
        if last:
            target = out_ref.at[pl.ds(at, step), pl.ds(first, count)]
            place = sent.at[len(done) + at // step]
            copies.append(pltpu.make_async_copy(result.at[pl.ds(at, step)], target, place))
            copies[-1].start()
    for copy in copies:
        copy.wait()


def band_by_sums(right, spans, window, row_count, col_count, columns):
    blocks_per_row = col_count // row_count
    col_pos = lax.axis_index("col")
    pieces = []
    for offset in range(window):
        block_id = (col_pos - offset) % col_count
        start = block_id % blocks_per_row * columns
        received = from_root(
            lax.dynamic_slice_in_dim(right, start, columns, 0), "row", block_id // blocks_per_row
        )
        pieces.append(received if offset == 0 else shifted(received, "col", -offset))
    bands = [[piece[first : first + count] for piece in pieces] for first, count in spans]
    return bands, [(offset, offset) for offset in range(window)]


def hops():
    near, far, share = [], [], []
    for c in range(4):
        first, second = (c, c), (c, (c + 1) % 4)
        inner, outer = ((2, c), (3, c)) if c < 2 else ((1, c), (0, c))
        near += [(first, (c ^ 1, c)), (second, first)]
        far += [(first, inner), (second, outer)]
        share += [(inner, outer), (outer, inner), (first, (c ^ 1, c))]
    return near, far, share


def hop_place():
    row_pos = lax.axis_index("row")
    near = row_pos ^ lax.axis_index("col")
    inner = (row_pos == 1) | (row_pos == 2)
    return jnp.where(near < 2, near, jnp.where(inner, 2, 3))


def move(array, pairs):
    return lax.ppermute(
        array, ("row", "col"), [(r * 4 + c, to_r * 4 + to_c) for (r, c), (to_r, to_c) in pairs]
    )


def on_device(
    pair_state,
    token_count,
    in_gain,
    in_bias,
    in_weights,
    gate_weights,
    out_gain,
    out_bias,
    out_weights,
):
    rows, columns, channels = pair_state.shape
    hidden = out_weights.shape[0]
    tokens = rows * columns
    col_count = lax.axis_size("col")
    row_count = lax.axis_size("row")
    window = col_count // 2
    depth = window * columns
    width = -(-depth // LANES) * LANES
    in_gain, in_bias = in_gain.reshape(1, channels), in_bias.reshape(1, channels)
    out_gain, out_bias = out_gain.reshape(1, hidden), out_bias.reshape(1, hidden)
    block = 2 * tokens * max(channels, hidden)
    by_hops = row_count == 4 and col_count == 4
    last = 16
    spans = [(0, columns - last), (columns - last, last)]

    if by_hops:
        near, far, share = hops()
        soon = pair_state[: spans[0][1]]
        arrived = [(move(soon, near), move(soon, far))]
    pairs = [pair_state]
    for _ in range(window - 1):
        pairs.append(shifted(pairs[-1], "col", -1))
    left_weights, right_weights = in_weights[:, : 2 * hidden].T, in_weights[:, 2 * hidden :]
    passed = [in_gain, in_bias, right_weights, left_weights, out_weights, pair_state]
    gate, right, *handed = pl.pallas_call(
        functools.partial(own_kernel, len(passed)),
        out_shape=[
            jax.ShapeDtypeStruct((rows, columns, channels), jnp.float32),
            jax.ShapeDtypeStruct((rows, columns, hidden), jnp.bfloat16),
        ]
        + [jax.ShapeDtypeStruct(array.shape, array.dtype) for array in passed],
        in_specs=[SMEM] + [VMEM] * (2 + len(passed)),
        out_specs=[VMEM] * (2 + len(passed)),
        compiler_params=params(6 * block),
        cost_estimate=cost(6 * tokens * channels * hidden, 8 * tokens * channels),
        name="own",
    )(token_count, pair_state, gate_weights, *passed)
    in_gain, in_bias, right_weights, left_weights, out_weights, pairs[0] = handed

    def left_of(here, *base):
        shapes = [jax.ShapeDtypeStruct((hidden, rows, width), jnp.bfloat16)]
        if here[0] == 0:
            shapes.append(jax.ShapeDtypeStruct((spans[1][1], columns, channels), jnp.bfloat16))
        return pl.pallas_call(
            functools.partial(left_kernel, here, window),
            out_shape=shapes,
            in_specs=[SMEM] + [VMEM] * (len(here) + 3 + len(base)),
            out_specs=[VMEM] * len(shapes),
            scratch_shapes=[
                pltpu.VMEM((width // LANES, hidden * pitch(rows), LANES), jnp.float32)
            ],
            compiler_params=params((len(here) + 2) * block, 6 * hidden * rows * width),
            cost_estimate=cost(
                4 * len(here) * tokens * channels * hidden, 6 * rows * width * hidden
            ),
            name="left",
        )(token_count, *[pairs[at] for at in here], in_gain, in_bias, left_weights, *base)

    left, later_pair = left_of([0])
    rest = list(range(1, window))

    def mine_of(first, near_pair, far_pair):
        count = near_pair.shape[0]
        return pl.pallas_call(
            functools.partial(mine_kernel, first),
            out_shape=jax.ShapeDtypeStruct((count, columns, hidden), jnp.bfloat16),
            in_specs=[SMEM] + [VMEM] * 5,
            out_specs=VMEM,
            compiler_params=params(2 * block),
            cost_estimate=cost(4 * count * columns * channels * hidden, 6 * count * columns * channels),
            name="mine",
        )(token_count, near_pair, far_pair, in_gain, in_bias, right_weights)

    if by_hops:
        arrived.append((move(later_pair, near), move(later_pair, far)))
        mine = [mine_of(0, *arrived[0])]
        left, mine[0] = lax.optimization_barrier((left, mine[0]))
        (left,) = left_of(rest, left)
        left, *last = lax.optimization_barrier((left, *arrived[1]))
        mine.append(mine_of(spans[1][0], *last))
        bands = [[right, piece, move(piece, share)] for piece in mine]
        picks, place = [(0, 1, 1, 2), (1, 2, 2, 1)], hop_place
    else:
        (left,) = left_of(rest, left)
        bands, picks = band_by_sums(right, spans, window, row_count, col_count, columns)
        place = lambda: 0

    done = []
    for (first, count), band in zip(spans, bands):
        last = first + count == columns
        scratch = [
            pltpu.VMEM((width // LANES, hidden * pitch(count), LANES), jnp.float32),
            pltpu.VMEM((hidden * pitch(count), LANES), jnp.float32),
            pltpu.VMEM((rows * pitch(count), channels), jnp.float32),
        ]
        if last:
            scratch += [
                pltpu.VMEM((rows, count, channels), jnp.bfloat16),
                pltpu.SemaphoreType.DMA((len(done) + rows // 16,)),
            ]
        filled = pl.pallas_call(
            functools.partial(product_kernel, picks, place, len(band), first, count, last),
            out_shape=jax.ShapeDtypeStruct(
                (rows, columns if last else count, channels), jnp.bfloat16
            ),
            in_specs=[VMEM] * (len(band) + 2) + [VMEM] * (3 + len(done) * last),
            out_specs=ANY if last else VMEM,
            scratch_shapes=scratch,
            compiler_params=params(2 * block, 2 * hidden * (rows + 2 * count) * width),
            cost_estimate=cost(2 * rows * count * depth * hidden, 4 * rows * depth * hidden),
            name="product",
        )(*band, left, gate, out_gain, out_bias, out_weights, *(done if last else []))
        done.append(filled)
    return filled


def solution(mesh):
    placed = (P(("crops", "row"), "col", None), P("crops"), P(), P(), P(), P(), P(), P(), P())
    return jax.shard_map(
        on_device,
        mesh=mesh,
        in_specs=placed,
        out_specs=P(("crops", "row"), "col", None),
        check_vma=False,
    )
```

```python
import functools

import jax
import jax.numpy as jnp
from jax import lax
from jax.experimental import pallas as pl
from jax.experimental.pallas import tpu as pltpu
from jax.sharding import PartitionSpec as P

LANES = 128
MIB = 1024 * 1024


def params(*sizes):
    return pltpu.CompilerParams(vmem_limit_bytes=min(6 * MIB + 2 * sum(sizes), 56 * MIB))


def cost(flops, bytes_accessed):
    return pl.CostEstimate(flops=flops, bytes_accessed=bytes_accessed, transcendentals=0)


VMEM = pl.BlockSpec(memory_space=pltpu.VMEM)
SMEM = pl.BlockSpec(memory_space=pltpu.SMEM)
ANY = pl.BlockSpec(memory_space=pl.ANY)


def pitch(rows):
    return (rows // 8 | 1) * 8


def shifted(array, axis, by):
    devices = lax.axis_size(axis)
    return lax.ppermute(array, axis, [(i, (i + by) % devices) for i in range(devices)])


def from_root(array, axis, root):
    mine = lax.axis_index(axis) == root
    return lax.psum(jnp.where(mine, array, jnp.zeros_like(array)), axis)


def layer_norm(values, gain, offset):
    average = jnp.mean(values, axis=-1, keepdims=True)
    centered = values - average
    variance = jnp.mean(centered * centered, axis=-1, keepdims=True)
    return centered * lax.rsqrt(variance + 1e-05) * gain + offset


def normed_rows(block, gain_ref, bias_ref):
    rows, columns, channels = block.shape
    values = block.reshape(rows * columns, channels).astype(jnp.float32)
    return layer_norm(values, gain_ref[...], bias_ref[...]).astype(jnp.bfloat16)


def mine_kernel(first, tokens_ref, far_ref, near_ref, gain_ref, bias_ref, weights_ref, out_ref):
    count, columns, _ = out_ref.shape
    col_pos, place = lax.axis_index("col"), hop_place()
    third_block = jnp.where((place == 0) | (place == 3), (col_pos + 1) % 4, col_pos)
    row_token = col_pos * columns + first
    step = 4
    for at in range(0, count, step):
        block = jnp.where(place < 2, near_ref[pl.ds(at, step)], far_ref[pl.ds(at, step)])
        normed = normed_rows(block, gain_ref, bias_ref)
        both = jnp.dot(normed, weights_ref[...], preferred_element_type=jnp.float32)
        parts = masked_right(both, tokens_ref[0], row_token + at, third_block, columns)
        for row, part in enumerate(parts):
            out_ref[at + row] = part


def masked_right(both, tokens, row_token, third_block, columns):
    hidden = both.shape[1] // 2
    right = jax.nn.sigmoid(both[:, :hidden]) * both[:, hidden:]
    position = lax.broadcasted_iota(jnp.int32, (columns, hidden), 0)
    parts = []
    for row in range(both.shape[0] // columns):
        limit = jnp.where(row_token + row < tokens, tokens - third_block * columns, 0)
        part = right[row * columns : (row + 1) * columns]
        parts.append(jnp.where(position < limit, part, 0.0).astype(jnp.bfloat16))
    return parts


def own_kernel(passes, tokens_ref, pair_ref, gate_weights_ref, *refs):
    passed, (gate_ref, right_ref, later_ref), handed = (
        refs[:passes],
        refs[passes : passes + 3],
        refs[passes + 3 :],
    )
    later_ref[...] = pair_ref[pl.ds(pair_ref.shape[0] - later_ref.shape[0], later_ref.shape[0])]
    gain_ref, bias_ref, right_weights_ref = passed[:3]
    for source, target in zip(passed, handed):
        target[...] = source[...]
    rows, columns, channels = pair_ref.shape
    row_start = lax.axis_index("row") * rows
    step = 4
    for first in range(0, rows, step):
        normed = normed_rows(pair_ref[pl.ds(first, step)], gain_ref, bias_ref)
        gate = jnp.dot(normed, gate_weights_ref[...], preferred_element_type=jnp.float32)
        gate_ref[pl.ds(first, step)] = jax.nn.sigmoid(gate).reshape(step, columns, channels)
        both = jnp.dot(normed, right_weights_ref[...], preferred_element_type=jnp.float32)
        parts = masked_right(
            both, tokens_ref[0], row_start + first, lax.axis_index("col"), columns
        )
        for row, part in enumerate(parts):
            right_ref[first + row] = part


def left_kernel(blocks, tokens_ref, *refs):
    pair_refs, (gain_ref, bias_ref, weights_ref, left_ref, scratch) = refs[:blocks], refs[blocks:]
    rows, columns, channels = pair_refs[0].shape
    hidden, _, width = left_ref.shape
    tokens = tokens_ref[0]
    row_start = lax.axis_index("row") * rows
    col_pos, col_count = lax.axis_index("col"), lax.axis_size("col")
    lane = lax.broadcasted_iota(jnp.int32, (1, width), 1)
    keep = jnp.zeros((1, width), jnp.float32)
    for at in range(blocks):
        end = at * columns + jnp.minimum(tokens - (col_pos + at) % col_count * columns, columns)
        keep += jnp.where((lane >= at * columns) & (lane < end), 1.0, 0.0)
    padding = [jnp.zeros((width - blocks * columns, channels), jnp.bfloat16)]
    if width == blocks * columns:
        padding = []
    step = 4
    for first in range(0, rows, step):
        normed = [normed_rows(ref[pl.ds(first, step)], gain_ref, bias_ref) for ref in pair_refs]
        for row in range(step):
            thirds = [piece[row * columns : (row + 1) * columns] for piece in normed]
            both = lax.dot_general(
                weights_ref[...],
                jnp.concatenate(thirds + padding, axis=0),
                (((1,), (1,)), ((), ())),
                preferred_element_type=jnp.float32,
            )
            left = jax.nn.sigmoid(both[:hidden]) * both[hidden:]
            valid = jnp.where(row_start + first + row < tokens, keep, 0.0)
            left = jnp.where(valid > 0.0, left, 0.0)
            for at in range(0, width, LANES):
                scratch[at // LANES, pl.ds(first + row, hidden, stride=pitch(rows)), :] = left[
                    :, at : at + LANES
                ]
    for channel in range(hidden):
        for at in range(0, width, LANES):
            one = scratch[at // LANES, pl.ds(channel * pitch(rows), rows), :].astype(jnp.bfloat16)
            left_ref[channel, :, at : at + LANES] = one


def turned(pieces, width):
    rows = sum(piece.shape[0] for piece in pieces)
    hidden = pieces[0].shape[1]
    if width > rows:
        pieces = pieces + [jnp.zeros((width - rows, hidden), pieces[0].dtype)]
    row = lax.broadcasted_iota(jnp.int32, (hidden, hidden), 0)
    column = lax.broadcasted_iota(jnp.int32, (hidden, hidden), 1)
    identity = (row == column).astype(jnp.float32).astype(jnp.bfloat16)
    return lax.dot_general(
        identity,
        jnp.concatenate(pieces, axis=0),
        (((1,), (1,)), ((), ())),
        preferred_element_type=jnp.float32,
    )


def product_kernel(picks, place, rights, first, count, last, *refs):
    right_refs, refs = refs[:rights], refs[rights:]
    left_ref, gate_ref, gain_ref, bias_ref, weights_ref, *done, out_ref = refs[: -5 if last else -3]
    right, product, updates = refs[-5:-2] if last else refs[-3:]
    result, sent = refs[-2:] if last else (out_ref, None)
    hidden, rows, width = left_ref.shape
    apart = pitch(count)
    mine = place()

    def row_of(source, token):
        ref = right_refs[source]
        return ref[token if ref.shape[0] == count else first + token]

    copies, start = [], 0
    for at, ref in enumerate(done):
        columns = pl.ds(start, ref.shape[1])
        copies.append(pltpu.make_async_copy(ref, out_ref.at[:, columns], sent.at[at]))
        copies[-1].start()
        start += ref.shape[1]

    for token in range(count):
        pieces = []
        for sources in picks:
            piece = row_of(sources[0], token)
            for at, source in enumerate(sources[1:], 1):
                if source != sources[at - 1]:
                    piece = jnp.where(mine >= at, row_of(source, token), piece)
            pieces.append(piece)
        one = turned(pieces, width)
        for at in range(0, width, LANES):
            right[at // LANES, pl.ds(token, hidden, stride=apart), :] = one[:, at : at + LANES]

    ways = 4
    totals = [jnp.zeros((count, rows), jnp.float32)] * ways
    for channel in range(hidden):
        one = 0.0
        for at in range(0, width, LANES):
            one += lax.dot_general(
                right[at // LANES, pl.ds(channel * apart, count), :].astype(jnp.bfloat16),
                left_ref[channel, :, at : at + LANES],
                (((1,), (1,)), ((), ())),
                preferred_element_type=jnp.float32,
            )
        product[pl.ds(channel * apart, count), :rows] = one
        totals[channel % ways] += one
    average = sum(totals) / hidden
    totals = [jnp.zeros((count, rows), jnp.float32)] * ways
    for channel in range(hidden):
        centered = product[pl.ds(channel * apart, count), :rows] - average
        totals[channel % ways] += centered * centered
    scale = lax.rsqrt(sum(totals) / hidden + 1e-05)
    gain, bias = (
        jnp.broadcast_to(ref[...], (LANES, hidden)).T[:, :rows] for ref in (gain_ref, bias_ref)
    )
    for token in range(count):
        values = product[pl.ds(token, hidden, stride=apart), :][:, :rows]
        centered = values - average[token : token + 1]
        mixed = (centered * scale[token : token + 1] * gain + bias).astype(jnp.bfloat16)
        updates[pl.ds(token, rows, stride=apart), :] = lax.dot_general(
            mixed, weights_ref[...], (((0,), (0,)), ((), ())), preferred_element_type=jnp.float32
        )
    step = 16
    for at in range(0, rows, step):
        gate = gate_ref[pl.ds(at, step), pl.ds(first, count)]
        for row in range(step):
            update = updates[pl.ds((at + row) * apart, count), :]
            result[at + row] = (gate[row] * update).astype(jnp.bfloat16)
        if last:
            target = out_ref.at[pl.ds(at, step), pl.ds(first, count)]
            place = sent.at[len(done) + at // step]
            copies.append(pltpu.make_async_copy(result.at[pl.ds(at, step)], target, place))
            copies[-1].start()
    for copy in copies:
        copy.wait()


def band_by_sums(right, spans, window, row_count, col_count, columns):
    blocks_per_row = col_count // row_count
    col_pos = lax.axis_index("col")
    pieces = []
    for offset in range(window):
        block_id = (col_pos - offset) % col_count
        start = block_id % blocks_per_row * columns
        received = from_root(
            lax.dynamic_slice_in_dim(right, start, columns, 0), "row", block_id // blocks_per_row
        )
        pieces.append(received if offset == 0 else shifted(received, "col", -offset))
    bands = [[piece[first : first + count] for piece in pieces] for first, count in spans]
    return bands, [(offset, offset) for offset in range(window)]


def hops():
    near, far, share = [], [], []
    for c in range(4):
        first, second = (c, c), (c, (c + 1) % 4)
        inner, outer = ((2, c), (3, c)) if c < 2 else ((1, c), (0, c))
        near += [(first, (c ^ 1, c)), (second, first)]
        far += [(first, inner), (second, outer)]
        share += [(inner, outer), (outer, inner), (first, (c ^ 1, c))]
    return near, far, share


def hop_place():
    row_pos = lax.axis_index("row")
    near = row_pos ^ lax.axis_index("col")
    inner = (row_pos == 1) | (row_pos == 2)
    return jnp.where(near < 2, near, jnp.where(inner, 2, 3))


def move(array, pairs):
    return lax.ppermute(
        array, ("row", "col"), [(r * 4 + c, to_r * 4 + to_c) for (r, c), (to_r, to_c) in pairs]
    )


def on_device(
    pair_state,
    token_count,
    in_gain,
    in_bias,
    in_weights,
    gate_weights,
    out_gain,
    out_bias,
    out_weights,
):
    rows, columns, channels = pair_state.shape
    hidden = out_weights.shape[0]
    tokens = rows * columns
    col_count = lax.axis_size("col")
    row_count = lax.axis_size("row")
    window = col_count // 2
    depth = window * columns
    width = -(-depth // LANES) * LANES
    in_gain, in_bias = in_gain.reshape(1, channels), in_bias.reshape(1, channels)
    out_gain, out_bias = out_gain.reshape(1, hidden), out_bias.reshape(1, hidden)
    block = 2 * tokens * max(channels, hidden)
    by_hops = row_count == 4 and col_count == 4
    last = 16
    spans = [(0, columns - last), (columns - last, last)]

    if by_hops:
        near, far, share = hops()
        soon = pair_state[: spans[0][1]]
        arrived = [(move(soon, far), move(soon, near))]
    pairs = [pair_state]
    for _ in range(window - 1):
        pairs.append(shifted(pairs[-1], "col", -1))
    left_weights, right_weights = in_weights[:, : 2 * hidden].T, in_weights[:, 2 * hidden :]
    passed = [in_gain, in_bias, right_weights, left_weights, out_weights, pair_state]
    gate, right, later, *handed = pl.pallas_call(
        functools.partial(own_kernel, len(passed)),
        out_shape=[
            jax.ShapeDtypeStruct((rows, columns, channels), jnp.float32),
            jax.ShapeDtypeStruct((rows, columns, hidden), jnp.bfloat16),
            jax.ShapeDtypeStruct((spans[1][1], columns, channels), jnp.bfloat16),
        ]
        + [jax.ShapeDtypeStruct(array.shape, array.dtype) for array in passed],
        in_specs=[SMEM] + [VMEM] * (2 + len(passed)),
        out_specs=[VMEM] * (3 + len(passed)),
        compiler_params=params(6 * block),
        cost_estimate=cost(6 * tokens * channels * hidden, 8 * tokens * channels),
        name="own",
    )(token_count, pair_state, gate_weights, *passed)
    in_gain, in_bias, right_weights, left_weights, out_weights, pairs[0] = handed

    def left_of(pairs):
        return pl.pallas_call(
            functools.partial(left_kernel, window),
            out_shape=jax.ShapeDtypeStruct((hidden, rows, width), jnp.bfloat16),
            in_specs=[SMEM] + [VMEM] * (window + 3),
            out_specs=VMEM,
            scratch_shapes=[
                pltpu.VMEM((width // LANES, hidden * pitch(rows), LANES), jnp.float32)
            ],
            compiler_params=params((window + 2) * block, 6 * hidden * rows * width),
            cost_estimate=cost(4 * window * tokens * channels * hidden, 6 * rows * width * hidden),
            name="left",
        )(token_count, *pairs, in_gain, in_bias, left_weights)

    def mine_of(first, far_pair, near_pair):
        count = near_pair.shape[0]
        return pl.pallas_call(
            functools.partial(mine_kernel, first),
            out_shape=jax.ShapeDtypeStruct((count, columns, hidden), jnp.bfloat16),
            in_specs=[SMEM] + [VMEM] * 5,
            out_specs=VMEM,
            compiler_params=params(2 * block),
            cost_estimate=cost(4 * count * columns * channels * hidden, 6 * count * columns * channels),
            name="mine",
        )(token_count, far_pair, near_pair, in_gain, in_bias, right_weights)

    if by_hops:
        arrived.append((move(later, far), move(later, near)))
        mine = [mine_of(0, *arrived[0])]
        pairs[0], mine[0] = lax.optimization_barrier((pairs[0], mine[0]))
        left = left_of(pairs)
        left, *last = lax.optimization_barrier((left, *arrived[1]))
        mine.append(mine_of(spans[1][0], *last))
        bands = [[right, piece, move(piece, share)] for piece in mine]
        picks, place = [(0, 1, 1, 2), (1, 2, 2, 1)], hop_place
    else:
        left = left_of(pairs)
        bands, picks = band_by_sums(right, spans, window, row_count, col_count, columns)
        place = lambda: 0

    done = []
    for (first, count), band in zip(spans, bands):
        last = first + count == columns
        scratch = [
            pltpu.VMEM((width // LANES, hidden * pitch(count), LANES), jnp.float32),
            pltpu.VMEM((hidden * pitch(count), LANES), jnp.float32),
            pltpu.VMEM((rows * pitch(count), channels), jnp.float32),
        ]
        if last:
            scratch += [
                pltpu.VMEM((rows, count, channels), jnp.bfloat16),
                pltpu.SemaphoreType.DMA((len(done) + rows // 16,)),
            ]
        filled = pl.pallas_call(
            functools.partial(product_kernel, picks, place, len(band), first, count, last),
            out_shape=jax.ShapeDtypeStruct(
                (rows, columns if last else count, channels), jnp.bfloat16
            ),
            in_specs=[VMEM] * (len(band) + 2) + [VMEM] * (3 + len(done) * last),
            out_specs=ANY if last else VMEM,
            scratch_shapes=scratch,
            compiler_params=params(2 * block, 2 * hidden * (rows + 2 * count) * width),
            cost_estimate=cost(2 * rows * count * depth * hidden, 4 * rows * depth * hidden),
            name="product",
        )(*band, left, gate, out_gain, out_bias, out_weights, *(done if last else []))
        done.append(filled)
    return filled


def solution(mesh):
    placed = (P(("crops", "row"), "col", None), P("crops"), P(), P(), P(), P(), P(), P(), P())
    return jax.shard_map(
        on_device,
        mesh=mesh,
        in_specs=placed,
        out_specs=P(("crops", "row"), "col", None),
        check_vma=False,
    )
```

```python
import functools

import jax
import jax.numpy as jnp
from jax import lax
from jax.experimental import pallas as pl
from jax.experimental.pallas import tpu as pltpu
from jax.sharding import PartitionSpec as P

LANES = 128
MIB = 1024 * 1024


def params(*sizes):
    return pltpu.CompilerParams(vmem_limit_bytes=min(6 * MIB + 2 * sum(sizes), 56 * MIB))


def cost(flops, bytes_accessed):
    return pl.CostEstimate(flops=flops, bytes_accessed=bytes_accessed, transcendentals=0)


VMEM = pl.BlockSpec(memory_space=pltpu.VMEM)
SMEM = pl.BlockSpec(memory_space=pltpu.SMEM)
ANY = pl.BlockSpec(memory_space=pl.ANY)


def pitch(rows):
    return (rows // 8 | 1) * 8


def shifted(array, axis, by):
    devices = lax.axis_size(axis)
    return lax.ppermute(array, axis, [(i, (i + by) % devices) for i in range(devices)])


def from_root(array, axis, root):
    mine = lax.axis_index(axis) == root
    return lax.psum(jnp.where(mine, array, jnp.zeros_like(array)), axis)


def layer_norm(values, gain, offset):
    average = jnp.mean(values, axis=-1, keepdims=True)
    centered = values - average
    variance = jnp.mean(centered * centered, axis=-1, keepdims=True)
    return centered * lax.rsqrt(variance + 1e-05) * gain + offset


def normed_rows(block, gain_ref, bias_ref):
    rows, columns, channels = block.shape
    values = block.reshape(rows * columns, channels).astype(jnp.float32)
    return layer_norm(values, gain_ref[...], bias_ref[...]).astype(jnp.bfloat16)


def mine_kernel(first, tokens_ref, near_ref, far_ref, gain_ref, bias_ref, weights_ref, out_ref):
    count, columns, _ = out_ref.shape
    col_pos, place = lax.axis_index("col"), hop_place()
    third_block = jnp.where((place == 0) | (place == 3), (col_pos + 1) % 4, col_pos)
    row_token = col_pos * columns + first
    step = 4
    for at in range(0, count, step):
        block = jnp.where(place < 2, near_ref[pl.ds(at, step)], far_ref[pl.ds(at, step)])
        normed = normed_rows(block, gain_ref, bias_ref)
        both = jnp.dot(normed, weights_ref[...], preferred_element_type=jnp.float32)
        parts = masked_right(both, tokens_ref[0], row_token + at, third_block, columns)
        for row, part in enumerate(parts):
            out_ref[at + row] = part


def masked_right(both, tokens, row_token, third_block, columns):
    hidden = both.shape[1] // 2
    right = jax.nn.sigmoid(both[:, :hidden]) * both[:, hidden:]
    position = lax.broadcasted_iota(jnp.int32, (columns, hidden), 0)
    parts = []
    for row in range(both.shape[0] // columns):
        limit = jnp.where(row_token + row < tokens, tokens - third_block * columns, 0)
        part = right[row * columns : (row + 1) * columns]
        parts.append(jnp.where(position < limit, part, 0.0).astype(jnp.bfloat16))
    return parts


def own_kernel(passes, tokens_ref, pair_ref, gate_weights_ref, *refs):
    passed, (gate_ref, right_ref, later_ref), handed = (
        refs[:passes],
        refs[passes : passes + 3],
        refs[passes + 3 :],
    )
    later_ref[...] = pair_ref[pl.ds(pair_ref.shape[0] - later_ref.shape[0], later_ref.shape[0])]
    gain_ref, bias_ref, right_weights_ref = passed[:3]
    for source, target in zip(passed, handed):
        target[...] = source[...]
    rows, columns, channels = pair_ref.shape
    row_start = lax.axis_index("row") * rows
    step = 4
    for first in range(0, rows, step):
        normed = normed_rows(pair_ref[pl.ds(first, step)], gain_ref, bias_ref)
        gate = jnp.dot(normed, gate_weights_ref[...], preferred_element_type=jnp.float32)
        gate_ref[pl.ds(first, step)] = jax.nn.sigmoid(gate).reshape(step, columns, channels)
        both = jnp.dot(normed, right_weights_ref[...], preferred_element_type=jnp.float32)
        parts = masked_right(
            both, tokens_ref[0], row_start + first, lax.axis_index("col"), columns
        )
        for row, part in enumerate(parts):
            right_ref[first + row] = part


def left_kernel(blocks, tokens_ref, *refs):
    pair_refs, (gain_ref, bias_ref, weights_ref, left_ref, scratch) = refs[:blocks], refs[blocks:]
    rows, columns, channels = pair_refs[0].shape
    hidden, _, width = left_ref.shape
    tokens = tokens_ref[0]
    row_start = lax.axis_index("row") * rows
    col_pos, col_count = lax.axis_index("col"), lax.axis_size("col")
    lane = lax.broadcasted_iota(jnp.int32, (1, width), 1)
    keep = jnp.zeros((1, width), jnp.float32)
    for at in range(blocks):
        end = at * columns + jnp.minimum(tokens - (col_pos + at) % col_count * columns, columns)
        keep += jnp.where((lane >= at * columns) & (lane < end), 1.0, 0.0)
    padding = [jnp.zeros((width - blocks * columns, channels), jnp.bfloat16)]
    if width == blocks * columns:
        padding = []
    step = 4
    for first in range(0, rows, step):
        normed = [normed_rows(ref[pl.ds(first, step)], gain_ref, bias_ref) for ref in pair_refs]
        for row in range(step):
            thirds = [piece[row * columns : (row + 1) * columns] for piece in normed]
            both = lax.dot_general(
                weights_ref[...],
                jnp.concatenate(thirds + padding, axis=0),
                (((1,), (1,)), ((), ())),
                preferred_element_type=jnp.float32,
            )
            left = jax.nn.sigmoid(both[:hidden]) * both[hidden:]
            valid = jnp.where(row_start + first + row < tokens, keep, 0.0)
            left = jnp.where(valid > 0.0, left, 0.0)
            for at in range(0, width, LANES):
                scratch[at // LANES, pl.ds(first + row, hidden, stride=pitch(rows)), :] = left[
                    :, at : at + LANES
                ]
    for channel in range(hidden):
        for at in range(0, width, LANES):
            one = scratch[at // LANES, pl.ds(channel * pitch(rows), rows), :].astype(jnp.bfloat16)
            left_ref[channel, :, at : at + LANES] = one


def turned(pieces, width):
    rows = sum(piece.shape[0] for piece in pieces)
    hidden = pieces[0].shape[1]
    if width > rows:
        pieces = pieces + [jnp.zeros((width - rows, hidden), pieces[0].dtype)]
    row = lax.broadcasted_iota(jnp.int32, (hidden, hidden), 0)
    column = lax.broadcasted_iota(jnp.int32, (hidden, hidden), 1)
    identity = (row == column).astype(jnp.float32).astype(jnp.bfloat16)
    return lax.dot_general(
        identity,
        jnp.concatenate(pieces, axis=0),
        (((1,), (1,)), ((), ())),
        preferred_element_type=jnp.float32,
    )


def product_kernel(picks, place, rights, first, count, last, *refs):
    right_refs, refs = refs[:rights], refs[rights:]
    left_ref, gate_ref, gain_ref, bias_ref, weights_ref, *done, out_ref = refs[: -5 if last else -3]
    right, product, updates = refs[-5:-2] if last else refs[-3:]
    result, sent = refs[-2:] if last else (out_ref, None)
    hidden, rows, width = left_ref.shape
    apart = pitch(count)
    mine = place()

    def row_of(source, token):
        ref = right_refs[source]
        return ref[token if ref.shape[0] == count else first + token]

    copies, start = [], 0
    for at, ref in enumerate(done):
        columns = pl.ds(start, ref.shape[1])
        copies.append(pltpu.make_async_copy(ref, out_ref.at[:, columns], sent.at[at]))
        copies[-1].start()
        start += ref.shape[1]

    for token in range(count):
        pieces = []
        for sources in picks:
            piece = row_of(sources[0], token)
            for at, source in enumerate(sources[1:], 1):
                if source != sources[at - 1]:
                    piece = jnp.where(mine >= at, row_of(source, token), piece)
            pieces.append(piece)
        one = turned(pieces, width)
        for at in range(0, width, LANES):
            right[at // LANES, pl.ds(token, hidden, stride=apart), :] = one[:, at : at + LANES]

    ways = 4
    totals = [jnp.zeros((count, rows), jnp.float32)] * ways
    for channel in range(hidden):
        one = 0.0
        for at in range(0, width, LANES):
            one += lax.dot_general(
                right[at // LANES, pl.ds(channel * apart, count), :].astype(jnp.bfloat16),
                left_ref[channel, :, at : at + LANES],
                (((1,), (1,)), ((), ())),
                preferred_element_type=jnp.float32,
            )
        product[pl.ds(channel * apart, count), :rows] = one
        totals[channel % ways] += one
    average = sum(totals) / hidden
    totals = [jnp.zeros((count, rows), jnp.float32)] * ways
    for channel in range(hidden):
        centered = product[pl.ds(channel * apart, count), :rows] - average
        totals[channel % ways] += centered * centered
    scale = lax.rsqrt(sum(totals) / hidden + 1e-05)
    gain, bias = (
        jnp.broadcast_to(ref[...], (LANES, hidden)).T[:, :rows] for ref in (gain_ref, bias_ref)
    )
    for token in range(count):
        values = product[pl.ds(token, hidden, stride=apart), :][:, :rows]
        centered = values - average[token : token + 1]
        mixed = (centered * scale[token : token + 1] * gain + bias).astype(jnp.bfloat16)
        updates[pl.ds(token, rows, stride=apart), :] = lax.dot_general(
            mixed, weights_ref[...], (((0,), (0,)), ((), ())), preferred_element_type=jnp.float32
        )
    step = 16
    for at in range(0, rows, step):
        gate = gate_ref[pl.ds(at, step), pl.ds(first, count)]
        for row in range(step):
            update = updates[pl.ds((at + row) * apart, count), :]
            result[at + row] = (gate[row] * update).astype(jnp.bfloat16)
        if last:
            target = out_ref.at[pl.ds(at, step), pl.ds(first, count)]
            place = sent.at[len(done) + at // step]
            copies.append(pltpu.make_async_copy(result.at[pl.ds(at, step)], target, place))
            copies[-1].start()
    for copy in copies:
        copy.wait()


def band_by_sums(right, spans, window, row_count, col_count, columns):
    blocks_per_row = col_count // row_count
    col_pos = lax.axis_index("col")
    pieces = []
    for offset in range(window):
        block_id = (col_pos - offset) % col_count
        start = block_id % blocks_per_row * columns
        received = from_root(
            lax.dynamic_slice_in_dim(right, start, columns, 0), "row", block_id // blocks_per_row
        )
        pieces.append(received if offset == 0 else shifted(received, "col", -offset))
    bands = [[piece[first : first + count] for piece in pieces] for first, count in spans]
    return bands, [(offset, offset) for offset in range(window)]


def hops():
    near, far, share = [], [], []
    for c in range(4):
        first, second = (c, c), (c, (c + 1) % 4)
        inner, outer = ((2, c), (3, c)) if c < 2 else ((1, c), (0, c))
        near += [(first, (c ^ 1, c)), (second, first)]
        far += [(first, inner), (second, outer)]
        share += [(inner, outer), (outer, inner), (first, (c ^ 1, c))]
    return near, far, share


def hop_place():
    row_pos = lax.axis_index("row")
    near = row_pos ^ lax.axis_index("col")
    inner = (row_pos == 1) | (row_pos == 2)
    return jnp.where(near < 2, near, jnp.where(inner, 2, 3))


def move(array, pairs):
    return lax.ppermute(
        array, ("row", "col"), [(r * 4 + c, to_r * 4 + to_c) for (r, c), (to_r, to_c) in pairs]
    )


def on_device(
    pair_state,
    token_count,
    in_gain,
    in_bias,
    in_weights,
    gate_weights,
    out_gain,
    out_bias,
    out_weights,
):
    rows, columns, channels = pair_state.shape
    hidden = out_weights.shape[0]
    tokens = rows * columns
    col_count = lax.axis_size("col")
    row_count = lax.axis_size("row")
    window = col_count // 2
    depth = window * columns
    width = -(-depth // LANES) * LANES
    in_gain, in_bias = in_gain.reshape(1, channels), in_bias.reshape(1, channels)
    out_gain, out_bias = out_gain.reshape(1, hidden), out_bias.reshape(1, hidden)
    block = 2 * tokens * max(channels, hidden)
    by_hops = row_count == 4 and col_count == 4
    last = 16
    spans = [(0, columns - last), (columns - last, last)]

    if by_hops:
        near, far, share = hops()
        soon = pair_state[: spans[0][1]]
        arrived = [(move(soon, near), move(soon, far))]
    pairs = [pair_state]
    for _ in range(window - 1):
        pairs.append(shifted(pairs[-1], "col", -1))
    left_weights, right_weights = in_weights[:, : 2 * hidden].T, in_weights[:, 2 * hidden :]
    passed = [in_gain, in_bias, right_weights, left_weights, out_weights, pair_state]
    gate, right, later, *handed = pl.pallas_call(
        functools.partial(own_kernel, len(passed)),
        out_shape=[
            jax.ShapeDtypeStruct((rows, columns, channels), jnp.float32),
            jax.ShapeDtypeStruct((rows, columns, hidden), jnp.bfloat16),
            jax.ShapeDtypeStruct((spans[1][1], columns, channels), jnp.bfloat16),
        ]
        + [jax.ShapeDtypeStruct(array.shape, array.dtype) for array in passed],
        in_specs=[SMEM] + [VMEM] * (2 + len(passed)),
        out_specs=[VMEM] * (3 + len(passed)),
        compiler_params=params(6 * block),
        cost_estimate=cost(6 * tokens * channels * hidden, 8 * tokens * channels),
        name="own",
    )(token_count, pair_state, gate_weights, *passed)
    in_gain, in_bias, right_weights, left_weights, out_weights, pairs[0] = handed

    def left_of(pairs):
        return pl.pallas_call(
            functools.partial(left_kernel, window),
            out_shape=jax.ShapeDtypeStruct((hidden, rows, width), jnp.bfloat16),
            in_specs=[SMEM] + [VMEM] * (window + 3),
            out_specs=VMEM,
            scratch_shapes=[
                pltpu.VMEM((width // LANES, hidden * pitch(rows), LANES), jnp.float32)
            ],
            compiler_params=params((window + 2) * block, 6 * hidden * rows * width),
            cost_estimate=cost(4 * window * tokens * channels * hidden, 6 * rows * width * hidden),
            name="left",
        )(token_count, *pairs, in_gain, in_bias, left_weights)

    def mine_of(first, near_pair, far_pair):
        count = near_pair.shape[0]
        return pl.pallas_call(
            functools.partial(mine_kernel, first),
            out_shape=jax.ShapeDtypeStruct((count, columns, hidden), jnp.bfloat16),
            in_specs=[SMEM] + [VMEM] * 5,
            out_specs=VMEM,
            compiler_params=params(2 * block),
            cost_estimate=cost(4 * count * columns * channels * hidden, 6 * count * columns * channels),
            name="mine",
        )(token_count, near_pair, far_pair, in_gain, in_bias, right_weights)

    if by_hops:
        arrived.append((move(later, near), move(later, far)))
        mine = [mine_of(0, *arrived[0])]
        pairs[0], mine[0] = lax.optimization_barrier((pairs[0], mine[0]))
        left = left_of(pairs)
        left, *last = lax.optimization_barrier((left, *arrived[1]))
        mine.append(mine_of(spans[1][0], *last))
        bands = [[right, piece, move(piece, share)] for piece in mine]
        picks, place = [(0, 1, 1, 2), (1, 2, 2, 1)], hop_place
    else:
        left = left_of(pairs)
        bands, picks = band_by_sums(right, spans, window, row_count, col_count, columns)
        place = lambda: 0

    done = []
    for (first, count), band in zip(spans, bands):
        last = first + count == columns
        scratch = [
            pltpu.VMEM((width // LANES, hidden * pitch(count), LANES), jnp.float32),
            pltpu.VMEM((hidden * pitch(count), LANES), jnp.float32),
            pltpu.VMEM((rows * pitch(count), channels), jnp.float32),
        ]
        if last:
            scratch += [
                pltpu.VMEM((rows, count, channels), jnp.bfloat16),
                pltpu.SemaphoreType.DMA((len(done) + rows // 16,)),
            ]
        filled = pl.pallas_call(
            functools.partial(product_kernel, picks, place, len(band), first, count, last),
            out_shape=jax.ShapeDtypeStruct(
                (rows, columns if last else count, channels), jnp.bfloat16
            ),
            in_specs=[VMEM] * (len(band) + 2) + [VMEM] * (3 + len(done) * last),
            out_specs=ANY if last else VMEM,
            scratch_shapes=scratch,
            compiler_params=params(2 * block, 2 * hidden * (rows + 2 * count) * width),
            cost_estimate=cost(2 * rows * count * depth * hidden, 4 * rows * depth * hidden),
            name="product",
        )(*band, left, gate, out_gain, out_bias, out_weights, *(done if last else []))
        done.append(filled)
    return filled


def solution(mesh):
    placed = (P(("crops", "row"), "col", None), P("crops"), P(), P(), P(), P(), P(), P(), P())
    return jax.shard_map(
        on_device,
        mesh=mesh,
        in_specs=placed,
        out_specs=P(("crops", "row"), "col", None),
        check_vma=False,
    )
```

```python
import functools

import jax
import jax.numpy as jnp
from jax import lax
from jax.experimental import pallas as pl
from jax.experimental.pallas import tpu as pltpu
from jax.sharding import PartitionSpec as P

LANES = 128
MIB = 1024 * 1024


def params(*sizes):
    return pltpu.CompilerParams(vmem_limit_bytes=min(6 * MIB + 2 * sum(sizes), 56 * MIB))


def cost(flops, bytes_accessed):
    return pl.CostEstimate(flops=flops, bytes_accessed=bytes_accessed, transcendentals=0)


VMEM = pl.BlockSpec(memory_space=pltpu.VMEM)
SMEM = pl.BlockSpec(memory_space=pltpu.SMEM)
ANY = pl.BlockSpec(memory_space=pl.ANY)


def pitch(rows):
    return (rows // 8 | 1) * 8


def shifted(array, axis, by):
    devices = lax.axis_size(axis)
    return lax.ppermute(array, axis, [(i, (i + by) % devices) for i in range(devices)])


def from_root(array, axis, root):
    mine = lax.axis_index(axis) == root
    return lax.psum(jnp.where(mine, array, jnp.zeros_like(array)), axis)


def layer_norm(values, gain, offset):
    average = jnp.mean(values, axis=-1, keepdims=True)
    centered = values - average
    variance = jnp.mean(centered * centered, axis=-1, keepdims=True)
    return centered * lax.rsqrt(variance + 1e-05) * gain + offset


def normed_rows(block, gain_ref, bias_ref):
    rows, columns, channels = block.shape
    values = block.reshape(rows * columns, channels).astype(jnp.float32)
    return layer_norm(values, gain_ref[...], bias_ref[...]).astype(jnp.bfloat16)


def mine_kernel(first, tokens_ref, far_ref, near_ref, gain_ref, bias_ref, weights_ref, out_ref):
    count, columns, _ = out_ref.shape
    col_pos, place = lax.axis_index("col"), hop_place()
    third_block = jnp.where((place == 0) | (place == 3), (col_pos + 1) % 4, col_pos)
    row_token = col_pos * columns + first
    step = 4
    for at in range(0, count, step):
        block = jnp.where(place < 2, near_ref[pl.ds(at, step)], far_ref[pl.ds(at, step)])
        normed = normed_rows(block, gain_ref, bias_ref)
        both = jnp.dot(normed, weights_ref[...], preferred_element_type=jnp.float32)
        parts = masked_right(both, tokens_ref[0], row_token + at, third_block, columns)
        for row, part in enumerate(parts):
            out_ref[at + row] = part


def masked_right(both, tokens, row_token, third_block, columns):
    hidden = both.shape[1] // 2
    right = jax.nn.sigmoid(both[:, :hidden]) * both[:, hidden:]
    position = lax.broadcasted_iota(jnp.int32, (columns, hidden), 0)
    parts = []
    for row in range(both.shape[0] // columns):
        limit = jnp.where(row_token + row < tokens, tokens - third_block * columns, 0)
        part = right[row * columns : (row + 1) * columns]
        parts.append(jnp.where(position < limit, part, 0.0).astype(jnp.bfloat16))
    return parts


def own_kernel(passes, tokens_ref, pair_ref, gate_weights_ref, *refs):
    passed, (gate_ref, right_ref, later_ref), handed = (
        refs[:passes],
        refs[passes : passes + 3],
        refs[passes + 3 :],
    )
    later_ref[...] = pair_ref[pl.ds(pair_ref.shape[0] - later_ref.shape[0], later_ref.shape[0])]
    gain_ref, bias_ref, right_weights_ref = passed[:3]
    for source, target in zip(passed, handed):
        target[...] = source[...]
    rows, columns, channels = pair_ref.shape
    row_start = lax.axis_index("row") * rows
    step = 4
    for first in range(0, rows, step):
        normed = normed_rows(pair_ref[pl.ds(first, step)], gain_ref, bias_ref)
        gate = jnp.dot(normed, gate_weights_ref[...], preferred_element_type=jnp.float32)
        gate_ref[pl.ds(first, step)] = jax.nn.sigmoid(gate).reshape(step, columns, channels)
        both = jnp.dot(normed, right_weights_ref[...], preferred_element_type=jnp.float32)
        parts = masked_right(
            both, tokens_ref[0], row_start + first, lax.axis_index("col"), columns
        )
        for row, part in enumerate(parts):
            right_ref[first + row] = part


def left_kernel(blocks, tokens_ref, *refs):
    pair_refs, (gain_ref, bias_ref, weights_ref, left_ref, scratch) = refs[:blocks], refs[blocks:]
    rows, columns, channels = pair_refs[0].shape
    hidden, _, width = left_ref.shape
    tokens = tokens_ref[0]
    row_start = lax.axis_index("row") * rows
    col_pos, col_count = lax.axis_index("col"), lax.axis_size("col")
    lane = lax.broadcasted_iota(jnp.int32, (1, width), 1)
    keep = jnp.zeros((1, width), jnp.float32)
    for at in range(blocks):
        end = at * columns + jnp.minimum(tokens - (col_pos + at) % col_count * columns, columns)
        keep += jnp.where((lane >= at * columns) & (lane < end), 1.0, 0.0)
    padding = [jnp.zeros((width - blocks * columns, channels), jnp.bfloat16)]
    if width == blocks * columns:
        padding = []
    step = 4
    for first in range(0, rows, step):
        normed = [normed_rows(ref[pl.ds(first, step)], gain_ref, bias_ref) for ref in pair_refs]
        for row in range(step):
            thirds = [piece[row * columns : (row + 1) * columns] for piece in normed]
            both = lax.dot_general(
                weights_ref[...],
                jnp.concatenate(thirds + padding, axis=0),
                (((1,), (1,)), ((), ())),
                preferred_element_type=jnp.float32,
            )
            left = jax.nn.sigmoid(both[:hidden]) * both[hidden:]
            valid = jnp.where(row_start + first + row < tokens, keep, 0.0)
            left = jnp.where(valid > 0.0, left, 0.0)
            for at in range(0, width, LANES):
                scratch[at // LANES, pl.ds(first + row, hidden, stride=pitch(rows)), :] = left[
                    :, at : at + LANES
                ]
    for channel in range(hidden):
        for at in range(0, width, LANES):
            one = scratch[at // LANES, pl.ds(channel * pitch(rows), rows), :].astype(jnp.bfloat16)
            left_ref[channel, :, at : at + LANES] = one


def turned(pieces, width):
    rows = sum(piece.shape[0] for piece in pieces)
    hidden = pieces[0].shape[1]
    if width > rows:
        pieces = pieces + [jnp.zeros((width - rows, hidden), pieces[0].dtype)]
    row = lax.broadcasted_iota(jnp.int32, (hidden, hidden), 0)
    column = lax.broadcasted_iota(jnp.int32, (hidden, hidden), 1)
    identity = (row == column).astype(jnp.float32).astype(jnp.bfloat16)
    return lax.dot_general(
        identity,
        jnp.concatenate(pieces, axis=0),
        (((1,), (1,)), ((), ())),
        preferred_element_type=jnp.float32,
    )


def product_kernel(picks, place, rights, first, count, last, *refs):
    right_refs, refs = refs[:rights], refs[rights:]
    left_ref, gate_ref, gain_ref, bias_ref, weights_ref, *done, out_ref = refs[: -5 if last else -3]
    right, product, updates = refs[-5:-2] if last else refs[-3:]
    result, sent = refs[-2:] if last else (out_ref, None)
    hidden, rows, width = left_ref.shape
    apart = pitch(count)
    mine = place()

    def row_of(source, token):
        ref = right_refs[source]
        return ref[token if ref.shape[0] == count else first + token]

    copies, start = [], 0
    for at, ref in enumerate(done):
        columns = pl.ds(start, ref.shape[1])
        copies.append(pltpu.make_async_copy(ref, out_ref.at[:, columns], sent.at[at]))
        copies[-1].start()
        start += ref.shape[1]

    for token in range(count):
        pieces = []
        for sources in picks:
            piece = row_of(sources[0], token)
            for at, source in enumerate(sources[1:], 1):
                if source != sources[at - 1]:
                    piece = jnp.where(mine >= at, row_of(source, token), piece)
            pieces.append(piece)
        one = turned(pieces, width)
        for at in range(0, width, LANES):
            right[at // LANES, pl.ds(token, hidden, stride=apart), :] = one[:, at : at + LANES]

    ways = 4
    totals = [jnp.zeros((count, rows), jnp.float32)] * ways
    for channel in range(hidden):
        one = 0.0
        for at in range(0, width, LANES):
            one += lax.dot_general(
                right[at // LANES, pl.ds(channel * apart, count), :].astype(jnp.bfloat16),
                left_ref[channel, :, at : at + LANES],
                (((1,), (1,)), ((), ())),
                preferred_element_type=jnp.float32,
            )
        product[pl.ds(channel * apart, count), :rows] = one
        totals[channel % ways] += one
    average = sum(totals) / hidden
    totals = [jnp.zeros((count, rows), jnp.float32)] * ways
    for channel in range(hidden):
        centered = product[pl.ds(channel * apart, count), :rows] - average
        totals[channel % ways] += centered * centered
    scale = lax.rsqrt(sum(totals) / hidden + 1e-05)
    gain, bias = (
        jnp.broadcast_to(ref[...], (LANES, hidden)).T[:, :rows] for ref in (gain_ref, bias_ref)
    )
    for token in range(count):
        values = product[pl.ds(token, hidden, stride=apart), :][:, :rows]
        centered = values - average[token : token + 1]
        mixed = (centered * scale[token : token + 1] * gain + bias).astype(jnp.bfloat16)
        updates[pl.ds(token, rows, stride=apart), :] = lax.dot_general(
            mixed, weights_ref[...], (((0,), (0,)), ((), ())), preferred_element_type=jnp.float32
        )
    step = 16
    for at in range(0, rows, step):
        gate = gate_ref[pl.ds(at, step), pl.ds(first, count)]
        for row in range(step):
            update = updates[pl.ds((at + row) * apart, count), :]
            result[at + row] = (gate[row] * update).astype(jnp.bfloat16)
        if last:
            target = out_ref.at[pl.ds(at, step), pl.ds(first, count)]
            place = sent.at[len(done) + at // step]
            copies.append(pltpu.make_async_copy(result.at[pl.ds(at, step)], target, place))
            copies[-1].start()
    for copy in copies:
        copy.wait()


def band_by_sums(right, spans, window, row_count, col_count, columns):
    blocks_per_row = col_count // row_count
    col_pos = lax.axis_index("col")
    pieces = []
    for offset in range(window):
        block_id = (col_pos - offset) % col_count
        start = block_id % blocks_per_row * columns
        received = from_root(
            lax.dynamic_slice_in_dim(right, start, columns, 0), "row", block_id // blocks_per_row
        )
        pieces.append(received if offset == 0 else shifted(received, "col", -offset))
    bands = [[piece[first : first + count] for piece in pieces] for first, count in spans]
    return bands, [(offset, offset) for offset in range(window)]


def hops():
    near, far, share = [], [], []
    for c in range(4):
        first, second = (c, c), (c, (c + 1) % 4)
        inner, outer = ((2, c), (3, c)) if c < 2 else ((1, c), (0, c))
        near += [(first, (c ^ 1, c)), (second, first)]
        far += [(first, inner), (second, outer)]
        share += [(inner, outer), (outer, inner), (first, (c ^ 1, c))]
    return near, far, share


def hop_place():
    row_pos = lax.axis_index("row")
    near = row_pos ^ lax.axis_index("col")
    inner = (row_pos == 1) | (row_pos == 2)
    return jnp.where(near < 2, near, jnp.where(inner, 2, 3))


def move(array, pairs):
    return lax.ppermute(
        array, ("row", "col"), [(r * 4 + c, to_r * 4 + to_c) for (r, c), (to_r, to_c) in pairs]
    )


def on_device(
    pair_state,
    token_count,
    in_gain,
    in_bias,
    in_weights,
    gate_weights,
    out_gain,
    out_bias,
    out_weights,
):
    rows, columns, channels = pair_state.shape
    hidden = out_weights.shape[0]
    tokens = rows * columns
    col_count = lax.axis_size("col")
    row_count = lax.axis_size("row")
    window = col_count // 2
    depth = window * columns
    width = -(-depth // LANES) * LANES
    in_gain, in_bias = in_gain.reshape(1, channels), in_bias.reshape(1, channels)
    out_gain, out_bias = out_gain.reshape(1, hidden), out_bias.reshape(1, hidden)
    block = 2 * tokens * max(channels, hidden)
    by_hops = row_count == 4 and col_count == 4
    last = 16
    spans = [(0, columns - last), (columns - last, last)]

    if by_hops:
        near, far, share = hops()
        soon = pair_state[: spans[0][1]]
        arrived = [(move(soon, far), move(soon, near))]
    pairs = [pair_state]
    for _ in range(window - 1):
        pairs.append(shifted(pairs[-1], "col", -1))
    left_weights, right_weights = in_weights[:, : 2 * hidden].T, in_weights[:, 2 * hidden :]
    passed = [in_gain, in_bias, right_weights, left_weights, pair_state]
    gate, right, later, *handed = pl.pallas_call(
        functools.partial(own_kernel, len(passed)),
        out_shape=[
            jax.ShapeDtypeStruct((rows, columns, channels), jnp.float32),
            jax.ShapeDtypeStruct((rows, columns, hidden), jnp.bfloat16),
            jax.ShapeDtypeStruct((spans[1][1], columns, channels), jnp.bfloat16),
        ]
        + [jax.ShapeDtypeStruct(array.shape, array.dtype) for array in passed],
        in_specs=[SMEM] + [VMEM] * (2 + len(passed)),
        out_specs=[VMEM] * (3 + len(passed)),
        compiler_params=params(6 * block),
        cost_estimate=cost(6 * tokens * channels * hidden, 8 * tokens * channels),
        name="own",
    )(token_count, pair_state, gate_weights, *passed)
    in_gain, in_bias, right_weights, left_weights, pairs[0] = handed

    def left_of(pairs):
        return pl.pallas_call(
            functools.partial(left_kernel, window),
            out_shape=jax.ShapeDtypeStruct((hidden, rows, width), jnp.bfloat16),
            in_specs=[SMEM] + [VMEM] * (window + 3),
            out_specs=VMEM,
            scratch_shapes=[
                pltpu.VMEM((width // LANES, hidden * pitch(rows), LANES), jnp.float32)
            ],
            compiler_params=params((window + 2) * block, 6 * hidden * rows * width),
            cost_estimate=cost(4 * window * tokens * channels * hidden, 6 * rows * width * hidden),
            name="left",
        )(token_count, *pairs, in_gain, in_bias, left_weights)

    def mine_of(first, far_pair, near_pair):
        count = near_pair.shape[0]
        return pl.pallas_call(
            functools.partial(mine_kernel, first),
            out_shape=jax.ShapeDtypeStruct((count, columns, hidden), jnp.bfloat16),
            in_specs=[SMEM] + [VMEM] * 5,
            out_specs=VMEM,
            compiler_params=params(2 * block),
            cost_estimate=cost(4 * count * columns * channels * hidden, 6 * count * columns * channels),
            name="mine",
        )(token_count, far_pair, near_pair, in_gain, in_bias, right_weights)

    if by_hops:
        arrived.append((move(later, far), move(later, near)))
        mine = [mine_of(0, *arrived[0])]
        pairs[0], mine[0] = lax.optimization_barrier((pairs[0], mine[0]))
        left = left_of(pairs)
        left, *last = lax.optimization_barrier((left, *arrived[1]))
        mine.append(mine_of(spans[1][0], *last))
        bands = [[right, piece, move(piece, share)] for piece in mine]
        picks, place = [(0, 1, 1, 2), (1, 2, 2, 1)], hop_place
    else:
        left = left_of(pairs)
        bands, picks = band_by_sums(right, spans, window, row_count, col_count, columns)
        place = lambda: 0

    done = []
    for (first, count), band in zip(spans, bands):
        last = first + count == columns
        scratch = [
            pltpu.VMEM((width // LANES, hidden * pitch(count), LANES), jnp.float32),
            pltpu.VMEM((hidden * pitch(count), LANES), jnp.float32),
            pltpu.VMEM((rows * pitch(count), channels), jnp.float32),
        ]
        if last:
            scratch += [
                pltpu.VMEM((rows, count, channels), jnp.bfloat16),
                pltpu.SemaphoreType.DMA((len(done) + rows // 16,)),
            ]
        filled = pl.pallas_call(
            functools.partial(product_kernel, picks, place, len(band), first, count, last),
            out_shape=jax.ShapeDtypeStruct(
                (rows, columns if last else count, channels), jnp.bfloat16
            ),
            in_specs=[VMEM] * (len(band) + 2) + [VMEM] * (3 + len(done) * last),
            out_specs=ANY if last else VMEM,
            scratch_shapes=scratch,
            compiler_params=params(2 * block, 2 * hidden * (rows + 2 * count) * width),
            cost_estimate=cost(2 * rows * count * depth * hidden, 4 * rows * depth * hidden),
            name="product",
        )(*band, left, gate, out_gain, out_bias, out_weights, *(done if last else []))
        done.append(filled)
    return filled


def solution(mesh):
    placed = (P(("crops", "row"), "col", None), P("crops"), P(), P(), P(), P(), P(), P(), P())
    return jax.shard_map(
        on_device,
        mesh=mesh,
        in_specs=placed,
        out_specs=P(("crops", "row"), "col", None),
        check_vma=False,
    )
```
